32 devices in a mesh: dp: 2 (over y), ctx: 4 (over z), tensor: 4 (over x, core).
Axes of the slice: x: 2, y: 2, z: 4, core: 2. Of those that a mesh axis runs over, the one named last changes fastest.
Arguments:
- activations: bfloat16 [2, 512, 2048], P('dp', 'ctx'), may hold values from -6 to 6
- cotangent: bfloat16 [2, 512, 2048], P('dp', 'ctx'), may hold values from -6 to 6
- doc_ids: int32 [2, 512], P('dp'), may hold values from 0 to 3, as said below
- attn_gain: bfloat16 [2048], replicated, may hold values from 0.25 to 1.75
- query_weight: bfloat16 [2048, 2048], P(None, 'tensor'), may hold values from -0.125 to 0.125
- key_weight: bfloat16 [2048, 2048], P(None, 'tensor'), may hold values from -0.125 to 0.125
- value_weight: bfloat16 [2048, 2048], P(None, 'tensor'), may hold values from -0.125 to 0.125
- out_weight: bfloat16 [2048, 2048], P('tensor'), may hold values from -1.5 to 1.5
- mlp_gain: bfloat16 [2048], replicated, may hold values from 0.25 to 1.75
- gate_weight: bfloat16 [2048, 8192], P(None, 'tensor'), may hold values from -0.125 to 0.125
- up_weight: bfloat16 [2048, 8192], P(None, 'tensor'), may hold values from -0.125 to 0.125
- down_weight: bfloat16 [8192, 2048], P('tensor'), may hold values from -0.0625 to 0.0625
Outputs:
- layer_out: bfloat16 [2, 512, 2048], P('dp', 'ctx')
- input_grad: bfloat16 [2, 512, 2048], P('dp', 'ctx')
- attn_gain_grad: float32 [2048], P(('dp', 'ctx'))
- query_grad: float32 [2048, 2048], P(('dp', 'ctx'), 'tensor')
- key_grad: float32 [2048, 2048], P(('dp', 'ctx'), 'tensor')
- value_grad: float32 [2048, 2048], P(('dp', 'ctx'), 'tensor')
- out_grad: float32 [2048, 2048], P('tensor', ('dp', 'ctx'))
- mlp_gain_grad: float32 [2048], P(('dp', 'ctx'))
- gate_grad: float32 [2048, 8192], P(('dp', 'ctx'), 'tensor')
- up_grad: float32 [2048, 8192], P(('dp', 'ctx'), 'tensor')
- down_grad: float32 [8192, 2048], P('tensor', ('dp', 'ctx'))
- attn_mass: float32 [2, 512, 16], P('dp', 'ctx', 'tensor')
The draws below stay inside these ranges and needn't reach their ends.
Inputs may be any that keep to these rules, and one draw needn't show every extreme that they name: `doc_ids`: in each sequence the numbers start at 0, never fall and rise by one at each of three places; document 1 begins within the first 128 tokens and ends within the last 128.
All inputs are finite; a program needn't handle non-finite values.
Results may differ from the reference program's by a relative error of at most 0.014.
Values may be sent and summed in bfloat16 or wider, within the bound.
No kernel may reach another device: no remote copies, remote signals or barrier semaphores. Data moves between devices by JAX's collectives and lax.ppermute only.
A program may use at most 256 MiB of HBM per device.

```python
import math
import jax
import jax.numpy as jnp
from jax import lax

D = 2048
H = 16
HD = 128
FF = 8192
TOK_DEV = 128
BATCH = 2
SEQ = 512


def draw_doc_ids(key, part):
    key = jax.random.fold_in(key, 11)
    first_key, second_key, third_key = jax.random.split(key, 3)
    first_cut = jax.random.randint(first_key, (BATCH, 1), 1, TOK_DEV)
    second_cut = SEQ - jax.random.randint(second_key, (BATCH, 1), 2, TOK_DEV)
    third_cut = jax.random.randint(third_key, (BATCH, 1), second_cut + 1, SEQ)
    positions = jnp.arange(SEQ, dtype=jnp.int32)[None, :]
    return (positions >= first_cut).astype(jnp.int32) + (positions >= second_cut).astype(jnp.int32) + (positions >= third_cut).astype(jnp.int32)


def raised(values, rng, source, target, blocks, factor):
    def block_of(dim):
        return (jnp.arange(values.shape[dim]) // (values.shape[dim] // blocks)).reshape((-1,) + (1,) * (values.ndim - 1 - dim))

    one_side = jax.random.permutation(rng, blocks)[block_of(target)]
    other_side = (block_of(target) + blocks // 2) % blocks
    return jnp.where((block_of(source) == one_side) | (block_of(source) == other_side), factor * values, values)


def block_levels(own_key, shape, cuts, low, largest):
    loudness = 1.0
    for axis_at, shards_of in cuts:
        draws = jax.random.uniform(jax.random.fold_in(jax.random.fold_in(own_key, 6), axis_at), (shards_of,), jnp.float32, low / len(cuts), largest / len(cuts))
        loudness = loudness * jnp.repeat(jnp.exp(draws), shape[axis_at] // shards_of).reshape((-1,) + (1,) * (len(shape) - 1 - axis_at))
    return loudness


def normal_values(key, extent, spread, limit, shards=(), held_as=jnp.bfloat16):
    entries = jax.random.normal(key, extent, jnp.float32) * spread
    if len(shards) > 0:
        entries = block_levels(key, extent, shards, -0.22, 0.18) * entries
    return jnp.clip(entries, min=-limit, max=limit).astype(held_as)


def gaussian_with(stream_key, extent, width, most, cuts, heavy, kind=jnp.bfloat16):
    entries = width * jax.random.normal(stream_key, extent, jnp.float32)
    if cuts:
        entries = entries * block_levels(stream_key, extent, cuts, -0.22, 0.18)
    return jnp.clip(raised(entries, jax.random.fold_in(stream_key, 3), *heavy), -most, most).astype(kind)


def setup_inputs(seed: int = 0) -> dict:
    streams_of = jax.random.split(jax.random.key(seed), 13)
    activations = normal_values(streams_of[0], (BATCH, SEQ, D), 1.0, 6.0, ((0, 2), (1, 4)))
    cotangent = gaussian_with(streams_of[1], (BATCH, SEQ, D), 1.0, 6.0, ((0, 2), (1, 4)), (1, 2, 4, 2.0))
    doc_ids = draw_doc_ids(jax.random.fold_in(streams_of[12], 71), 0)
    attn_gain = jnp.clip(1.0 + 0.15 * jax.random.normal(streams_of[3], (D,), jnp.float32), 0.25, 1.75).astype(jnp.bfloat16)
    query_weight = normal_values(streams_of[4], (D, H * HD), D ** -0.5, 0.125, ((1, 4),))
    key_weight = normal_values(streams_of[5], (D, H * HD), D ** -0.5, 0.125, ((1, 4),))
    value_weight = normal_values(streams_of[6], (D, H * HD), D ** -0.5, 0.125, ((1, 4),))
    out_weight = normal_values(streams_of[7], (H * HD, D), (max(1, H * HD * 4 // SEQ)) ** -0.5, 1.5, ((0, 4),))
    mlp_gain = jnp.clip(1.0 + 0.15 * jax.random.normal(streams_of[8], (D,), jnp.float32), 0.25, 1.75).astype(jnp.bfloat16)
    gate_weight = normal_values(streams_of[9], (D, FF), D ** -0.5, 0.125, ((1, 4),))
    up_weight = normal_values(streams_of[10], (D, FF), D ** -0.5, 0.125, ((1, 4),))
    down_weight = normal_values(streams_of[11], (FF, D), FF ** -0.5, 0.0625, ((0, 4),))
    return {"activations": activations, "cotangent": cotangent, "doc_ids": doc_ids, "attn_gain": attn_gain, "query_weight": query_weight, "key_weight": key_weight, "value_weight": value_weight, "out_weight": out_weight, "mlp_gain": mlp_gain, "gate_weight": gate_weight, "up_weight": up_weight, "down_weight": down_weight}


epsilon = 1e-05

@jax.custom_vjp
def low(v):
    return lax.optimization_barrier(v.astype(jnp.bfloat16)).astype(jnp.float32)

@jax.custom_vjp
def low_back(v):
    return v

def low_keep(v):
    return (low(v), None)

def low_pass(kept, grad):
    return (grad,)

def back_keep(v):
    return (v, None)

def back_low(kept, grad):
    return (low(grad),)
low.defvjp(low_keep, low_pass)
low_back.defvjp(back_keep, back_low)

def product(left_side, right_side):
    return jnp.dot(left_side, right_side, precision=lax.Precision.HIGHEST)

def rms_norm(values, gain_vec):
    return values * lax.rsqrt(lax.optimization_barrier(jnp.mean(values * values, axis=-1, keepdims=True)) + epsilon) * gain_vec

def rotate(values):
    half_width = values.shape[-1] // 2
    return jnp.concatenate([-values[..., half_width:], values[..., :half_width]], axis=-1)

def rotary(values, cosine_table, sine_table):
    return values * cosine_table + rotate(values) * sine_table

def rope_tables(length):
    half_width = HD // 2
    frequency = 10000.0 ** (-jnp.arange(half_width, dtype=jnp.float32) * 2.0 / HD)
    angles = jnp.arange(length, dtype=jnp.float32)[:, None] * frequency[None, :]
    cosine_table = jnp.concatenate([jnp.cos(angles), jnp.cos(angles)], axis=1)
    sine_table = jnp.concatenate([jnp.sin(angles), jnp.sin(angles)], axis=1)
    return (cosine_table[:, None, :], sine_table[:, None, :])

def forward(inputs, attn_gain, query_weight, key_weight, value_weight, out_weight, mlp_gain, gate_weight, up_weight, down_weight, doc_row):
    length = inputs.shape[0]
    cosine_table, sine_table = rope_tables(length)
    normed = low(rms_norm(inputs, attn_gain))
    queries = low(rotary(low_back(product(normed, query_weight)).reshape(length, H, HD), cosine_table, sine_table))
    key_rows = low(rotary(low_back(product(normed, key_weight)).reshape(length, H, HD), cosine_table, sine_table))
    values = low(low_back(product(normed, value_weight))).reshape(length, H, HD)
    positions = jnp.arange(length, dtype=jnp.int32)
    block_rows = min(512, length)
    block_count = length // block_rows
    bias_shift = -math.log(length)
    score_scale = HD ** (-0.5)

    def attend(pieces):
        query_block, spot_block, doc_block = pieces
        scores = jnp.einsum('qhd,khd->hqk', query_block, key_rows, precision=lax.Precision.HIGHEST) * score_scale + bias_shift
        scores = low_back(scores)
        allowed = (positions[None, :] <= spot_block[:, None]) & (doc_row[None, :] == doc_block[:, None])
        weights = jax.nn.sigmoid(scores) * allowed[None].astype(jnp.float32)
        seq_mass = lax.optimization_barrier(jnp.sum(weights, axis=-1))
        mixed_rows = jnp.einsum('hqk,khd->qhd', low(weights), values, precision=lax.Precision.HIGHEST)
        return (mixed_rows, seq_mass.T)
    mixed_rows, seq_mass = lax.map(jax.checkpoint(attend), (queries.reshape(block_count, block_rows, H, HD), positions.reshape(block_count, block_rows), doc_row.reshape(block_count, block_rows)))
    attended = low(low_back(mixed_rows.reshape(length, H * HD)))
    branch = low_back(product(attended, out_weight))
    middle = inputs + branch
    normed_mlp = low(rms_norm(middle, mlp_gain))
    gate_proj = low_back(product(normed_mlp, gate_weight))
    up_proj = low_back(product(normed_mlp, up_weight))
    hidden = low(jax.nn.silu(gate_proj) * up_proj)
    return (middle + product(hidden, down_weight), seq_mass.reshape(length, H))

def reference(activations, cotangent, doc_ids, attn_gain, query_weight, key_weight, value_weight, out_weight, mlp_gain, gate_weight, up_weight, down_weight):
    params = tuple((item.astype(jnp.float32) for item in (attn_gain, query_weight, key_weight, value_weight, out_weight, mlp_gain, gate_weight, up_weight, down_weight)))

    def sequence_step(totals, pieces):
        seq_rows, cot_rows, doc_row = pieces

        def run_layer(inputs, *weight_list):
            return forward(inputs, *weight_list, doc_row)
        result, pullback, seq_mass = jax.vjp(run_layer, seq_rows.astype(jnp.float32), *params, has_aux=True)
        gradients = pullback(cot_rows.astype(jnp.float32))
        totals = tuple((total + grad for total, grad in zip(totals, gradients[1:])))
        return (totals, (result.astype(jnp.bfloat16), gradients[0].astype(jnp.bfloat16), seq_mass))
    zero_grads = tuple((jnp.zeros(item.shape, jnp.float32) for item in params))
    totals, (layer_out, input_grad, attn_mass) = lax.scan(sequence_step, zero_grads, (activations, cotangent, doc_ids))
    return (layer_out, input_grad, totals[0], totals[1], totals[2], totals[3], totals[4], totals[5], totals[6], totals[7], totals[8], attn_mass)
```

```python
import functools
import math

import jax
import jax.numpy as jnp
from jax import lax
from jax.experimental import pallas as pl
from jax.experimental.pallas import tpu as pltpu
from jax.sharding import PartitionSpec as P

HD = 128
EPS = 1e-05
BF = jnp.bfloat16
F32 = jnp.float32
VMEM_LIMIT = 56 * 1024 * 1024


def swap(values, axis, distance):
    count = lax.axis_size(axis)
    return lax.ppermute(values, axis, [(i, i ^ distance) for i in range(count)])


def turn(values, axis, shift):
    count = lax.axis_size(axis)
    return lax.ppermute(values, axis, [(i, (i + shift) % count) for i in range(count)])


def bits_of(count):
    return [1 << i for i in range(count.bit_length() - 1)]


def slot_order(count):
    order = [0]
    for bit in reversed(bits_of(count)):
        order = order + [slot ^ bit for slot in order]
    return order


def gather_tensor(rows):
    for bit in reversed(bits_of(lax.axis_size("tensor"))):
        rows = jnp.concatenate([rows, swap(rows, "tensor", bit)], axis=0)
    return rows


def scatter_tensor(rows):
    for bit in bits_of(lax.axis_size("tensor")):
        half = rows.shape[0] // 2
        got = swap(rows[half:].astype(BF), "tensor", bit)
        rows = rows[:half].astype(F32) + got.astype(F32)
    return rows


def gather_tokens(rows):
    return jnp.concatenate(
        [rows] + [turn(rows, "ctx", k) for k in range(1, lax.axis_size("ctx"))], axis=0
    )


def gather_dp(rows):
    return jnp.concatenate(
        [rows] + [turn(rows, "dp", k) for k in range(1, lax.axis_size("dp"))], axis=0
    )


def from_slots(blocks, slots, place):
    size = blocks.shape[0] // len(slots)
    out = jnp.zeros_like(blocks)
    for index, slot in enumerate(slots):
        out = lax.dynamic_update_slice_in_dim(
            out, blocks[index * size : (index + 1) * size], (place ^ slot) * size, 0
        )
    return out


def rope_rows(u, cos, sin):
    return u * cos + pltpu.roll(u, HD // 2, 1) * sin


def rope_back_rows(u, cos, sin):
    return u * cos - pltpu.roll(u, HD // 2, 1) * sin


def dot(a, b):
    return lax.dot_general(a, b, (((1,), (0,)), ((), ())), preferred_element_type=F32)


def dot_nt(a, b):
    return lax.dot_general(a, b, (((1,), (1,)), ((), ())), preferred_element_type=F32)


def dot_tn(a, b):
    return lax.dot_general(a, b, (((0,), (0,)), ((), ())), preferred_element_type=F32)


def own_rows(values, chunk, ring):
    step = chunk * ring
    return jnp.concatenate(
        [values[i * step : i * step + chunk] for i in range(values.shape[0] // step)], axis=0
    )


def attend_kernel(
    chunk, ring, scale, shift,
    x_ref, wq_ref, wk_ref, wv_ref, cos_ref, sin_ref, ok_ref,
    q_ref, k_ref, v_ref, att_ref, mass_ref,
):
    rows = x_ref[...]
    cos, sin, ok = cos_ref[...], sin_ref[...], ok_ref[...]
    q_all = dot(rows, wq_ref[...])
    k_all = dot(rows, wk_ref[...])
    v_all = dot(rows, wv_ref[...]).astype(BF)
    v_ref[...] = v_all
    for j in range(q_all.shape[1] // HD):
        cols = slice(j * HD, (j + 1) * HD)
        q = rope_rows(q_all[:, cols], cos, sin).astype(BF)
        k = rope_rows(k_all[:, cols], cos, sin).astype(BF)
        q_ref[:, cols] = q
        k_ref[:, cols] = k
        scores = dot_nt(own_rows(q, chunk, ring), k) * scale + shift
        weights = jax.nn.sigmoid(scores) * ok
        mass_ref[j] = jnp.sum(weights, axis=-1, keepdims=True)
        att_ref[:, cols] = dot(weights.astype(BF), v_all[:, cols]).astype(BF)


def attend(x_seq, wq, wk, wv, cos, sin, ok_own, chunk, ring, scale, shift):
    seq, width = x_seq.shape
    cols = wq.shape[1]
    heads = cols // HD
    step = min(2, heads)
    own = ok_own.shape[0]
    whole = lambda *shape: pl.BlockSpec(shape, lambda i: (0,) * len(shape))
    wspec = pl.BlockSpec((width, step * HD), lambda i: (0, i))
    sspec = pl.BlockSpec((seq, step * HD), lambda i: (0, i))
    return pl.pallas_call(
        functools.partial(attend_kernel, chunk, ring, scale, shift),
        grid=(heads // step,),
        in_specs=[whole(seq, width), wspec, wspec, wspec, whole(seq, HD), whole(seq, HD),
                  whole(own, seq)],
        out_specs=[sspec, sspec, sspec,
                   pl.BlockSpec((own, step * HD), lambda i: (0, i)),
                   pl.BlockSpec((step, own, 1), lambda i: (i, 0, 0))],
        out_shape=[jax.ShapeDtypeStruct((seq, cols), BF)] * 3
        + [jax.ShapeDtypeStruct((own, cols), BF), jax.ShapeDtypeStruct((heads, own, 1), F32)],
        compiler_params=pltpu.CompilerParams(vmem_limit_bytes=VMEM_LIMIT),
        cost_estimate=pl.CostEstimate(
            flops=2 * seq * width * cols * 3, bytes_accessed=6 * width * cols, transcendentals=0
        ),
    )(x_seq, wq, wk, wv, cos, sin, ok_own)


def attend_back_kernel(
    chunk, ring, scale, shift,
    bb_ref, wo_ref, q_ref, k_ref, v_ref, cos_ref, sin_ref, ok_ref,
    qb_ref, kb_ref, vb_ref, att_ref, qo_ref, ko_ref, vo_ref,
):
    cos, sin, ok = cos_ref[...], sin_ref[...], ok_ref[...]
    ab_all = dot_nt(bb_ref[...], wo_ref[...]).astype(BF)
    for j in range(ab_all.shape[1] // HD):
        cols = slice(j * HD, (j + 1) * HD)
        q, k, v, ab = q_ref[:, cols], k_ref[:, cols], v_ref[:, cols], ab_all[:, cols]
        sig = jax.nn.sigmoid(dot_nt(q, k) * scale + shift)
        weights = (sig * ok).astype(BF)
        att_ref[:, cols] = dot(weights, v).astype(BF)
        back = (dot_nt(ab, v) * sig * (1.0 - sig) * ok).astype(BF)
        qb = rope_back_rows(dot(back, k) * scale, cos, sin).astype(BF)
        kb = rope_back_rows(dot_tn(back, q) * scale, cos, sin).astype(BF)
        vb = dot_tn(weights, ab).astype(BF)
        qb_ref[:, cols] = qb
        kb_ref[:, cols] = kb
        vb_ref[:, cols] = vb
        qo_ref[:, cols] = own_rows(qb, chunk, ring)
        ko_ref[:, cols] = own_rows(kb, chunk, ring)
        vo_ref[:, cols] = own_rows(vb, chunk, ring)


def attend_back(bb_seq, wo, q, k, v, cos, sin, ok, chunk, ring, scale, shift):
    seq, width = bb_seq.shape
    cols = wo.shape[0]
    heads = cols // HD
    step = min(2, heads)
    own = seq // ring
    whole = lambda *shape: pl.BlockSpec(shape, lambda i: (0,) * len(shape))
    sspec = pl.BlockSpec((seq, step * HD), lambda i: (0, i))
    ospec = pl.BlockSpec((own, step * HD), lambda i: (0, i))
    return pl.pallas_call(
        functools.partial(attend_back_kernel, chunk, ring, scale, shift),
        grid=(heads // step,),
        in_specs=[whole(seq, width), pl.BlockSpec((step * HD, width), lambda i: (i, 0)),
                  sspec, sspec, sspec, whole(seq, HD), whole(seq, HD), whole(seq, seq)],
        out_specs=[sspec] * 4 + [ospec] * 3,
        out_shape=[jax.ShapeDtypeStruct((seq, cols), BF)] * 4
        + [jax.ShapeDtypeStruct((own, cols), BF)] * 3,
        compiler_params=pltpu.CompilerParams(vmem_limit_bytes=VMEM_LIMIT),
        cost_estimate=pl.CostEstimate(
            flops=2 * seq * width * cols + 14 * seq * seq * cols,
            bytes_accessed=2 * (seq + cols) * width + 20 * seq * cols,
            transcendentals=seq * seq * heads,
        ),
    )(bb_seq, wo, q, k, v, cos, sin, ok)


def gate_math(gate, up, hidden_back):
    sig = jax.nn.sigmoid(gate)
    act = gate * sig
    hidden = (act * up).astype(BF)
    gate_back = (hidden_back * up * sig * (1.0 + gate * (1.0 - sig))).astype(BF)
    up_back = (hidden_back * act).astype(BF)
    return hidden, gate_back, up_back


def mlp_kernel(x_ref, cot_ref, wg_ref, wu_ref, wd_ref, back_ref, out_ref, back_acc, out_acc):
    step = pl.program_id(0)
    x, cot = x_ref[...], cot_ref[...]
    wg, wu, wd = wg_ref[...], wu_ref[...], wd_ref[...]
    hidden, gate_back, up_back = gate_math(dot(x, wg), dot(x, wu), dot_nt(cot, wd))
    back = dot_nt(gate_back, wg) + dot_nt(up_back, wu)
    out = dot(hidden, wd)

    @pl.when(step == 0)
    def _():
        back_acc[...] = back
        out_acc[...] = out

    @pl.when(step > 0)
    def _():
        back_acc[...] += back
        out_acc[...] += out

    @pl.when(step == pl.num_programs(0) - 1)
    def _():
        back_ref[...] = back_acc[...].astype(BF)
        out_ref[...] = out_acc[...].astype(BF)


def mlp(x, cot, wg, wu, wd):
    rows, width = x.shape
    units = wg.shape[1]
    block = min(512, units)
    whole = pl.BlockSpec((rows, width), lambda i: (0, 0))
    wspec = pl.BlockSpec((width, block), lambda i: (0, i))
    return pl.pallas_call(
        mlp_kernel,
        grid=(units // block,),
        in_specs=[whole, whole, wspec, wspec, pl.BlockSpec((block, width), lambda i: (i, 0))],
        out_specs=[whole, whole],
        out_shape=[jax.ShapeDtypeStruct((rows, width), BF)] * 2,
        scratch_shapes=[pltpu.VMEM((rows, width), F32)] * 2,
        compiler_params=pltpu.CompilerParams(vmem_limit_bytes=VMEM_LIMIT),
        cost_estimate=pl.CostEstimate(
            flops=12 * rows * width * units, bytes_accessed=6 * width * units, transcendentals=0
        ),
    )(x, cot, wg, wu, wd)


def mlp_grad_kernel(
    tile, x_ref, cot_ref, xb_ref, cb_ref, wg_ref, wu_ref, wd_ref, *rest
):
    gg_ref, ug_ref, dg_ref, hid, gbk, ubk = rest[-6:]
    wg, wu, wd = wg_ref[...], wu_ref[...], wd_ref[...]

    def part(i, _):
        at = pl.ds(pl.multiple_of(i * tile, tile), tile)
        x, cot = x_ref[at, :], cot_ref[at, :]
        hid[at, :], gbk[at, :], ubk[at, :] = gate_math(dot(x, wg), dot(x, wu), dot_nt(cot, wd))
        return 0

    lax.fori_loop(0, x_ref.shape[0] // tile, part, 0)
    xb = xb_ref[...]
    gg_ref[...] = dot_tn(xb, gbk[...])
    ug_ref[...] = dot_tn(xb, ubk[...])
    dg_ref[...] = dot_tn(hid[...], cb_ref[...])


def mlp_grad(x, cot, xb, cb, wg, wu, wd, first, count, before):
    rows, width = x.shape
    units = wg.shape[1]
    block = 256
    out = xb.shape[1]
    whole = lambda a: pl.BlockSpec(a.shape, lambda i: (0, 0))
    wspec = pl.BlockSpec((width, block), lambda i: (0, i + first))
    dspec = pl.BlockSpec((block, width), lambda i: (i + first, 0))
    any_spec = pl.BlockSpec(memory_space=pl.ANY)
    return pl.pallas_call(
        functools.partial(mlp_grad_kernel, min(512, rows)),
        grid=(count,),
        in_specs=[whole(x), whole(cot), whole(xb), whole(cb), wspec, wspec, dspec]
        + [any_spec] * len(before),
        out_specs=[pl.BlockSpec((out, block), lambda i: (0, i + first))] * 2
        + [pl.BlockSpec((block, out), lambda i: (i + first, 0))],
        out_shape=[jax.ShapeDtypeStruct((out, units), F32)] * 2
        + [jax.ShapeDtypeStruct((units, out), F32)],
        scratch_shapes=[pltpu.VMEM((rows, block), BF)] * 3,
        input_output_aliases={7 + i: i for i in range(len(before))},
        compiler_params=pltpu.CompilerParams(vmem_limit_bytes=VMEM_LIMIT),
        cost_estimate=pl.CostEstimate(
            flops=6 * rows * block * count * (width + out),
            bytes_accessed=6 * width * block * count + 8 * rows * width,
            transcendentals=0,
        ),
    )(x, cot, xb, cb, wg, wu, wd, *before)


def row_mean(values):
    return jnp.mean(values, axis=-1, keepdims=True)


def norm_parts(values):
    root = lax.rsqrt(row_mean(values * values) + EPS)
    return values * root, root


def norm_back(upstream, scaled, root, gain):
    inner = upstream * gain
    return root * (inner - scaled * row_mean(inner * scaled))


def per_device(
    activations, cotangent, doc_ids, attn_gain, query_weight, key_weight, value_weight,
    out_weight, mlp_gain, gate_weight, up_weight, down_weight,
):
    rows, width = activations.shape[1:]
    n_dp, n_ctx, n_t = lax.axis_size("dp"), lax.axis_size("ctx"), lax.axis_size("tensor")
    dp, ctx, place = lax.axis_index("dp"), lax.axis_index("ctx"), lax.axis_index("tensor")
    chunk = rows // n_t
    length = rows * n_ctx
    slots = slot_order(n_t)
    scale, shift = HD ** (-0.5), -math.log(length)
    gain_first, gain_second = attn_gain.astype(F32), mlp_gain.astype(F32)

    def slotted(values):
        return jnp.concatenate(
            [lax.dynamic_slice_in_dim(values, (place ^ s) * chunk, chunk, 0) for s in slots], axis=0
        )

    inputs = slotted(activations[0])
    cot = slotted(cotangent[0])
    inputs32 = inputs.astype(F32)
    scaled_first, root_first = norm_parts(inputs32)
    normed_first = (scaled_first * gain_first).astype(BF)

    half = rows // 2 if n_t > 1 else rows
    mine = normed_first[:half]
    rings = [mine] + [turn(mine, "ctx", k) for k in range(1, n_ctx)]
    part = jnp.concatenate(
        [r[i * chunk : (i + 1) * chunk] for i in range(half // chunk) for r in rings], axis=0
    )
    x_seq = jnp.concatenate([part, swap(part, "tensor", 1)], axis=0) if n_t > 1 else part

    ring_at = ((ctx - jnp.arange(n_ctx, dtype=jnp.int32)) % n_ctx) * rows
    slot_at = (place ^ jnp.array(slots, jnp.int32)) * chunk
    spots = (
        slot_at[:, None, None] + ring_at[None, :, None]
        + jnp.arange(chunk, dtype=jnp.int32)[None, None, :]
    ).reshape(-1)
    cuts = [jnp.sum((doc_ids[0] < j).astype(jnp.int32)) for j in range(1, 4)]
    docs = sum((spots >= cut).astype(jnp.int32) for cut in cuts)
    allowed = (
        (spots[None, :] <= spots[:, None]) & (docs[None, :] == docs[:, None])
    ).astype(F32)
    allowed_own = allowed.reshape(n_t, n_ctx, chunk, length)[:, 0].reshape(rows, length)
    frequency = 10000.0 ** (-jnp.arange(HD // 2, dtype=F32) * 2.0 / HD)
    angles = spots.astype(F32)[:, None] * frequency[None, :]
    cos, sin = jnp.cos(angles), jnp.sin(angles)
    cos = jnp.concatenate([cos, cos], axis=1)
    sin = jnp.concatenate([-sin, sin], axis=1)

    cot_all = gather_tensor(gather_dp(gather_tokens(cot[:chunk])))

    q, k, v, attended, mass = attend(
        x_seq, query_weight, key_weight, value_weight, cos, sin, allowed_own,
        chunk, n_ctx, scale, shift,
    )
    attn_mass = from_slots(mass[:, :, 0].T, slots, place)

    branch = scatter_tensor(jnp.dot(attended, out_weight, preferred_element_type=F32).astype(BF))
    middle = inputs32[:chunk] + branch
    scaled_second, root_second = norm_parts(middle)
    normed_chunk = (scaled_second * gain_second).astype(BF)
    normed_second = gather_tensor(normed_chunk)
    second_part, mlp_part = mlp(normed_second, cot, gate_weight, up_weight, down_weight)
    x_all = gather_tensor(gather_dp(gather_tokens(normed_chunk)))

    second_back = scatter_tensor(second_part)
    mlp_gain_part = jnp.sum(second_back * scaled_second, axis=0)
    middle_back = cot[:chunk].astype(F32) + norm_back(
        second_back, scaled_second, root_second, gain_second
    )
    branch_back = gather_tensor(gather_tokens(middle_back.astype(BF)))

    layer_out = (middle + scatter_tensor(mlp_part)).astype(BF)
    layer_out = from_slots(gather_tensor(layer_out), slots, place)

    qb, kb, vb, attended_all, q_own, k_own, v_own = attend_back(
        branch_back, out_weight, q, k, v, cos, sin, allowed, chunk, n_ctx, scale, shift
    )
    first_part = (
        jnp.einsum("tc,dc->td", q_own, query_weight, preferred_element_type=F32)
        + jnp.einsum("tc,dc->td", k_own, key_weight, preferred_element_type=F32)
        + jnp.einsum("tc,dc->td", v_own, value_weight, preferred_element_type=F32)
    )
    first_back = scatter_tensor(first_part.astype(BF))
    scaled_chunk, root_chunk = scaled_first[:chunk], root_first[:chunk]
    attn_gain_part = jnp.sum(first_back * scaled_chunk, axis=0)
    input_grad = (
        middle_back + norm_back(first_back, scaled_chunk, root_chunk, gain_first)
    ).astype(BF)
    input_grad = from_slots(gather_tensor(input_grad), slots, place)

    out_cols = width // (n_dp * n_ctx)

    def block_of(values, step):
        owner = ((dp + step) % n_dp) * n_ctx + ctx
        return lax.dynamic_slice_in_dim(values, owner * out_cols, out_cols, 1)

    def summed(make):
        total = make(0)
        for step in range(1, n_dp):
            total = total + turn(make(step).astype(BF), "dp", step).astype(F32)
        return total

    grads = jnp.concatenate([qb, kb, vb], axis=1)
    qkv_grad = summed(
        lambda step: jnp.einsum(
            "td,tc->dc", block_of(x_seq, step), grads, preferred_element_type=F32
        )
    )
    query_grad, key_grad, value_grad = jnp.split(qkv_grad, 3, axis=1)
    out_grad = summed(
        lambda step: jnp.einsum(
            "tc,td->cd", attended_all, block_of(branch_back, step), preferred_element_type=F32
        )
    )
    blocks = gate_weight.shape[1] // 256
    calls = min(4, blocks)
    mlp_grads = ()
    for call in range(calls):
        mlp_grads = mlp_grad(
            x_all, cot_all, block_of(x_all, 0), block_of(cot_all, 0),
            gate_weight, up_weight, down_weight,
            call * blocks // calls, blocks // calls, mlp_grads,
        )
    gate_grad, up_grad, down_grad = mlp_grads

    gains = jnp.stack([attn_gain_part, mlp_gain_part])
    for bit in bits_of(n_t):
        gains = gains + swap(gains, "tensor", bit)
    gains = gains.reshape(2, n_dp * n_ctx, out_cols)

    def gain_block(step_dp, step_ctx):
        owner = ((dp + step_dp) % n_dp) * n_ctx + (ctx + step_ctx) % n_ctx
        return lax.dynamic_index_in_dim(gains, owner, 1, False)

    total = []
    for step_ctx in range(n_ctx):
        piece = gain_block(0, step_ctx)
        for step_dp in range(1, n_dp):
            piece = piece + turn(gain_block(step_dp, step_ctx), "dp", step_dp)
        total.append(turn(piece, "ctx", step_ctx) if step_ctx else piece)
    gain_grads = sum(total)

    return (
        layer_out[None], input_grad[None], gain_grads[0], query_grad, key_grad, value_grad,
        out_grad, gain_grads[1], gate_grad, up_grad, down_grad, attn_mass[None],
    )


def solution(mesh):
    return jax.shard_map(
        per_device,
        mesh=mesh,
        in_specs=(
            P("dp", "ctx", None),
            P("dp", "ctx", None),
            P("dp", None),
            P(),
            P(None, "tensor"),
            P(None, "tensor"),
            P(None, "tensor"),
            P("tensor", None),
            P(),
            P(None, "tensor"),
            P(None, "tensor"),
            P("tensor", None),
        ),
        out_specs=(
            P("dp", "ctx", None),
            P("dp", "ctx", None),
            P(("dp", "ctx")),
            P(("dp", "ctx"), "tensor"),
            P(("dp", "ctx"), "tensor"),
            P(("dp", "ctx"), "tensor"),
            P("tensor", ("dp", "ctx")),
            P(("dp", "ctx")),
            P(("dp", "ctx"), "tensor"),
            P(("dp", "ctx"), "tensor"),
            P("tensor", ("dp", "ctx")),
            P("dp", "ctx", "tensor"),
        ),
        check_vma=False,
    )
```

```python
import functools
import math

import jax
import jax.numpy as jnp
import numpy as np
from jax import lax
from jax.experimental import pallas as pl
from jax.experimental.pallas import tpu as pltpu
from jax.sharding import PartitionSpec as P

HD = 128
EPS = 1e-05
BF = jnp.bfloat16
F32 = jnp.float32
MIB = 1024 * 1024


def swap(values, axis, distance):
    count = lax.axis_size(axis)
    return lax.ppermute(values, axis, [(i, i ^ distance) for i in range(count)])


def turn(values, axis, shift):
    count = lax.axis_size(axis)
    return lax.ppermute(values, axis, [(i, (i + shift) % count) for i in range(count)])


def after(value, *others):
    return lax.optimization_barrier((value, others))[0]


def in_hbm(values):
    return pltpu.with_memory_space_constraint(values, pltpu.HBM)


def in_vmem(values):
    return pltpu.with_memory_space_constraint(values, pltpu.VMEM)


def bits_of(count):
    return [1 << i for i in range(count.bit_length() - 1)]


def slot_order(count):
    order = [0]
    for bit in reversed(bits_of(count)):
        order = order + [slot ^ bit for slot in order]
    return order


def gather_tensor(rows):
    for bit in reversed(bits_of(lax.axis_size("tensor"))):
        rows = jnp.concatenate([rows, swap(rows, "tensor", bit)], axis=0)
    return rows


def scatter_tensor(rows, beside=()):
    bits = bits_of(lax.axis_size("tensor"))
    for bit in bits:
        half = rows.shape[0] // 2
        got = swap(rows[half:].astype(BF), "tensor", bit)
        if bit == bits[-1]:
            got = after(got, beside)
        rows = rows[:half].astype(F32) + got.astype(F32)
    return rows


def ring_of(rows):
    return [rows] + [turn(rows, "ctx", k) for k in range(1, lax.axis_size("ctx"))]


def from_slots(blocks, slots, place):
    size = blocks.shape[0] // len(slots)
    out = jnp.zeros_like(blocks)
    for index, slot in enumerate(slots):
        out = lax.dynamic_update_slice_in_dim(
            out, blocks[index * size : (index + 1) * size], (place ^ slot) * size, 0
        )
    return out


def rope_rows(u, cos, sin):
    return u * cos + pltpu.roll(u, HD // 2, 1) * sin


def rope_back_rows(u, cos, sin):
    return u * cos - pltpu.roll(u, HD // 2, 1) * sin


def dot(a, b):
    return lax.dot_general(a, b, (((1,), (0,)), ((), ())), preferred_element_type=F32)


def dot_nt(a, b):
    return lax.dot_general(a, b, (((1,), (1,)), ((), ())), preferred_element_type=F32)


def dot_tn(a, b):
    return lax.dot_general(a, b, (((0,), (0,)), ((), ())), preferred_element_type=F32)


def place_rows(step, pieces, places, rows, sem, start=True, wait=True):
    @pl.when(step == 0)
    def _():
        copies = []
        for i, (piece, place) in enumerate(zip(pieces, places, strict=True)):
            copies.append(pltpu.make_async_copy(piece, rows.at[place], sem.at[i]))
        if start:
            for copy in copies:
                copy.start()
        if wait:
            for copy in copies:
                copy.wait()


def chunk_places(at_ref, first, count, chunk):
    return [
        pl.ds(pl.multiple_of(at_ref[first + i] * chunk, chunk), chunk) for i in range(count)
    ]


NEVER = -1e30


def attend_kernel(chunk, slots, scale, shift, at_ref, *refs):
    count = len(refs) - 17
    pieces = refs[:count]
    (own_spot_ref, own_doc_ref, doc_ref, cos_ref, sin_ref, wq_ref, wk_ref, wv_ref,
     q_ref, k_ref, v_ref, att_ref, mass_ref, seq_hbm, x, sem, out_sem) = refs[count:]
    step, last = pl.program_id(0), pl.num_programs(0) - 1
    place_rows(step, pieces, chunk_places(at_ref, 0, count, chunk), x, sem)
    keep = pltpu.make_async_copy(x, seq_hbm, out_sem)

    @pl.when(step == 0)
    def _():
        keep.start()

    cos, sin = cos_ref[...], sin_ref[...]
    shape = (own_spot_ref.shape[0], doc_ref.shape[1])
    allowed = (lax.broadcasted_iota(jnp.int32, shape, 1) <= own_spot_ref[...]) & (
        own_doc_ref[...] == doc_ref[...]
    )
    bias = jnp.where(allowed, shift, NEVER)
    rows = x[...]
    q_all = dot(rows, wq_ref[...])
    k_all = dot(rows, wk_ref[...])
    v_all = dot(rows, wv_ref[...]).astype(BF)
    v_ref[...] = v_all
    own = chunk_places(at_ref, 0, slots, chunk)
    for j in range(q_all.shape[1] // HD):
        cols = slice(j * HD, (j + 1) * HD)
        q_ref[:, cols] = rope_rows(q_all[:, cols], cos, sin).astype(BF)
        k = rope_rows(k_all[:, cols], cos, sin).astype(BF)
        k_ref[:, cols] = k
        q = jnp.concatenate([q_ref[spot, cols] for spot in own], axis=0)
        weights = jax.nn.sigmoid(dot_nt(q, k) * scale + bias)
        mass_ref[j] = jnp.sum(weights, axis=-1, keepdims=True)
        att_ref[:, cols] = dot(weights.astype(BF), v_all[:, cols]).astype(BF)

    @pl.when(step == last)
    def _():
        keep.wait()


def attend(places, pieces, own_spots, own_docs, docs, cos, sin, wq, wk, wv, slots, scale, shift):
    chunk, width = pieces[0].shape
    seq, rows = chunk * len(pieces), own_spots.shape[0]
    cols = wq.shape[1]
    heads = cols // HD
    step = min(2, heads)
    whole = lambda *shape: pl.BlockSpec(
        shape, lambda i: (0,) * len(shape), pipeline_mode=pl.Buffered(1)
    )
    hbm = pl.BlockSpec(memory_space=pl.ANY)
    wspec = pl.BlockSpec((width, step * HD), lambda i: (0, i))
    sspec = pl.BlockSpec((seq, step * HD), lambda i: (0, i))
    return pl.pallas_call(
        functools.partial(attend_kernel, chunk, slots, scale, shift),
        grid=(heads // step,),
        in_specs=[pl.BlockSpec(memory_space=pltpu.SMEM)] + [hbm] * len(pieces)
        + [whole(rows, 1), whole(rows, 1), whole(1, seq), whole(seq, HD), whole(seq, HD)]
        + [wspec] * 3,
        out_specs=[sspec, sspec, sspec,
                   pl.BlockSpec((rows, step * HD), lambda i: (0, i)),
                   pl.BlockSpec((step, rows, 1), lambda i: (i, 0, 0)),
                   pl.BlockSpec(memory_space=pltpu.HBM)],
        out_shape=[jax.ShapeDtypeStruct((seq, cols), BF)] * 3
        + [jax.ShapeDtypeStruct((rows, cols), BF), jax.ShapeDtypeStruct((heads, rows, 1), F32),
           jax.ShapeDtypeStruct((seq, width), BF)],
        scratch_shapes=[pltpu.VMEM((seq, width), BF),
                        pltpu.SemaphoreType.DMA((len(pieces),)), pltpu.SemaphoreType.DMA],
        compiler_params=pltpu.CompilerParams(vmem_limit_bytes=56 * MIB),
        cost_estimate=pl.CostEstimate(
            flops=2 * seq * width * cols * 3, bytes_accessed=6 * width * cols, transcendentals=0
        ),
    )(places, *pieces, own_spots, own_docs, docs, cos, sin,
      wq, wk, wv)


def attend_back_kernel(chunk, slots, scale, shift, at_ref, starts_ref, *refs):
    count = len(refs) - 23
    pieces = refs[:count]
    (wo_ref, q_ref, k_ref, v_ref, cos_ref, sin_ref, doc_row_ref, doc_ref,
     x_hbm, wq_hbm, wk_hbm, wv_hbm, mine_ref, theirs_ref, first_ref,
     bb, x_cols, w_cols, acc, every, bb_sem, x_sem, w_sem) = refs[count:]
    step = pl.program_id(0)
    owners = x_cols.shape[0]
    spots = chunk_places(at_ref, 0, count, chunk)
    place_rows(step, pieces, spots, bb, bb_sem, wait=False)
    seq, size, width = bb.shape[0], x_cols.shape[2], w_cols.shape[2]
    starts = [pl.multiple_of(starts_ref[i], HD) for i in range(owners)]
    at = pl.ds(pl.multiple_of(step * width, HD), width)
    copies = [
        pltpu.make_async_copy(x_hbm.at[:, pl.ds(starts[i], size)], x_cols.at[i], x_sem.at[i])
        for i in range(owners)
    ] + [
        pltpu.make_async_copy(w_hbm.at[:, at], w_cols.at[i], w_sem.at[i])
        for i, w_hbm in enumerate((wq_hbm, wk_hbm, wv_hbm))
    ]
    for copy in copies:
        copy.start()

    block = min(256, seq)
    parts = [slice(i * block, (i + 1) * block) for i in range(seq // block)]
    heads = [slice(j * HD, (j + 1) * HD) for j in range(width // HD)]
    weights, attended = {}, []
    for i, part in enumerate(parts):
        shape = (block, part.stop)
        allowed = (
            lax.broadcasted_iota(jnp.int32, shape, 1)
            <= lax.broadcasted_iota(jnp.int32, shape, 0) + part.start
        ) & (doc_ref[part, :] == doc_row_ref[:, : part.stop])
        bias = jnp.where(allowed, shift, NEVER)
        row = []
        for j, cols in enumerate(heads):
            scores = dot_nt(q_ref[part, cols], k_ref[: part.stop, cols]) * scale + bias
            weights[i, j] = jax.nn.sigmoid(scores)
            row.append(dot(weights[i, j].astype(BF), v_ref[: part.stop, cols]).astype(BF))
        attended.append(jnp.concatenate(row, axis=1))
    attended = jnp.concatenate(attended, axis=0)

    place_rows(step, pieces, spots, bb, bb_sem, start=False)
    ab_all = dot_nt(bb[...], wo_ref[...]).astype(BF)
    for j, cols in enumerate(heads):
        key_sums, value_sums = [None] * len(parts), [None] * len(parts)
        for i, part in enumerate(parts):
            ab, weight = ab_all[part, cols], weights[i, j]
            slope = weight - weight * weight
            back = (dot_nt(ab, v_ref[: part.stop, cols]) * slope).astype(BF)
            weight = weight.astype(BF)
            query_back = dot(back, k_ref[: part.stop, cols]) * scale
            every[part, cols] = rope_back_rows(
                query_back, cos_ref[part, :], sin_ref[part, :]
            ).astype(BF)
            for n in range(i + 1):
                key_part = dot_tn(back[:, parts[n]], q_ref[part, cols])
                value_part = dot_tn(weight[:, parts[n]], ab)
                key_sums[n] = key_part if i == n else key_sums[n] + key_part
                value_sums[n] = value_part if i == n else value_sums[n] + value_part
        for n, part in enumerate(parts):
            at_key = slice(width + cols.start, width + cols.stop)
            at_value = slice(2 * width + cols.start, 2 * width + cols.stop)
            every[part, at_key] = rope_back_rows(
                key_sums[n] * scale, cos_ref[part, :], sin_ref[part, :]
            ).astype(BF)
            every[part, at_value] = value_sums[n].astype(BF)

    def give(i, n, part):
        if i == 0:
            mine_ref[n] = part
        else:
            theirs_ref[i - 1, n] = part.astype(BF)

    for i in range(owners):
        give(i, 3, dot_tn(bb[:, pl.ds(starts[i], size)], attended))

    for copy in copies:
        copy.wait()
    for i in range(owners):
        total = dot_tn(x_cols[i], every[...])
        for n in range(3):
            give(i, n, total[:, n * width : (n + 1) * width])
    own = jnp.concatenate([every[spot, :] for spot in spots[:slots]], axis=0)
    first = sum(dot_nt(own[:, n * width : (n + 1) * width], w_cols[n]) for n in range(3))

    @pl.when(step == 0)
    def _():
        acc[...] = first

    @pl.when(step > 0)
    def _():
        acc[...] += first

    @pl.when(step == pl.num_programs(0) - 1)
    def _():
        first_ref[...] = acc[...].astype(BF)


def attend_back(
    places, starts, pieces, wo, q, k, v, cos, sin, docs, doc_column, x_seq, wq, wk, wv,
    size, slots, scale, shift,
):
    seq, width = x_seq.shape
    chunk = pieces[0].shape[0]
    cols = wo.shape[0]
    heads = cols // HD
    step = min(2, heads)
    own = slots * chunk
    owners = starts.shape[0]
    whole = lambda *shape: pl.BlockSpec(
        shape, lambda i: (0,) * len(shape), pipeline_mode=pl.Buffered(1)
    )
    sspec = pl.BlockSpec((seq, step * HD), lambda i: (0, i))
    hbm = pl.BlockSpec(memory_space=pl.ANY)
    return pl.pallas_call(
        functools.partial(attend_back_kernel, chunk, slots, scale, shift),
        grid=(heads // step,),
        in_specs=[pl.BlockSpec(memory_space=pltpu.SMEM)] * 2 + [hbm] * len(pieces)
        + [pl.BlockSpec((step * HD, width), lambda i: (i, 0)),
           sspec, sspec, sspec, whole(seq, HD), whole(seq, HD), whole(1, seq), whole(seq, 1)]
        + [hbm] * 4,
        out_specs=[pl.BlockSpec((4, size, step * HD), lambda i: (0, 0, i)),
                   pl.BlockSpec((owners - 1, 4, size, step * HD), lambda i: (0, 0, 0, i)),
                   whole(own, width)],
        out_shape=[jax.ShapeDtypeStruct((4, size, cols), F32),
                   jax.ShapeDtypeStruct((owners - 1, 4, size, cols), BF),
                   jax.ShapeDtypeStruct((own, width), BF)],
        scratch_shapes=[pltpu.VMEM((seq, width), BF), pltpu.VMEM((owners, seq, size), BF),
                        pltpu.VMEM((3, width, step * HD), BF),
                        pltpu.VMEM((own, width), F32),
                        pltpu.VMEM((seq, 3 * step * HD), BF),
                        pltpu.SemaphoreType.DMA((len(pieces),)),
                        pltpu.SemaphoreType.DMA((owners,)), pltpu.SemaphoreType.DMA((3,))],
        compiler_params=pltpu.CompilerParams(vmem_limit_bytes=56 * MIB),
        cost_estimate=pl.CostEstimate(
            flops=2 * seq * width * cols + 14 * seq * seq * cols,
            bytes_accessed=2 * (seq + cols) * width + 20 * seq * cols,
            transcendentals=seq * seq * heads,
        ),
    )(
        places, starts, *pieces, in_hbm(wo), q, k, v, cos, sin,
        docs, doc_column, in_hbm(x_seq), in_hbm(wq), in_hbm(wk), in_hbm(wv),
    )


def gate_math(gate, up, hidden_back):
    sig = jax.nn.sigmoid(gate)
    act = gate * sig
    hidden = (act * up).astype(BF)
    gate_back = (hidden_back * up * sig * (1.0 + gate * (1.0 - sig))).astype(BF)
    up_back = (hidden_back * act).astype(BF)
    return hidden, gate_back, up_back


def mlp_kernel(x_ref, hb_ref, wg_ref, wu_ref, hidden_ref, back_ref, acc):
    step = pl.program_id(0)
    x, wg, wu = x_ref[...], wg_ref[...], wu_ref[...]
    hidden, gate_back, up_back = gate_math(dot(x, wg), dot(x, wu), hb_ref[...].astype(F32))
    hidden_ref[...] = hidden
    back = dot_nt(gate_back, wg) + dot_nt(up_back, wu)

    @pl.when(step == 0)
    def _():
        acc[...] = back

    @pl.when(step > 0)
    def _():
        acc[...] += back

    @pl.when(step == pl.num_programs(0) - 1)
    def _():
        back_ref[...] = acc[...].astype(BF)


def mlp(x, hidden_back, wg, wu):
    rows, width = x.shape
    units = wg.shape[1]
    block = min(512, units)
    whole = pl.BlockSpec((rows, width), lambda i: (0, 0), pipeline_mode=pl.Buffered(1))
    wspec = pl.BlockSpec((width, block), lambda i: (0, i))
    uspec = pl.BlockSpec((rows, block), lambda i: (0, i))
    return pl.pallas_call(
        mlp_kernel,
        grid=(units // block,),
        in_specs=[whole, uspec, wspec, wspec],
        out_specs=[uspec, whole],
        out_shape=[
            jax.ShapeDtypeStruct((rows, units), BF), jax.ShapeDtypeStruct((rows, width), BF)
        ],
        scratch_shapes=[pltpu.VMEM((rows, width), F32)],
        compiler_params=pltpu.CompilerParams(vmem_limit_bytes=56 * MIB),
        cost_estimate=pl.CostEstimate(
            flops=8 * rows * width * units, bytes_accessed=4 * width * units, transcendentals=0
        ),
    )(x, hidden_back, in_hbm(wg), in_hbm(wu))


def hidden_back_kernel(tile, cot_hbm, wd_ref, out_ref, cot, sem):
    tiles = [pl.ds(i * tile, tile) for i in range(cot.shape[0] // tile)]
    copies = [
        pltpu.make_async_copy(cot_hbm.at[at], cot.at[at], sem.at[i]) for i, at in enumerate(tiles)
    ]

    def every_tile(waits):
        wd = wd_ref[...]
        for copy, at in zip(copies, tiles, strict=True):
            if waits:
                copy.wait()
            out_ref[at, :] = dot_nt(cot[at, :], wd).astype(BF)

    @pl.when(pl.program_id(0) == 0)
    def _():
        for copy in copies:
            copy.start()
        every_tile(True)

    @pl.when(pl.program_id(0) > 0)
    def _():
        every_tile(False)


def hidden_back_of(cot, wd):
    rows, width = cot.shape
    units = wd.shape[0]
    block, tile = min(512, units), 256
    return pl.pallas_call(
        functools.partial(hidden_back_kernel, tile),
        grid=(units // block,),
        in_specs=[pl.BlockSpec(memory_space=pl.ANY),
                  pl.BlockSpec((block, width), lambda i: (i, 0))],
        out_specs=pl.BlockSpec((rows, block), lambda i: (0, i)),
        out_shape=jax.ShapeDtypeStruct((rows, units), BF),
        scratch_shapes=[pltpu.VMEM((rows, width), BF), pltpu.SemaphoreType.DMA((rows // tile,))],
        compiler_params=pltpu.CompilerParams(vmem_limit_bytes=56 * MIB),
        cost_estimate=pl.CostEstimate(
            flops=2 * rows * width * units, bytes_accessed=2 * width * (rows + units),
            transcendentals=0,
        ),
    )(cot, in_hbm(wd))


def mlp_grad_kernel(count, chunk, at_ref, *refs):
    pieces = refs[:count]
    hb_ref, cb_ref, wg_ref, wu_ref = refs[count : count + 4]
    gg_ref, ug_ref, dg_ref, gain_ref, x_all, hid, gbk, ubk, sem = refs[-9:]
    size = cb_ref.shape[1]
    per = pieces[0].shape[0] // chunk
    own = pl.ds(pl.multiple_of(at_ref[0] * size, size), size)

    @pl.when(pl.program_id(0) == 0)
    def _():
        copies = []
        for i in range(count * per):
            spot = pl.ds(pl.multiple_of(at_ref[1 + i] * chunk, chunk), chunk)
            part = pieces[i // per].at[pl.ds(i % per * chunk, chunk)]
            copies.append(pltpu.make_async_copy(part, x_all.at[spot], sem.at[i]))
        for copy in copies:
            copy.start()
        for copy in copies:
            copy.wait()

    wg, wu = wg_ref[...], wu_ref[...]
    for i in range(x_all.shape[0] // 128):
        at = pl.ds(i * 128, 128)
        x = x_all[at, :]
        hid[at, :], gbk[at, :], ubk[at, :] = gate_math(
            dot(x, wg), dot(x, wu), hb_ref[at, :].astype(F32)
        )
    xb = x_all[:, own]
    gate_grad = dot_tn(xb, gbk[...])
    up_grad = dot_tn(xb, ubk[...])
    gg_ref[...] = gate_grad
    ug_ref[...] = up_grad
    dg_ref[...] = dot_tn(hid[...], cb_ref[...])
    gain = jnp.sum(
        wg_ref[own, :].astype(F32) * gate_grad + wu_ref[own, :].astype(F32) * up_grad,
        axis=1, keepdims=True,
    )

    @pl.when(pl.program_id(0) == 0)
    def _():
        gain_ref[...] = gain

    @pl.when(pl.program_id(0) > 0)
    def _():
        gain_ref[...] += gain


def mlp_grad(places, chunk, pieces, cot, hb, wg, wu, size, first, count, before):
    tile, width = pieces[0].shape
    rows, units = hb.shape
    block = min(256, count)
    skip = first // block
    wspec = pl.BlockSpec((width, block), lambda i, at: (0, i + skip))
    hbm = pl.BlockSpec(memory_space=pl.ANY)
    grid_spec = pltpu.PrefetchScalarGridSpec(
        num_scalar_prefetch=1,
        grid=(count // block,),
        in_specs=[hbm] * len(pieces)
        + [pl.BlockSpec((rows, block), lambda i, at: (0, i + skip)),
           pl.BlockSpec((rows, size), lambda i, at: (0, at[0]), pipeline_mode=pl.Buffered(1)),
           wspec, wspec]
        + [hbm] * len(before),
        out_specs=[pl.BlockSpec((size, block), lambda i, at: (0, i + skip))] * 2
        + [pl.BlockSpec((block, size), lambda i, at: (i + skip, 0)),
           pl.BlockSpec((size, 1), lambda i, at: (0, 0))],
        scratch_shapes=[pltpu.VMEM((rows, width), BF)]
        + [pltpu.VMEM((rows, block), BF)] * 3
        + [pltpu.SemaphoreType.DMA((rows // chunk,))],
    )
    return pl.pallas_call(
        functools.partial(mlp_grad_kernel, len(pieces), chunk),
        grid_spec=grid_spec,
        out_shape=[jax.ShapeDtypeStruct((size, units), F32)] * 2
        + [jax.ShapeDtypeStruct((units, size), F32), jax.ShapeDtypeStruct((size, 1), F32)],
        input_output_aliases={len(pieces) + 5 + i: i for i in range(len(before))},
        compiler_params=pltpu.CompilerParams(vmem_limit_bytes=56 * MIB),
        cost_estimate=pl.CostEstimate(
            flops=2 * rows * count * (2 * width + 3 * size),
            bytes_accessed=4 * width * count + 4 * rows * width,
            transcendentals=0,
        ),
    )(places, *pieces, hb, cot, in_hbm(wg), in_hbm(wu), *before)


def row_mean(values):
    return jnp.mean(values, axis=-1, keepdims=True)


def norm_parts(values):
    root = lax.rsqrt(row_mean(values * values) + EPS)
    return values * root, root


def norm_back(upstream, scaled, root, gain):
    inner = upstream * gain
    return root * (inner - scaled * row_mean(inner * scaled))


def per_device(
    activations, cotangent, doc_ids, attn_gain, query_weight, key_weight, value_weight,
    out_weight, mlp_gain, gate_weight, up_weight, down_weight,
):
    rows, width = activations.shape[1:]
    n_dp, n_ctx, n_t = lax.axis_size("dp"), lax.axis_size("ctx"), lax.axis_size("tensor")
    dp, ctx, place = lax.axis_index("dp"), lax.axis_index("ctx"), lax.axis_index("tensor")
    chunk = rows // n_t
    length = rows * n_ctx
    slots = slot_order(n_t)
    scale, shift = HD ** (-0.5), -math.log(length)
    gain_first, gain_second = attn_gain.astype(F32), mlp_gain.astype(F32)

    def slotted(values):
        return jnp.concatenate(
            [lax.dynamic_slice_in_dim(values, (place ^ s) * chunk, chunk, 0) for s in slots], axis=0
        )

    inputs32 = slotted(activations[0]).astype(F32)
    scaled_first, root_first = norm_parts(inputs32)
    normed_first = (scaled_first * gain_first).astype(BF)

    bits = list(reversed(bits_of(n_t)))

    def spread(rings, beside=()):
        lists = [[ring] for ring in rings]
        for bit in bits:
            lists = [items + [swap(item, "tensor", bit) for item in items] for items in lists]
            if bit == bits[0]:
                lists = after(lists, beside)
        return lists

    mine, *rings = ring_of(normed_first[:chunk])
    cot_all = lax.all_gather(
        lax.dynamic_slice_in_dim(after(cotangent[0], normed_first), place * chunk, chunk, 0),
        ("dp", "ctx", "tensor"), axis=0, tiled=True,
    )

    ring_at = (ctx - jnp.arange(n_ctx, dtype=jnp.int32) + n_ctx) % n_ctx
    seq_places = jnp.concatenate([
        ring_at[k : k + 1] * n_t + (place ^ slot) for k in range(n_ctx) for slot in slots
    ])
    docs = doc_ids
    doc_column = doc_ids.reshape(length, 1)
    out_cols = width // (n_dp * n_ctx)
    owners = jnp.stack([((dp + step) % n_dp) * n_ctx + ctx for step in range(n_dp)])
    starts = owners * out_cols
    owner = owners[0]
    places = [owner[None]]
    for flip in (0, 1):
        for step in range(n_dp):
            for slot in slots[: n_t // 2]:
                group = ((dp - step + n_dp) % n_dp) * n_ctx + ring_at
                places.append(group * n_t + (place ^ slot ^ flip))
    places = jnp.concatenate(places)
    own_spots = slotted(ctx * rows + jnp.arange(rows, dtype=jnp.int32)[:, None])
    own_docs = slotted(
        lax.dynamic_slice_in_dim(doc_ids.reshape(length, 1), ctx * rows, rows, 0)
    )
    frequency = np.float32(10000.0) ** (
        -np.arange(HD // 2, dtype=np.float32) * np.float32(2.0) / np.float32(HD)
    )
    angles = np.arange(length, dtype=np.float32)[:, None] * frequency[None, :]
    cos = jnp.asarray(np.concatenate([np.cos(angles), np.cos(angles)], axis=1))
    sin = jnp.asarray(np.concatenate([-np.sin(angles), np.sin(angles)], axis=1))
    cot = slotted(cotangent[0])
    rings = after(rings, seq_places, own_spots, own_docs, cot, starts, places, doc_column)
    hidden_back = lax.dot_general(
        after(cot, rings), down_weight, (((1,), (1,)), ((), ())), preferred_element_type=F32
    ).astype(BF)
    seq_pieces = spread(rings, hidden_back)
    own_pieces = [normed_first[i * chunk : (i + 1) * chunk] for i in range(n_t)]
    q, k, v, attended, mass, x_seq = attend(
        seq_places, own_pieces + sum(seq_pieces, []), own_spots, own_docs, docs, cos, sin,
        query_weight, key_weight, value_weight, n_t, scale, shift,
    )
    attn_mass = from_slots(mass[:, :, 0].T, slots, place)

    def over_dp(items):
        return [turn(item, "dp", step) for step in range(1, n_dp) for item in items]

    def over_tensor(items, bits):
        for bit in bits:
            items = items + [swap(item, "tensor", bit) for item in items]
        return items

    branch = scatter_tensor(
        jnp.dot(attended, out_weight, preferred_element_type=F32).astype(BF), attn_mass
    )
    middle = inputs32[:chunk] + branch
    scaled_second, root_second = norm_parts(middle)
    normed_chunk = (scaled_second * gain_second).astype(BF)
    normed_second = gather_tensor(normed_chunk)
    chunk_rings = ring_of(normed_chunk)
    hidden, second_part = mlp(normed_second, hidden_back, gate_weight, up_weight)
    second_part, chunk_rings = lax.optimization_barrier((second_part, chunk_rings))
    x_near = [jnp.concatenate(chunk_rings, axis=0)]
    x_far = over_dp(x_near)
    x_near_more = over_tensor(x_near, bits[:-1])[1:]
    second_back = scatter_tensor(second_part)
    middle_back = cot[:chunk].astype(F32) + norm_back(
        second_back, scaled_second, root_second, gain_second
    )
    branch_back = middle_back.astype(BF)
    bb_rings = ring_of(branch_back)
    hidden_back_all = hidden_back_of(after(cot_all, branch_back), down_weight)
    bb_rings, x_far, x_near_more = after((bb_rings, x_far, x_near_more), hidden_back_all)
    mlp_part = jnp.dot(
        after(hidden, bb_rings), down_weight, preferred_element_type=F32
    ).astype(BF)
    bb_pieces = spread(bb_rings, mlp_part)
    x_far_more = over_tensor(x_far, bits[:-1])[len(x_far) :]

    mine_grads, theirs_grads, first_part = attend_back(
        seq_places, starts, sum(bb_pieces, []), out_weight, q, k, v, cos, sin, docs, doc_column,
        x_seq, query_weight, key_weight, value_weight, out_cols, n_t, scale, shift,
    )

    theirs = [turn(theirs_grads[step - 1], "dp", step) for step in range(1, n_dp)]

    x_pieces = over_tensor(x_near + x_near_more + x_far + x_far_more, bits[-1:])

    gate_grad, up_grad, down_grad, mlp_gain_sum = mlp_grad(
        after(places, first_part), chunk, x_pieces, cot_all, hidden_back_all,
        gate_weight, up_weight, out_cols, 0, gate_weight.shape[1], (),
    )
    mlp_gain_sum = mlp_gain_sum[:, 0]
    theirs = after(theirs, gate_grad)
    both = scatter_tensor(jnp.concatenate([first_part, mlp_part], axis=1), gate_grad)
    first_back, mlp_out = both[:, :width], both[:, width:]
    scaled_chunk, root_chunk = scaled_first[:chunk], root_first[:chunk]
    input_grad = (
        middle_back + norm_back(first_back, scaled_chunk, root_chunk, gain_first)
    ).astype(BF)
    layer_out = (middle + mlp_out).astype(BF)
    results = gather_tensor(jnp.concatenate([layer_out, input_grad], axis=1))
    results = from_slots(results, slots, place)
    layer_out, input_grad = results[:, :width], results[:, width:]
    attn_grads = mine_grads + sum(part.astype(F32) for part in theirs)
    query_grad, key_grad, value_grad = attn_grads[0], attn_grads[1], attn_grads[2]
    out_grad = attn_grads[3].T

    def rows_of(weight):
        return lax.dynamic_slice_in_dim(weight, owner * out_cols, out_cols, 0).astype(F32)

    attn_gain_sum = jnp.sum(
        rows_of(query_weight) * query_grad + rows_of(key_weight) * key_grad
        + rows_of(value_weight) * value_grad, axis=1,
    )
    gains = jnp.stack([attn_gain_sum, mlp_gain_sum])
    for bit in bits_of(n_t):
        gains = gains + swap(gains, "tensor", bit)
    gain_grads = gains / lax.dynamic_slice_in_dim(
        jnp.stack([gain_first, gain_second]), owner * out_cols, out_cols, 1
    )

    return (
        layer_out[None], input_grad[None], gain_grads[0], query_grad, key_grad, value_grad,
        out_grad, gain_grads[1], gate_grad, up_grad, down_grad, attn_mass[None],
    )


def solution(mesh):
    return jax.shard_map(
        per_device,
        mesh=mesh,
        in_specs=(
            P("dp", "ctx", None),
            P("dp", "ctx", None),
            P("dp", None),
            P(),
            P(None, "tensor"),
            P(None, "tensor"),
            P(None, "tensor"),
            P("tensor", None),
            P(),
            P(None, "tensor"),
            P(None, "tensor"),
            P("tensor", None),
        ),
        out_specs=(
            P("dp", "ctx", None),
            P("dp", "ctx", None),
            P(("dp", "ctx")),
            P(("dp", "ctx"), "tensor"),
            P(("dp", "ctx"), "tensor"),
            P(("dp", "ctx"), "tensor"),
            P("tensor", ("dp", "ctx")),
            P(("dp", "ctx")),
            P(("dp", "ctx"), "tensor"),
            P(("dp", "ctx"), "tensor"),
            P("tensor", ("dp", "ctx")),
            P("dp", "ctx", "tensor"),
        ),
        check_vma=False,
    )
```

```python
import functools
import math

import jax
import jax.numpy as jnp
import numpy as np
from jax import lax
from jax.experimental import pallas as pl
from jax.experimental.pallas import tpu as pltpu
from jax.sharding import PartitionSpec as P

HD = 128
EPS = 1e-05
BF = jnp.bfloat16
F32 = jnp.float32
MIB = 1024 * 1024


def swap(values, axis, distance):
    count = lax.axis_size(axis)
    return lax.ppermute(values, axis, [(i, i ^ distance) for i in range(count)])


def turn(values, axis, shift):
    count = lax.axis_size(axis)
    return lax.ppermute(values, axis, [(i, (i + shift) % count) for i in range(count)])


def after(value, *others):
    return lax.optimization_barrier((value, others))[0]


def in_hbm(values):
    return pltpu.with_memory_space_constraint(values, pltpu.HBM)


def in_vmem(values):
    return pltpu.with_memory_space_constraint(values, pltpu.VMEM)


def bits_of(count):
    return [1 << i for i in range(count.bit_length() - 1)]


def slot_order(count):
    order = [0]
    for bit in reversed(bits_of(count)):
        order = order + [slot ^ bit for slot in order]
    return order


def gather_tensor(rows, beside=()):
    for bit in reversed(bits_of(lax.axis_size("tensor"))):
        got = after(swap(rows, "tensor", bit), beside)
        rows, beside = jnp.concatenate([rows, got], axis=0), ()
    return rows


def scatter_tensor(rows, beside=()):
    bits = bits_of(lax.axis_size("tensor"))
    for bit in bits:
        if not isinstance(rows, tuple):
            half = rows.shape[0] // 2
            rows = rows[:half], rows[half:]
        got = swap(rows[1].astype(BF), "tensor", bit)
        if bit == bits[-1]:
            got = after(got, beside)
        rows = rows[0].astype(F32) + got.astype(F32)
    return rows


def ring_of(rows):
    return [rows] + [turn(rows, "ctx", k) for k in range(1, lax.axis_size("ctx"))]


def from_slots(blocks, slots, place):
    size = blocks.shape[0] // len(slots)
    out = jnp.zeros_like(blocks)
    for index, slot in enumerate(slots):
        out = lax.dynamic_update_slice_in_dim(
            out, blocks[index * size : (index + 1) * size], (place ^ slot) * size, 0
        )
    return out


def rope_rows(u, cos, sin):
    return u * cos + pltpu.roll(u, HD // 2, 1) * sin


def rope_back_rows(u, cos, sin):
    return u * cos - pltpu.roll(u, HD // 2, 1) * sin


def dot(a, b):
    return lax.dot_general(a, b, (((1,), (0,)), ((), ())), preferred_element_type=F32)


def dot_nt(a, b):
    return lax.dot_general(a, b, (((1,), (1,)), ((), ())), preferred_element_type=F32)


def dot_tn(a, b):
    return lax.dot_general(a, b, (((0,), (0,)), ((), ())), preferred_element_type=F32)


def place_rows(step, pieces, places, rows, sem, start=True, wait=True):
    @pl.when(step == 0)
    def _():
        copies = []
        for i, (piece, place) in enumerate(zip(pieces, places, strict=True)):
            copies.append(pltpu.make_async_copy(piece, rows.at[place], sem.at[i]))
        if start:
            for copy in copies:
                copy.start()
        if wait:
            for copy in copies:
                copy.wait()


def chunk_places(at_ref, first, count, chunk):
    return [
        pl.ds(pl.multiple_of(at_ref[first + i] * chunk, chunk), chunk) for i in range(count)
    ]


NEVER = -1e30
VMEM_WHOLE = pl.BlockSpec(memory_space=pltpu.VMEM)
HBM_WHOLE = pl.BlockSpec(memory_space=pl.ANY)


def fetch_kernel(count, *refs):
    sources, targets, sem = refs[:count], refs[count : 2 * count], refs[-1]
    copies = [
        pltpu.make_async_copy(source, target, sem.at[i])
        for i, (source, target) in enumerate(zip(sources, targets, strict=True))
    ]
    for copy in copies:
        copy.start()
    for copy in copies:
        copy.wait()


def fetch(*weights):
    return pl.pallas_call(
        functools.partial(fetch_kernel, len(weights)),
        in_specs=[HBM_WHOLE] * len(weights),
        out_specs=[VMEM_WHOLE] * len(weights),
        out_shape=[pltpu.VMEM(weight.shape, weight.dtype) for weight in weights],
        scratch_shapes=[pltpu.SemaphoreType.DMA((len(weights),))],
        compiler_params=pltpu.CompilerParams(vmem_limit_bytes=2 * MIB),
        cost_estimate=pl.CostEstimate(
            flops=0, bytes_accessed=0, transcendentals=0
        ),
    )(*[in_hbm(weight) for weight in weights])


def arrange_kernel(
    at_ref, rows_hbm, cot_hbm, gain_ref, normed_ref, mine_ref, cots_ref, cot_mine_ref,
    inputs_ref, scaled_ref, root_ref, rows_in, rows_sem, cot_sem,
):
    chunk = mine_ref.shape[0]
    spots = chunk_places(at_ref, 0, normed_ref.shape[0] // chunk, chunk)
    parts = [slice(i * chunk, (i + 1) * chunk) for i in range(len(spots))]
    copies = []
    for i, (spot, part) in enumerate(zip(spots, parts, strict=True)):
        copies.append((
            pltpu.make_async_copy(rows_hbm.at[spot], rows_in.at[part], rows_sem.at[i]),
            pltpu.make_async_copy(cot_hbm.at[spot], cots_ref.at[part], cot_sem.at[i]),
        ))
    for pair in copies:
        for copy in pair:
            copy.start()
    gain = gain_ref[...].astype(F32)
    for i, (part, pair) in enumerate(zip(parts, copies, strict=True)):
        pair[0].wait()
        rows = rows_in[part, :].astype(F32)
        root = lax.rsqrt(jnp.mean(rows * rows, axis=-1, keepdims=True) + EPS)
        normed = (rows * root * gain).astype(BF)
        normed_ref[part, :] = normed
        pair[1].wait()
        if i == 0:
            mine_ref[...] = normed
            cot_mine_ref[...] = cots_ref[part, :]
            inputs_ref[...] = rows
            scaled_ref[...] = rows * root
            root_ref[...] = jnp.broadcast_to(root, root_ref.shape)


def arrange(places, rows, cot, gain):
    count, width = rows.shape
    slots = places.shape[0]
    chunk = count // slots
    shapes = [(count, width), (chunk, width)] * 2
    more = [(chunk, width)] * 3
    return pl.pallas_call(
        arrange_kernel,
        in_specs=[pl.BlockSpec(memory_space=pltpu.SMEM), HBM_WHOLE, HBM_WHOLE, VMEM_WHOLE],
        out_specs=[VMEM_WHOLE] * 7,
        out_shape=[jax.ShapeDtypeStruct(shape, BF) for shape in shapes]
        + [jax.ShapeDtypeStruct(shape, F32) for shape in more],
        scratch_shapes=[pltpu.VMEM((count, width), BF),
                        pltpu.SemaphoreType.DMA((slots,)), pltpu.SemaphoreType.DMA((slots,))],
        compiler_params=pltpu.CompilerParams(vmem_limit_bytes=16 * MIB),
        cost_estimate=pl.CostEstimate(
            flops=8 * count * width, bytes_accessed=8 * count * width, transcendentals=0
        ),
    )(places, in_hbm(rows), in_hbm(cot), gain)


def column_of(row):
    return jnp.broadcast_to(row, (HD, row.shape[1])).T[:, :1]


def attend_kernel(chunk, slots, scale, shift, at_ref, *refs):
    count = len(refs) - 16
    pieces = refs[:count]
    (doc_ref, cos_ref, sin_ref, wq_ref, wk_ref, wv_ref, q_ref, k_ref, v_ref, att_ref, mass_ref,
     seq_hbm, x, doc_column, sem, out_sem) = refs[count:]
    step, last = pl.program_id(0), pl.num_programs(0) - 1
    place_rows(step, pieces, chunk_places(at_ref, 0, count, chunk), x, sem)
    keep = pltpu.make_async_copy(x, seq_hbm, out_sem)

    @pl.when(step == 0)
    def _():
        keep.start()

    cos, sin = cos_ref[...], sin_ref[...]
    own = chunk_places(at_ref, 0, slots, chunk)
    doc_column[...] = column_of(doc_ref[...])
    shape = (chunk, doc_ref.shape[1])
    bias = []
    for i, spot in enumerate(own):
        own_spots = lax.broadcasted_iota(jnp.int32, shape, 0) + at_ref[i] * chunk
        allowed = (lax.broadcasted_iota(jnp.int32, shape, 1) <= own_spots) & (
            doc_column[spot, :] == doc_ref[...]
        )
        bias.append(jnp.where(allowed, shift, NEVER))
    bias = jnp.concatenate(bias, axis=0)
    rows = x[...]
    q_all = dot(rows, wq_ref[...])
    k_all = dot(rows, wk_ref[...])
    v_all = dot(rows, wv_ref[...]).astype(BF)
    v_ref[...] = v_all
    for j in range(q_all.shape[1] // HD):
        cols = slice(j * HD, (j + 1) * HD)
        q_ref[:, cols] = rope_rows(q_all[:, cols], cos, sin).astype(BF)
        k = rope_rows(k_all[:, cols], cos, sin).astype(BF)
        k_ref[:, cols] = k
        q = jnp.concatenate([q_ref[spot, cols] for spot in own], axis=0)
        weights = jax.nn.sigmoid(dot_nt(q, k) * scale + bias)
        mass_ref[j] = jnp.sum(weights, axis=-1, keepdims=True)
        att_ref[:, cols] = dot(weights.astype(BF), v_all[:, cols]).astype(BF)

    @pl.when(step == last)
    def _():
        keep.wait()


def attend(places, pieces, docs, cos, sin, wq, wk, wv, slots, scale, shift):
    chunk, width = pieces[0].shape
    seq, rows = chunk * len(pieces), chunk * slots
    cols = wq.shape[1]
    heads = cols // HD
    step = min(2, heads)
    whole = lambda *shape: pl.BlockSpec(
        shape, lambda i: (0,) * len(shape), pipeline_mode=pl.Buffered(1)
    )
    hbm = pl.BlockSpec(memory_space=pl.ANY)
    wspec = pl.BlockSpec((width, step * HD), lambda i: (0, i))
    sspec = pl.BlockSpec((seq, step * HD), lambda i: (0, i))
    return pl.pallas_call(
        functools.partial(attend_kernel, chunk, slots, scale, shift),
        grid=(heads // step,),
        in_specs=[pl.BlockSpec(memory_space=pltpu.SMEM)] + [hbm] * len(pieces)
        + [whole(1, seq), whole(seq, HD), whole(seq, HD)]
        + [wspec] * 3,
        out_specs=[sspec, sspec, sspec,
                   pl.BlockSpec((rows, step * HD), lambda i: (0, i)),
                   pl.BlockSpec((step, rows, 1), lambda i: (i, 0, 0)),
                   pl.BlockSpec(memory_space=pltpu.HBM)],
        out_shape=[jax.ShapeDtypeStruct((seq, cols), BF)] * 3
        + [jax.ShapeDtypeStruct((rows, cols), BF), jax.ShapeDtypeStruct((heads, rows, 1), F32),
           jax.ShapeDtypeStruct((seq, width), BF)],
        scratch_shapes=[pltpu.VMEM((seq, width), BF), pltpu.VMEM((seq, 1), jnp.int32),
                        pltpu.SemaphoreType.DMA((len(pieces),)), pltpu.SemaphoreType.DMA],
        compiler_params=pltpu.CompilerParams(vmem_limit_bytes=56 * MIB),
        cost_estimate=pl.CostEstimate(
            flops=2 * seq * width * cols * 3, bytes_accessed=6 * width * cols, transcendentals=0
        ),
    )(places, *pieces, docs, cos, sin, wq, wk, wv)


def attend_back_kernel(chunk, slots, scale, shift, at_ref, starts_ref, *refs):
    count = len(refs) - 24
    pieces = refs[:count]
    (wo_ref, q_ref, k_ref, v_ref, cos_ref, sin_ref, doc_row_ref, more_ref,
     x_hbm, wq_hbm, wk_hbm, wv_hbm, mine_ref, theirs_ref, first_ref, give_ref,
     bb, x_cols, w_cols, acc, every, bb_sem, x_sem, w_sem) = refs[count:]
    step = pl.program_id(0)
    owners = x_cols.shape[0]
    spots = chunk_places(at_ref, 0, count, chunk)
    place_rows(step, pieces, spots, bb, bb_sem, wait=False)
    seq, size, width = bb.shape[0], x_cols.shape[2], w_cols.shape[2]
    starts = [pl.multiple_of(starts_ref[i], HD) for i in range(owners)]
    at = pl.ds(pl.multiple_of(step * width, HD), width)
    copies = [
        pltpu.make_async_copy(x_hbm.at[:, pl.ds(starts[i], size)], x_cols.at[i], x_sem.at[i])
        for i in range(owners)
    ] + [
        pltpu.make_async_copy(w_hbm.at[:, at], w_cols.at[i], w_sem.at[i])
        for i, w_hbm in enumerate((wq_hbm, wk_hbm, wv_hbm))
    ]
    for copy in copies:
        copy.start()

    block = min(256, seq)
    parts = [slice(i * block, (i + 1) * block) for i in range(seq // block)]
    heads = [slice(j * HD, (j + 1) * HD) for j in range(width // HD)]
    weights, attended = {}, []
    doc_column = column_of(doc_row_ref[...])
    for i, part in enumerate(parts):
        shape = (block, part.stop)
        allowed = (
            lax.broadcasted_iota(jnp.int32, shape, 1)
            <= lax.broadcasted_iota(jnp.int32, shape, 0) + part.start
        ) & (doc_column[part, :] == doc_row_ref[:, : part.stop])
        bias = jnp.where(allowed, shift, NEVER)
        row = []
        for j, cols in enumerate(heads):
            scores = dot_nt(q_ref[part, cols], k_ref[: part.stop, cols]) * scale + bias
            weights[i, j] = jax.nn.sigmoid(scores)
            row.append(dot(weights[i, j].astype(BF), v_ref[: part.stop, cols]).astype(BF))
        attended.append(jnp.concatenate(row, axis=1))
    attended = jnp.concatenate(attended, axis=0)

    place_rows(step, pieces, spots, bb, bb_sem, start=False)
    ab_all = dot_nt(bb[...], wo_ref[...]).astype(BF)
    for j, cols in enumerate(heads):
        key_sums, value_sums = [None] * len(parts), [None] * len(parts)
        for i, part in enumerate(parts):
            ab, weight = ab_all[part, cols], weights[i, j]
            slope = weight - weight * weight
            back = (dot_nt(ab, v_ref[: part.stop, cols]) * slope).astype(BF)
            weight = weight.astype(BF)
            query_back = dot(back, k_ref[: part.stop, cols]) * scale
            every[part, cols] = rope_back_rows(
                query_back, cos_ref[part, :], sin_ref[part, :]
            ).astype(BF)
            for n in range(i + 1):
                key_part = dot_tn(back[:, parts[n]], q_ref[part, cols])
                value_part = dot_tn(weight[:, parts[n]], ab)
                key_sums[n] = key_part if i == n else key_sums[n] + key_part
                value_sums[n] = value_part if i == n else value_sums[n] + value_part
        for n, part in enumerate(parts):
            at_key = slice(width + cols.start, width + cols.stop)
            at_value = slice(2 * width + cols.start, 2 * width + cols.stop)
            every[part, at_key] = rope_back_rows(
                key_sums[n] * scale, cos_ref[part, :], sin_ref[part, :]
            ).astype(BF)
            every[part, at_value] = value_sums[n].astype(BF)

    def give(i, n, part):
        if i == 0:
            mine_ref[n] = part
        else:
            theirs_ref[i - 1, n] = part.astype(BF)

    for i in range(owners):
        give(i, 3, dot_tn(bb[:, pl.ds(starts[i], size)], attended))

    for copy in copies:
        copy.wait()
    for i in range(owners):
        total = dot_tn(x_cols[i], every[...])
        for n in range(3):
            give(i, n, total[:, n * width : (n + 1) * width])
    own = jnp.concatenate([every[spot, :] for spot in spots[:slots]], axis=0)
    first = sum(dot_nt(own[:, n * width : (n + 1) * width], w_cols[n]) for n in range(3))

    @pl.when(step == 0)
    def _():
        acc[...] = first

    @pl.when(step > 0)
    def _():
        acc[...] += first

    @pl.when(step == pl.num_programs(0) - 1)
    def _():
        total, half = acc[...].astype(BF), acc.shape[0] // 2
        for n, at in enumerate((slice(0, half), slice(half, 2 * half))):
            keep_ref = first_ref if n == 0 else give_ref
            keep_ref[:, : acc.shape[1]] = total[at]
            keep_ref[:, acc.shape[1] :] = more_ref[at, :]


def attend_back(
    places, starts, pieces, wo, q, k, v, cos, sin, docs, more, x_seq, wq, wk, wv,
    size, slots, scale, shift,
):
    seq, width = x_seq.shape
    chunk = pieces[0].shape[0]
    cols = wo.shape[0]
    heads = cols // HD
    step = min(2, heads)
    own = slots * chunk
    owners = starts.shape[0]
    whole = lambda *shape: pl.BlockSpec(
        shape, lambda i: (0,) * len(shape), pipeline_mode=pl.Buffered(1)
    )
    sspec = pl.BlockSpec((seq, step * HD), lambda i: (0, i))
    hbm = pl.BlockSpec(memory_space=pl.ANY)
    return pl.pallas_call(
        functools.partial(attend_back_kernel, chunk, slots, scale, shift),
        grid=(heads // step,),
        in_specs=[pl.BlockSpec(memory_space=pltpu.SMEM)] * 2 + [hbm] * len(pieces)
        + [pl.BlockSpec((step * HD, width), lambda i: (i, 0)),
           sspec, sspec, sspec, whole(seq, HD), whole(seq, HD), whole(1, seq), whole(*more.shape)]
        + [hbm] * 4,
        out_specs=[pl.BlockSpec((4, size, step * HD), lambda i: (0, 0, i)),
                   pl.BlockSpec((owners - 1, 4, size, step * HD), lambda i: (0, 0, 0, i)),
                   whole(own // 2, 2 * width), whole(own // 2, 2 * width)],
        out_shape=[jax.ShapeDtypeStruct((4, size, cols), F32),
                   jax.ShapeDtypeStruct((owners - 1, 4, size, cols), BF),
                   jax.ShapeDtypeStruct((own // 2, 2 * width), BF),
                   jax.ShapeDtypeStruct((own // 2, 2 * width), BF)],
        scratch_shapes=[pltpu.VMEM((seq, width), BF), pltpu.VMEM((owners, seq, size), BF),
                        pltpu.VMEM((3, width, step * HD), BF),
                        pltpu.VMEM((own, width), F32),
                        pltpu.VMEM((seq, 3 * step * HD), BF),
                        pltpu.SemaphoreType.DMA((len(pieces),)),
                        pltpu.SemaphoreType.DMA((owners,)), pltpu.SemaphoreType.DMA((3,))],
        compiler_params=pltpu.CompilerParams(vmem_limit_bytes=56 * MIB),
        cost_estimate=pl.CostEstimate(
            flops=2 * seq * width * cols + 14 * seq * seq * cols,
            bytes_accessed=2 * (seq + cols) * width + 20 * seq * cols,
            transcendentals=seq * seq * heads,
        ),
    )(
        places, starts, *pieces, in_hbm(wo), q, k, v, cos, sin,
        docs, more, in_hbm(x_seq), in_hbm(wq), in_hbm(wk), in_hbm(wv),
    )


def gate_math(gate, up, hidden_back):
    sig = jax.nn.sigmoid(gate)
    act = gate * sig
    hidden = (act * up).astype(BF)
    gate_back = (hidden_back * up * sig * (1.0 + gate * (1.0 - sig))).astype(BF)
    up_back = (hidden_back * act).astype(BF)
    return hidden, gate_back, up_back


def mlp_kernel(
    block, x_ref, hb_ref, wg_ref, wu_ref, hidden_ref, gate_ref, up_ref, back_ref
):
    x, total = x_ref[...], None
    for i in range(wg_ref.shape[1] // block):
        at = slice(i * block, (i + 1) * block)
        wg, wu = wg_ref[:, at], wu_ref[:, at]
        hidden_ref[:, at], gate_back, up_back = gate_math(
            dot(x, wg), dot(x, wu), hb_ref[:, at].astype(F32)
        )
        gate_ref[:, at] = gate_back
        up_ref[:, at] = up_back
        back = dot_nt(gate_back, wg) + dot_nt(up_back, wu)
        total = back if total is None else total + back
    back_ref[...] = total.astype(BF)


def mlp(x, hidden_back, wg, wu):
    rows, width = x.shape
    units = wg.shape[1]
    return pl.pallas_call(
        functools.partial(mlp_kernel, min(512, units)),
        in_specs=[VMEM_WHOLE] * 4,
        out_specs=[VMEM_WHOLE] * 4,
        out_shape=[
            *[jax.ShapeDtypeStruct((rows, units), BF)] * 3, jax.ShapeDtypeStruct((rows, width), BF)
        ],
        compiler_params=pltpu.CompilerParams(vmem_limit_bytes=20 * MIB),
        cost_estimate=pl.CostEstimate(
            flops=0, bytes_accessed=0, transcendentals=0
        ),
    )(x, hidden_back, in_vmem(wg), in_vmem(wu))


def hidden_back_kernel(tile, at_ref, cot_hbm, wd_ref, out_ref, cot, sem):
    copies = []
    for i in range(cot.shape[0] // tile):
        source = pl.ds(pl.multiple_of(at_ref[i] * tile, tile), tile)
        target = cot.at[pl.ds(i * tile, tile)]
        copies.append(pltpu.make_async_copy(cot_hbm.at[source], target, sem.at[i]))

    def every_tile(waits):
        wd = wd_ref[...]
        for i in range(0, len(copies), 2):
            if waits:
                copies[i].wait()
                copies[i + 1].wait()
            at = pl.ds(i * tile, 2 * tile)
            out_ref[at, :] = dot_nt(cot[at, :], wd).astype(BF)

    @pl.when(pl.program_id(0) == 0)
    def _():
        for copy in copies:
            copy.start()
        every_tile(True)

    @pl.when(pl.program_id(0) > 0)
    def _():
        every_tile(False)


def hidden_back_of(turns, cot, wd):
    rows, width = cot.shape
    units, tiles = wd.shape[0], turns.shape[0]
    block = min(512, units)
    return pl.pallas_call(
        functools.partial(hidden_back_kernel, rows // tiles),
        grid=(units // block,),
        in_specs=[pl.BlockSpec(memory_space=pltpu.SMEM), HBM_WHOLE,
                  pl.BlockSpec((block, width), lambda i: (i, 0))],
        out_specs=pl.BlockSpec((rows, block), lambda i: (0, i)),
        out_shape=jax.ShapeDtypeStruct((rows, units), BF),
        scratch_shapes=[pltpu.VMEM((rows, width), BF), pltpu.SemaphoreType.DMA((tiles,))],
        compiler_params=pltpu.CompilerParams(vmem_limit_bytes=56 * MIB),
        cost_estimate=pl.CostEstimate(
            flops=2 * rows * width * units, bytes_accessed=2 * width * (rows + units),
            transcendentals=0,
        ),
    )(turns, in_hbm(cot), in_hbm(wd))


def mlp_grad_kernel(count, chunk, at_ref, *refs):
    pieces = refs[:count]
    (own_hid, own_gate, own_up, hb_ref, cot_hbm, wg_ref, wu_ref, gg_ref, ug_ref, dg_ref, gain_ref,
     x_all, cb, hid, gbk, ubk, gain_sum, sem, cot_sem) = refs[count:]
    size = cb.shape[1]
    tile = pieces[0].shape[0]
    per = tile // chunk
    tiles = x_all.shape[0] // tile
    own = pl.ds(pl.multiple_of(at_ref[0] * size, size), size)

    @pl.when(pl.program_id(0) == 0)
    def _():
        copies = []
        for i in range(count * per):
            spot = pl.ds(pl.multiple_of(at_ref[1 + i] * chunk, chunk), chunk)
            part = pieces[i // per].at[pl.ds(i % per * chunk, chunk)]
            copies.append(pltpu.make_async_copy(part, x_all.at[spot], sem.at[i]))
        base = 1 + count * per
        for i in range(per):
            spot = pl.ds(pl.multiple_of(at_ref[base + tiles + i] * chunk, chunk), chunk)
            target = cb.at[pl.ds(i * chunk, chunk)]
            copies.append(pltpu.make_async_copy(cot_hbm.at[spot, own], target, cot_sem.at[i]))
        for i in range(1, tiles):
            spot = pl.ds(pl.multiple_of(at_ref[base + i] * tile, tile), tile)
            target = cb.at[pl.ds(i * tile, tile)]
            copies.append(
                pltpu.make_async_copy(cot_hbm.at[spot, own], target, cot_sem.at[per + i])
            )
        for copy in copies:
            copy.start()
        for copy in copies:
            copy.wait()

    hid[:tile, :], gbk[:tile, :], ubk[:tile, :] = own_hid[...], own_gate[...], own_up[...]
    wg, wu = wg_ref[...], wu_ref[...]
    for i in range(1, tiles):
        at = pl.ds(i * tile, tile)
        x = x_all[at, :]
        hid[at, :], gbk[at, :], ubk[at, :] = gate_math(
            dot(x, wg), dot(x, wu), hb_ref[at, :].astype(F32)
        )
    xb = x_all[:, own]
    gate_grad = dot_tn(xb, gbk[...])
    up_grad = dot_tn(xb, ubk[...])
    gg_ref[...] = gate_grad
    ug_ref[...] = up_grad
    dg_ref[...] = dot_tn(hid[...], cb[...])
    gain = jnp.sum(
        wg_ref[own, :].astype(F32) * gate_grad + wu_ref[own, :].astype(F32) * up_grad,
        axis=1, keepdims=True,
    )

    @pl.when(pl.program_id(0) == 0)
    def _():
        gain_sum[...] = gain

    @pl.when(pl.program_id(0) > 0)
    def _():
        gain_sum[...] += gain

    @pl.when(pl.program_id(0) == pl.num_programs(0) - 1)
    def _():
        gain_ref[...] = jnp.broadcast_to(gain_sum[...], (size, HD)).T[:1, :]


def mlp_grad(places, chunk, pieces, own, cot, hb, wg, wu, size):
    tile, width = pieces[0].shape
    rows, units = hb.shape
    block = min(256, units)
    wspec = pl.BlockSpec((width, block), lambda i, at: (0, i))
    ospec = pl.BlockSpec((tile, block), lambda i, at: (0, i))
    grid_spec = pltpu.PrefetchScalarGridSpec(
        num_scalar_prefetch=1,
        grid=(units // block,),
        in_specs=[HBM_WHOLE] * len(pieces) + [ospec] * 3
        + [pl.BlockSpec((rows, block), lambda i, at: (0, i)), HBM_WHOLE, wspec, wspec],
        out_specs=[pl.BlockSpec((size, block), lambda i, at: (0, i))] * 2
        + [pl.BlockSpec((block, size), lambda i, at: (i, 0)),
           pl.BlockSpec((1, size), lambda i, at: (0, 0))],
        scratch_shapes=[pltpu.VMEM((rows, width), BF), pltpu.VMEM((rows, size), BF)]
        + [pltpu.VMEM((rows, block), BF)] * 3
        + [pltpu.VMEM((size, 1), F32), pltpu.SemaphoreType.DMA((rows // chunk,)),
           pltpu.SemaphoreType.DMA((tile // chunk + rows // tile,))],
    )
    return pl.pallas_call(
        functools.partial(mlp_grad_kernel, len(pieces), chunk),
        grid_spec=grid_spec,
        out_shape=[jax.ShapeDtypeStruct((size, units), F32)] * 2
        + [jax.ShapeDtypeStruct((units, size), F32), jax.ShapeDtypeStruct((1, size), F32)],
        compiler_params=pltpu.CompilerParams(vmem_limit_bytes=56 * MIB),
        cost_estimate=pl.CostEstimate(
            flops=2 * rows * units * (2 * width + 3 * size),
            bytes_accessed=4 * width * units + 4 * rows * width,
            transcendentals=0,
        ),
    )(
        places, *pieces, *[in_hbm(rows) for rows in own], in_hbm(hb), in_hbm(cot),
        in_hbm(wg), in_hbm(wu),
    )


def row_mean(values):
    return jnp.mean(values, axis=-1, keepdims=True)


def norm_parts(values):
    root = lax.rsqrt(row_mean(values * values) + EPS)
    return values * root, root


def norm_back(upstream, scaled, root, gain):
    inner = upstream * gain
    return root * (inner - scaled * row_mean(inner * scaled))


def per_device(
    activations, cotangent, doc_ids, attn_gain, query_weight, key_weight, value_weight,
    out_weight, mlp_gain, gate_weight, up_weight, down_weight,
):
    rows, width = activations.shape[1:]
    n_dp, n_ctx, n_t = lax.axis_size("dp"), lax.axis_size("ctx"), lax.axis_size("tensor")
    dp, ctx, place = lax.axis_index("dp"), lax.axis_index("ctx"), lax.axis_index("tensor")
    chunk = rows // n_t
    length = rows * n_ctx
    slots = slot_order(n_t)
    scale, shift = HD ** (-0.5), -math.log(length)
    gain_first, gain_second = attn_gain.astype(F32), mlp_gain.astype(F32)

    slot_places = jnp.stack([place ^ slot for slot in slots])
    normed_first, mine, cot, cot_mine, inputs_mine, scaled_mine, root_mine = arrange(
        slot_places, activations[0], cotangent[0], attn_gain[None]
    )

    bits = list(reversed(bits_of(n_t)))

    def spread(rings, beside=()):
        lists = [[ring] for ring in rings]
        for bit in bits:
            lists = [items + [swap(item, "tensor", bit) for item in items] for items in lists]
            if bit == bits[0]:
                lists = after(lists, beside)
        return lists

    rings = ring_of(mine)[1:]
    cot_all = lax.all_gather(
        cot_mine, ("dp", "ctx", "tensor"), axis=0, tiled=True
    )

    ring_at = (ctx - jnp.arange(n_ctx, dtype=jnp.int32) + n_ctx) % n_ctx
    seq_places = jnp.concatenate([
        ring_at[k : k + 1] * n_t + (place ^ slot) for k in range(n_ctx) for slot in slots
    ])
    docs = doc_ids
    out_cols = width // (n_dp * n_ctx)
    owners = jnp.stack([((dp + step) % n_dp) * n_ctx + ctx for step in range(n_dp)])
    starts = owners * out_cols
    owner = owners[0]
    tiles = n_dp * n_ctx
    turns = (owner + jnp.arange(tiles, dtype=jnp.int32)) % tiles
    places = [owner[None]]
    for flip in (0, 1):
        for step in range(n_dp):
            for index in range(n_t // 2):
                group = ((dp - step + n_dp) % n_dp) * n_ctx + ring_at
                group = (group - owner + tiles) % tiles
                inside = jnp.where(
                    group == 0, index + flip * (n_t // 2), place ^ slots[index] ^ flip
                )
                places.append(group * n_t + inside)
    places = jnp.concatenate(places + [turns, owner * n_t + slot_places])
    frequency = np.float32(10000.0) ** (
        -np.arange(HD // 2, dtype=np.float32) * np.float32(2.0) / np.float32(HD)
    )
    angles = np.arange(length, dtype=np.float32)[:, None] * frequency[None, :]
    cos = jnp.asarray(np.concatenate([np.cos(angles), np.cos(angles)], axis=1))
    sin = jnp.asarray(np.concatenate([-np.sin(angles), np.sin(angles)], axis=1))
    rings = after(rings, seq_places, starts, places, turns)
    hidden_back = lax.dot_general(
        after(cot, rings), down_weight, (((1,), (1,)), ((), ())), preferred_element_type=F32
    ).astype(BF)
    seq_pieces = spread(rings, hidden_back)
    own_pieces = [normed_first[i * chunk : (i + 1) * chunk] for i in range(n_t)]
    q, k, v, attended, mass, x_seq = attend(
        seq_places, own_pieces + sum(seq_pieces, []), docs, cos, sin,
        query_weight, key_weight, value_weight, n_t, scale, shift,
    )
    attn_mass = from_slots(mass[:, :, 0].T, slots, place)

    def over_dp(items):
        return [turn(item, "dp", step) for step in range(1, n_dp) for item in items]

    def over_tensor(items, bits):
        for bit in bits:
            items = items + [swap(item, "tensor", bit) for item in items]
        return items

    branch = scatter_tensor(
        jnp.dot(attended, out_weight, preferred_element_type=F32).astype(BF), attn_mass
    )
    middle = inputs_mine + branch
    scaled_second, root_second = norm_parts(middle)
    normed_chunk = (scaled_second * gain_second).astype(BF)
    gate, up = fetch(after(gate_weight, normed_chunk), up_weight)
    normed_second = gather_tensor(normed_chunk, (gate, up))
    chunk_rings = ring_of(normed_chunk)
    hidden, gate_back, up_back, second_part = mlp(normed_second, hidden_back, gate, up)
    second_part, chunk_rings = lax.optimization_barrier((second_part, chunk_rings))
    x_near = [jnp.concatenate(chunk_rings, axis=0)]
    x_far = over_dp(x_near)
    x_near_more = over_tensor(x_near, bits[:-1])[1:]
    second_back = scatter_tensor(second_part)
    middle_back = cot_mine.astype(F32) + norm_back(
        second_back, scaled_second, root_second, gain_second
    )
    branch_back = middle_back.astype(BF)
    bb_rings = ring_of(branch_back)[1:]
    bb_own = over_tensor([branch_back], bits[:-1])
    hidden_back_all = hidden_back_of(turns, after(cot_all, branch_back), down_weight)
    bb_rings, bb_own, x_far, x_near_more = after(
        (bb_rings, bb_own, x_far, x_near_more), hidden_back_all
    )
    mlp_part = jnp.dot(
        after(hidden, bb_rings), down_weight, preferred_element_type=F32
    ).astype(BF)
    bb_pieces = [over_tensor(bb_own, bits[-1:])] + spread(bb_rings, mlp_part)
    x_far_more = over_tensor(x_far, bits[:-1])[len(x_far) :]

    mine_grads, theirs_grads, kept_half, given_half = attend_back(
        seq_places, starts, sum(bb_pieces, []), out_weight, q, k, v, cos, sin, docs, mlp_part,
        x_seq, query_weight, key_weight, value_weight, out_cols, n_t, scale, shift,
    )

    theirs = [turn(theirs_grads[step - 1], "dp", step) for step in range(1, n_dp)]

    x_pieces = over_tensor(x_near + x_near_more + x_far + x_far_more, bits[-1:])

    gate_grad, up_grad, down_grad, mlp_gain_sum = mlp_grad(
        after(places, kept_half), chunk, x_pieces, (hidden, gate_back, up_back), cot_all,
        hidden_back_all, gate_weight, up_weight, out_cols,
    )
    mlp_gain_sum = mlp_gain_sum[0]
    theirs = after(theirs, gate_grad)
    both = scatter_tensor((kept_half, given_half), gate_grad)
    first_back, mlp_out = both[:, :width], both[:, width:]
    input_grad = (
        middle_back + norm_back(first_back, scaled_mine, root_mine, gain_first)
    ).astype(BF)
    layer_out = (middle + mlp_out).astype(BF)
    results = gather_tensor(jnp.concatenate([layer_out, input_grad], axis=1))
    results = from_slots(results, slots, place)
    layer_out, input_grad = results[:, :width], results[:, width:]
    attn_grads = mine_grads + sum(part.astype(F32) for part in theirs)
    query_grad, key_grad, value_grad = attn_grads[0], attn_grads[1], attn_grads[2]
    out_grad = attn_grads[3].T

    def rows_of(weight):
        return lax.dynamic_slice_in_dim(weight, owner * out_cols, out_cols, 0).astype(F32)

    attn_gain_sum = jnp.sum(
        rows_of(query_weight) * query_grad + rows_of(key_weight) * key_grad
        + rows_of(value_weight) * value_grad, axis=1,
    )
    gains = jnp.stack([attn_gain_sum, mlp_gain_sum])
    for bit in bits:
        gains = gains + swap(gains, "tensor", bit)
    gain_grads = gains / lax.dynamic_slice_in_dim(
        jnp.stack([gain_first, gain_second]), owner * out_cols, out_cols, 1
    )

    return (
        layer_out[None], input_grad[None], gain_grads[0], query_grad, key_grad, value_grad,
        out_grad, gain_grads[1], gate_grad, up_grad, down_grad, attn_mass[None],
    )


def solution(mesh):
    return jax.shard_map(
        per_device,
        mesh=mesh,
        in_specs=(
            P("dp", "ctx", None),
            P("dp", "ctx", None),
            P("dp", None),
            P(),
            P(None, "tensor"),
            P(None, "tensor"),
            P(None, "tensor"),
            P("tensor", None),
            P(),
            P(None, "tensor"),
            P(None, "tensor"),
            P("tensor", None),
        ),
        out_specs=(
            P("dp", "ctx", None),
            P("dp", "ctx", None),
            P(("dp", "ctx")),
            P(("dp", "ctx"), "tensor"),
            P(("dp", "ctx"), "tensor"),
            P(("dp", "ctx"), "tensor"),
            P("tensor", ("dp", "ctx")),
            P(("dp", "ctx")),
            P(("dp", "ctx"), "tensor"),
            P(("dp", "ctx"), "tensor"),
            P("tensor", ("dp", "ctx")),
            P("dp", "ctx", "tensor"),
        ),
        check_vma=False,
    )
```

```python
import functools
import math

import jax
import jax.numpy as jnp
import numpy as np
from jax import lax
from jax.experimental import pallas as pl
from jax.experimental.pallas import tpu as pltpu
from jax.sharding import PartitionSpec as P

HD = 128
EPS = 1e-05
BF = jnp.bfloat16
F32 = jnp.float32
MIB = 1024 * 1024


def swap(values, axis, distance):
    count = lax.axis_size(axis)
    return lax.ppermute(values, axis, [(i, i ^ distance) for i in range(count)])


def turn(values, axis, shift):
    count = lax.axis_size(axis)
    return lax.ppermute(values, axis, [(i, (i + shift) % count) for i in range(count)])


def after(value, *others):
    return lax.optimization_barrier((value, others))[0]


def in_hbm(values):
    return pltpu.with_memory_space_constraint(values, pltpu.HBM)


def in_vmem(values):
    return pltpu.with_memory_space_constraint(values, pltpu.VMEM)


def bits_of(count):
    return [1 << i for i in range(count.bit_length() - 1)]


def slot_order(count):
    order = [0]
    for bit in reversed(bits_of(count)):
        order = order + [slot ^ bit for slot in order]
    return order


def gather_tensor(rows, beside=()):
    for bit in reversed(bits_of(lax.axis_size("tensor"))):
        got = after(swap(rows, "tensor", bit), beside)
        rows, beside = jnp.concatenate([rows, got], axis=0), ()
    return rows


def scatter_tensor(rows, beside=()):
    bits = bits_of(lax.axis_size("tensor"))
    for bit in bits:
        if not isinstance(rows, tuple):
            half = rows.shape[0] // 2
            rows = rows[:half], rows[half:]
        got = swap(rows[1].astype(BF), "tensor", bit)
        if bit == bits[-1]:
            got = after(got, beside)
        rows = rows[0].astype(F32) + got.astype(F32)
    return rows


def ring_of(rows):
    return [rows] + [swap(rows, "ctx", k) for k in range(1, lax.axis_size("ctx"))]


def from_slots(blocks, slots, place):
    size = blocks.shape[0] // len(slots)
    out = jnp.zeros_like(blocks)
    for index, slot in enumerate(slots):
        out = lax.dynamic_update_slice_in_dim(
            out, blocks[index * size : (index + 1) * size], (place ^ slot) * size, 0
        )
    return out


def rope_rows(u, cos, sin):
    return u * cos + pltpu.roll(u, HD // 2, 1) * sin


def rope_back_rows(u, cos, sin):
    return u * cos - pltpu.roll(u, HD // 2, 1) * sin


def dot(a, b):
    return lax.dot_general(a, b, (((1,), (0,)), ((), ())), preferred_element_type=F32)


def dot_nt(a, b):
    return lax.dot_general(a, b, (((1,), (1,)), ((), ())), preferred_element_type=F32)


def dot_tn(a, b):
    return lax.dot_general(a, b, (((0,), (0,)), ((), ())), preferred_element_type=F32)


def place_rows(step, pieces, places, rows, sem, start=True, wait=True):
    @pl.when(step == 0)
    def _():
        copies = []
        for i, (piece, place) in enumerate(zip(pieces, places, strict=True)):
            copies.append(pltpu.make_async_copy(piece, rows.at[place], sem.at[i]))
        if start:
            for copy in copies:
                copy.start()
        if wait:
            for copy in copies:
                copy.wait()


def chunk_places(at_ref, first, count, chunk):
    return [
        pl.ds(pl.multiple_of(at_ref[first + i] * chunk, chunk), chunk) for i in range(count)
    ]


NEVER = -1e30
VMEM_WHOLE = pl.BlockSpec(memory_space=pltpu.VMEM)
HBM_WHOLE = pl.BlockSpec(memory_space=pl.ANY)


def fetch_kernel(count, *refs):
    sources, targets, sem = refs[:count], refs[count : 2 * count], refs[-1]
    copies = [
        pltpu.make_async_copy(source, target, sem.at[i])
        for i, (source, target) in enumerate(zip(sources, targets, strict=True))
    ]
    for copy in copies:
        copy.start()
    for copy in copies:
        copy.wait()


def fetch(*weights):
    return pl.pallas_call(
        functools.partial(fetch_kernel, len(weights)),
        in_specs=[HBM_WHOLE] * len(weights),
        out_specs=[VMEM_WHOLE] * len(weights),
        out_shape=[pltpu.VMEM(weight.shape, weight.dtype) for weight in weights],
        scratch_shapes=[pltpu.SemaphoreType.DMA((len(weights),))],
        compiler_params=pltpu.CompilerParams(vmem_limit_bytes=2 * MIB),
        cost_estimate=pl.CostEstimate(
            flops=0, bytes_accessed=0, transcendentals=0
        ),
    )(*[in_hbm(weight) for weight in weights])


def arrange_kernel(
    at_ref, rows_hbm, cot_hbm, gain_ref, normed_ref, mine_ref, cots_ref, cot_mine_ref,
    inputs_ref, scaled_ref, root_ref, rows_in, rows_sem, cot_sem,
):
    chunk = mine_ref.shape[0]
    spots = chunk_places(at_ref, 0, normed_ref.shape[0] // chunk, chunk)
    parts = [slice(i * chunk, (i + 1) * chunk) for i in range(len(spots))]
    copies = []
    for i, (spot, part) in enumerate(zip(spots, parts, strict=True)):
        copies.append((
            pltpu.make_async_copy(rows_hbm.at[spot], rows_in.at[part], rows_sem.at[i]),
            pltpu.make_async_copy(cot_hbm.at[spot], cots_ref.at[part], cot_sem.at[i]),
        ))
    for pair in copies:
        for copy in pair:
            copy.start()
    gain = gain_ref[...].astype(F32)
    for i, (part, pair) in enumerate(zip(parts, copies, strict=True)):
        pair[0].wait()
        rows = rows_in[part, :].astype(F32)
        root = lax.rsqrt(jnp.mean(rows * rows, axis=-1, keepdims=True) + EPS)
        normed = (rows * root * gain).astype(BF)
        normed_ref[part, :] = normed
        pair[1].wait()
        if i == 0:
            mine_ref[...] = normed
            cot_mine_ref[...] = cots_ref[part, :]
            inputs_ref[...] = rows
            scaled_ref[...] = rows * root
            root_ref[...] = jnp.broadcast_to(root, root_ref.shape)


def arrange(places, rows, cot, gain):
    count, width = rows.shape
    slots = places.shape[0]
    chunk = count // slots
    shapes = [(count, width), (chunk, width)] * 2
    more = [(chunk, width)] * 3
    return pl.pallas_call(
        arrange_kernel,
        in_specs=[pl.BlockSpec(memory_space=pltpu.SMEM), HBM_WHOLE, HBM_WHOLE, VMEM_WHOLE],
        out_specs=[VMEM_WHOLE] * 7,
        out_shape=[jax.ShapeDtypeStruct(shape, BF) for shape in shapes]
        + [jax.ShapeDtypeStruct(shape, F32) for shape in more],
        scratch_shapes=[pltpu.VMEM((count, width), BF),
                        pltpu.SemaphoreType.DMA((slots,)), pltpu.SemaphoreType.DMA((slots,))],
        compiler_params=pltpu.CompilerParams(vmem_limit_bytes=16 * MIB),
        cost_estimate=pl.CostEstimate(
            flops=8 * count * width, bytes_accessed=8 * count * width, transcendentals=0
        ),
    )(places, in_hbm(rows), in_hbm(cot), gain)


def column_of(row):
    return jnp.broadcast_to(row, (HD, row.shape[1])).T[:, :1]


def attend_kernel(chunk, slots, scale, shift, at_ref, *refs):
    count = len(refs) - 16
    pieces = refs[:count]
    (doc_ref, cos_ref, sin_ref, wq_ref, wk_ref, wv_ref, q_ref, k_ref, v_ref, att_ref, mass_ref,
     seq_hbm, x, doc_column, sem, out_sem) = refs[count:]
    step, last = pl.program_id(0), pl.num_programs(0) - 1
    place_rows(step, pieces, chunk_places(at_ref, 0, count, chunk), x, sem)
    keep = pltpu.make_async_copy(x, seq_hbm, out_sem)

    @pl.when(step == 0)
    def _():
        keep.start()

    cos, sin = cos_ref[...], sin_ref[...]
    own = chunk_places(at_ref, 0, slots, chunk)
    doc_column[...] = column_of(doc_ref[...])
    shape = (chunk, doc_ref.shape[1])
    bias = []
    for i, spot in enumerate(own):
        own_spots = lax.broadcasted_iota(jnp.int32, shape, 0) + at_ref[i] * chunk
        allowed = (lax.broadcasted_iota(jnp.int32, shape, 1) <= own_spots) & (
            doc_column[spot, :] == doc_ref[...]
        )
        bias.append(jnp.where(allowed, shift, NEVER))
    bias = jnp.concatenate(bias, axis=0)
    rows = x[...]
    q_all = dot(rows, wq_ref[...])
    k_all = dot(rows, wk_ref[...])
    v_all = dot(rows, wv_ref[...]).astype(BF)
    v_ref[...] = v_all
    for j in range(q_all.shape[1] // HD):
        cols = slice(j * HD, (j + 1) * HD)
        q_ref[:, cols] = rope_rows(q_all[:, cols], cos, sin).astype(BF)
        k = rope_rows(k_all[:, cols], cos, sin).astype(BF)
        k_ref[:, cols] = k
        q = jnp.concatenate([q_ref[spot, cols] for spot in own], axis=0)
        weights = jax.nn.sigmoid(dot_nt(q, k) * scale + bias)
        mass_ref[j] = jnp.sum(weights, axis=-1, keepdims=True)
        att_ref[:, cols] = dot(weights.astype(BF), v_all[:, cols]).astype(BF)

    @pl.when(step == last)
    def _():
        keep.wait()


def attend(places, pieces, docs, cos, sin, wq, wk, wv, slots, scale, shift):
    chunk, width = pieces[0].shape
    seq, rows = chunk * len(pieces), chunk * slots
    cols = wq.shape[1]
    heads = cols // HD
    step = min(2, heads)
    whole = lambda *shape: pl.BlockSpec(
        shape, lambda i: (0,) * len(shape), pipeline_mode=pl.Buffered(1)
    )
    hbm = pl.BlockSpec(memory_space=pl.ANY)
    wspec = pl.BlockSpec((width, step * HD), lambda i: (0, i))
    sspec = pl.BlockSpec((seq, step * HD), lambda i: (0, i))
    return pl.pallas_call(
        functools.partial(attend_kernel, chunk, slots, scale, shift),
        grid=(heads // step,),
        in_specs=[pl.BlockSpec(memory_space=pltpu.SMEM)] + [hbm] * len(pieces)
        + [whole(1, seq), whole(seq, HD), whole(seq, HD)]
        + [wspec] * 3,
        out_specs=[sspec, sspec, sspec,
                   pl.BlockSpec((rows, step * HD), lambda i: (0, i)),
                   pl.BlockSpec((step, rows, 1), lambda i: (i, 0, 0)),
                   pl.BlockSpec(memory_space=pltpu.HBM)],
        out_shape=[jax.ShapeDtypeStruct((seq, cols), BF)] * 3
        + [jax.ShapeDtypeStruct((rows, cols), BF), jax.ShapeDtypeStruct((heads, rows, 1), F32),
           jax.ShapeDtypeStruct((seq, width), BF)],
        scratch_shapes=[pltpu.VMEM((seq, width), BF), pltpu.VMEM((seq, 1), jnp.int32),
                        pltpu.SemaphoreType.DMA((len(pieces),)), pltpu.SemaphoreType.DMA],
        compiler_params=pltpu.CompilerParams(vmem_limit_bytes=56 * MIB),
        cost_estimate=pl.CostEstimate(
            flops=2 * seq * width * cols * 3, bytes_accessed=6 * width * cols, transcendentals=0
        ),
    )(places, *pieces, docs, cos, sin, wq, wk, wv)


def attend_back_kernel(chunk, slots, scale, shift, at_ref, starts_ref, *refs):
    count = len(refs) - 24
    pieces = refs[:count]
    (wo_ref, q_ref, k_ref, v_ref, cos_ref, sin_ref, doc_row_ref, more_ref,
     x_hbm, wq_hbm, wk_hbm, wv_hbm, mine_ref, theirs_ref, first_ref, give_ref,
     bb, x_cols, w_cols, acc, every, bb_sem, x_sem, w_sem) = refs[count:]
    step = pl.program_id(0)
    owners = x_cols.shape[0]
    spots = chunk_places(at_ref, 0, count, chunk)
    place_rows(step, pieces, spots, bb, bb_sem, wait=False)
    seq, size, width = bb.shape[0], x_cols.shape[2], w_cols.shape[2]
    starts = [pl.multiple_of(starts_ref[i], HD) for i in range(owners)]
    at = pl.ds(pl.multiple_of(step * width, HD), width)
    copies = [
        pltpu.make_async_copy(x_hbm.at[:, pl.ds(starts[i], size)], x_cols.at[i], x_sem.at[i])
        for i in range(owners)
    ] + [
        pltpu.make_async_copy(w_hbm.at[:, at], w_cols.at[i], w_sem.at[i])
        for i, w_hbm in enumerate((wq_hbm, wk_hbm, wv_hbm))
    ]
    for copy in copies:
        copy.start()

    block = min(256, seq)
    parts = [slice(i * block, (i + 1) * block) for i in range(seq // block)]
    heads = [slice(j * HD, (j + 1) * HD) for j in range(width // HD)]
    weights, attended = {}, []
    doc_column = column_of(doc_row_ref[...])
    for i, part in enumerate(parts):
        shape = (block, part.stop)
        allowed = (
            lax.broadcasted_iota(jnp.int32, shape, 1)
            <= lax.broadcasted_iota(jnp.int32, shape, 0) + part.start
        ) & (doc_column[part, :] == doc_row_ref[:, : part.stop])
        bias = jnp.where(allowed, shift, NEVER)
        row = []
        for j, cols in enumerate(heads):
            scores = dot_nt(q_ref[part, cols], k_ref[: part.stop, cols]) * scale + bias
            weights[i, j] = jax.nn.sigmoid(scores)
            row.append(dot(weights[i, j].astype(BF), v_ref[: part.stop, cols]).astype(BF))
        attended.append(jnp.concatenate(row, axis=1))
    attended = jnp.concatenate(attended, axis=0)

    place_rows(step, pieces, spots, bb, bb_sem, start=False)
    ab_all = dot_nt(bb[...], wo_ref[...]).astype(BF)
    for j, cols in enumerate(heads):
        key_sums, value_sums = [None] * len(parts), [None] * len(parts)
        for i, part in enumerate(parts):
            ab, weight = ab_all[part, cols], weights[i, j]
            slope = weight - weight * weight
            back = (dot_nt(ab, v_ref[: part.stop, cols]) * slope).astype(BF)
            weight = weight.astype(BF)
            query_back = dot(back, k_ref[: part.stop, cols]) * scale
            every[part, cols] = rope_back_rows(
                query_back, cos_ref[part, :], sin_ref[part, :]
            ).astype(BF)
            for n in range(i + 1):
                key_part = dot_tn(back[:, parts[n]], q_ref[part, cols])
                value_part = dot_tn(weight[:, parts[n]], ab)
                key_sums[n] = key_part if i == n else key_sums[n] + key_part
                value_sums[n] = value_part if i == n else value_sums[n] + value_part
        for n, part in enumerate(parts):
            at_key = slice(width + cols.start, width + cols.stop)
            at_value = slice(2 * width + cols.start, 2 * width + cols.stop)
            every[part, at_key] = rope_back_rows(
                key_sums[n] * scale, cos_ref[part, :], sin_ref[part, :]
            ).astype(BF)
            every[part, at_value] = value_sums[n].astype(BF)

    def give(i, n, part):
        if i == 0:
            mine_ref[n] = part
        else:
            theirs_ref[i - 1, n] = part.astype(BF)

    for i in range(owners):
        give(i, 3, dot_tn(bb[:, pl.ds(starts[i], size)], attended))

    for copy in copies:
        copy.wait()
    for i in range(owners):
        total = dot_tn(x_cols[i], every[...])
        for n in range(3):
            give(i, n, total[:, n * width : (n + 1) * width])
    own = jnp.concatenate([every[spot, :] for spot in spots[:slots]], axis=0)
    first = sum(dot_nt(own[:, n * width : (n + 1) * width], w_cols[n]) for n in range(3))

    @pl.when(step == 0)
    def _():
        acc[...] = first

    @pl.when(step > 0)
    def _():
        acc[...] += first

    @pl.when(step == pl.num_programs(0) - 1)
    def _():
        total, half = acc[...].astype(BF), acc.shape[0] // 2
        for n, at in enumerate((slice(0, half), slice(half, 2 * half))):
            keep_ref = first_ref if n == 0 else give_ref
            keep_ref[:, : acc.shape[1]] = total[at]
            keep_ref[:, acc.shape[1] :] = more_ref[at, :]


def attend_back(
    places, starts, pieces, wo, q, k, v, cos, sin, docs, more, x_seq, wq, wk, wv,
    size, slots, scale, shift,
):
    seq, width = x_seq.shape
    chunk = pieces[0].shape[0]
    cols = wo.shape[0]
    heads = cols // HD
    step = min(2, heads)
    own = slots * chunk
    owners = starts.shape[0]
    whole = lambda *shape: pl.BlockSpec(
        shape, lambda i: (0,) * len(shape), pipeline_mode=pl.Buffered(1)
    )
    sspec = pl.BlockSpec((seq, step * HD), lambda i: (0, i))
    hbm = pl.BlockSpec(memory_space=pl.ANY)
    return pl.pallas_call(
        functools.partial(attend_back_kernel, chunk, slots, scale, shift),
        grid=(heads // step,),
        in_specs=[pl.BlockSpec(memory_space=pltpu.SMEM)] * 2 + [hbm] * len(pieces)
        + [pl.BlockSpec((step * HD, width), lambda i: (i, 0)),
           sspec, sspec, sspec, whole(seq, HD), whole(seq, HD), whole(1, seq), whole(*more.shape)]
        + [hbm] * 4,
        out_specs=[pl.BlockSpec((4, size, step * HD), lambda i: (0, 0, i)),
                   pl.BlockSpec((owners - 1, 4, size, step * HD), lambda i: (0, 0, 0, i)),
                   whole(own // 2, 2 * width), whole(own // 2, 2 * width)],
        out_shape=[jax.ShapeDtypeStruct((4, size, cols), F32),
                   jax.ShapeDtypeStruct((owners - 1, 4, size, cols), BF),
                   jax.ShapeDtypeStruct((own // 2, 2 * width), BF),
                   jax.ShapeDtypeStruct((own // 2, 2 * width), BF)],
        scratch_shapes=[pltpu.VMEM((seq, width), BF), pltpu.VMEM((owners, seq, size), BF),
                        pltpu.VMEM((3, width, step * HD), BF),
                        pltpu.VMEM((own, width), F32),
                        pltpu.VMEM((seq, 3 * step * HD), BF),
                        pltpu.SemaphoreType.DMA((len(pieces),)),
                        pltpu.SemaphoreType.DMA((owners,)), pltpu.SemaphoreType.DMA((3,))],
        compiler_params=pltpu.CompilerParams(vmem_limit_bytes=56 * MIB),
        cost_estimate=pl.CostEstimate(
            flops=2 * seq * width * cols + 14 * seq * seq * cols,
            bytes_accessed=2 * (seq + cols) * width + 20 * seq * cols,
            transcendentals=seq * seq * heads,
        ),
    )(
        places, starts, *pieces, in_hbm(wo), q, k, v, cos, sin,
        docs, more, in_hbm(x_seq), in_hbm(wq), in_hbm(wk), in_hbm(wv),
    )


def gate_math(gate, up, hidden_back):
    sig = jax.nn.sigmoid(gate)
    act = gate * sig
    hidden = (act * up).astype(BF)
    gate_back = (hidden_back * up * sig * (1.0 + gate * (1.0 - sig))).astype(BF)
    up_back = (hidden_back * act).astype(BF)
    return hidden, gate_back, up_back


def mlp_kernel(
    block, x_ref, hb_ref, wg_ref, wu_ref, hidden_ref, gate_ref, up_ref, back_ref
):
    x, total = x_ref[...], None
    for i in range(wg_ref.shape[1] // block):
        at = slice(i * block, (i + 1) * block)
        wg, wu = wg_ref[:, at], wu_ref[:, at]
        hidden_ref[:, at], gate_back, up_back = gate_math(
            dot(x, wg), dot(x, wu), hb_ref[:, at].astype(F32)
        )
        gate_ref[:, at] = gate_back
        up_ref[:, at] = up_back
        back = dot_nt(gate_back, wg) + dot_nt(up_back, wu)
        total = back if total is None else total + back
    back_ref[...] = total.astype(BF)


def mlp(x, hidden_back, wg, wu):
    rows, width = x.shape
    units = wg.shape[1]
    return pl.pallas_call(
        functools.partial(mlp_kernel, min(512, units)),
        in_specs=[VMEM_WHOLE] * 4,
        out_specs=[VMEM_WHOLE] * 4,
        out_shape=[
            *[jax.ShapeDtypeStruct((rows, units), BF)] * 3, jax.ShapeDtypeStruct((rows, width), BF)
        ],
        compiler_params=pltpu.CompilerParams(vmem_limit_bytes=20 * MIB),
        cost_estimate=pl.CostEstimate(
            flops=0, bytes_accessed=0, transcendentals=0
        ),
    )(x, hidden_back, in_vmem(wg), in_vmem(wu))


def tiles_of(sources, at_ref, first, tile):
    listed = []
    for n, source in enumerate(sources):
        for i in range(source.shape[0] // tile):
            index = at_ref[first + i] if n == 0 else i
            at = pl.ds(pl.multiple_of(index * tile, tile), tile) if n == 0 else pl.ds(i * tile, tile)
            listed.append((source, at))
    return listed


def hidden_back_kernel(tile, more, count, at_ref, *refs):
    sources, (wd_ref, hidden_ref, before) = refs[:count], refs[count : count + 3]
    out_ref, sum_ref, cot, total, sem = refs[-5:]
    step, block = pl.program_id(0), wd_ref.shape[0]
    copies = []
    for i, (source, at) in enumerate(tiles_of(sources, at_ref, 0, tile)):
        target = cot.at[pl.ds(i * tile, tile)]
        copies.append(pltpu.make_async_copy(source.at[at], target, sem.at[i]))

    def every_tile(waits):
        wd = wd_ref[...]
        own = dot(hidden_ref[...], wd)
        for i in range(0, len(copies), 2):
            if waits:
                copies[i].wait()
                copies[i + 1].wait()
            at = pl.ds(i * tile, 2 * tile)
            out_ref[at, :] = dot_nt(cot[at, :], wd).astype(BF)
        return own

    @pl.when(step == 0)
    def _():
        for copy in copies:
            copy.start()
        own = every_tile(True)
        total[...] = own + before[...] if more else own

    @pl.when(step > 0)
    def _():
        total[...] += every_tile(False)

    @pl.when(step == pl.num_programs(0) - 1)
    def _():
        sum_ref[...] = total[...].astype(sum_ref.dtype)


def hidden_back_of(turns, cots, wd, hidden, part, before=()):
    width = cots[0].shape[1]
    rows, units = sum(cot.shape[0] for cot in cots), wd.shape[0]
    tiles = rows // hidden.shape[0]
    block = min(512, units // 2)
    steps = units // 2 // block
    skip = part * steps
    tile = hidden.shape[0]
    whole = pl.BlockSpec((tile, width), lambda i: (0, 0), pipeline_mode=pl.Buffered(1))
    return pl.pallas_call(
        functools.partial(hidden_back_kernel, tile, len(before) > 0, len(cots)),
        grid=(steps,),
        in_specs=[pl.BlockSpec(memory_space=pltpu.SMEM)] + [HBM_WHOLE] * len(cots)
        + [pl.BlockSpec((block, width), lambda i: (i + skip, 0)),
           pl.BlockSpec((tile, block), lambda i: (0, i + skip))]
        + [whole, HBM_WHOLE][: len(before)],
        out_specs=[pl.BlockSpec((rows, block), lambda i: (0, i + skip)), whole],
        out_shape=[jax.ShapeDtypeStruct((rows, units), BF),
                   jax.ShapeDtypeStruct((tile, width), BF if part else F32)],
        scratch_shapes=[pltpu.VMEM((rows, width), BF), pltpu.VMEM((tile, width), F32),
                        pltpu.SemaphoreType.DMA((tiles,))],
        input_output_aliases={len(cots) + 4: 0} if before else {},
        compiler_params=pltpu.CompilerParams(vmem_limit_bytes=56 * MIB),
        cost_estimate=pl.CostEstimate(
            flops=rows * width * units, bytes_accessed=2 * width * (rows + units),
            transcendentals=0,
        ),
    )(turns, *[in_hbm(cot) for cot in cots], in_hbm(wd), hidden, *before)


def join_kernel(count, *refs):
    pieces, out_ref, sem = refs[:count], refs[count], refs[-1]
    size = pieces[0].shape[0]
    copies = [
        pltpu.make_async_copy(piece, out_ref.at[pl.ds(i * size, size)], sem.at[i])
        for i, piece in enumerate(pieces)
    ]
    for copy in copies:
        copy.start()
    for copy in copies:
        copy.wait()


def join(pieces):
    size, width = pieces[0].shape
    return pl.pallas_call(
        functools.partial(join_kernel, len(pieces)),
        in_specs=[HBM_WHOLE] * len(pieces),
        out_specs=pl.BlockSpec(memory_space=pl.ANY),
        out_shape=jax.ShapeDtypeStruct((size * len(pieces), width), BF),
        scratch_shapes=[pltpu.SemaphoreType.DMA((len(pieces),))],
        compiler_params=pltpu.CompilerParams(vmem_limit_bytes=2 * MIB),
        cost_estimate=pl.CostEstimate(flops=0, bytes_accessed=0, transcendentals=0),
    )(*pieces)


def mlp_grad_kernel(count, chunk, parts, at_ref, *refs):
    pieces, cots, refs = refs[:count], refs[count : count + parts], refs[count + parts :]
    (own_hid, own_gate, own_up, hb_ref, wg_ref, wu_ref, gg_ref, ug_ref, dg_ref, gain_ref,
     x_all, cb, hid, gbk, ubk, gain_sum, sem, cot_sem) = refs
    size = cb.shape[1]
    tile = pieces[0].shape[0]
    per = tile // chunk
    tiles = x_all.shape[0] // tile
    own = pl.ds(pl.multiple_of(at_ref[0] * size, size), size)

    @pl.when(pl.program_id(0) == 0)
    def _():
        copies = []
        for i in range(count * per):
            spot = pl.ds(pl.multiple_of(at_ref[1 + i] * chunk, chunk), chunk)
            part = pieces[i // per].at[pl.ds(i % per * chunk, chunk)]
            copies.append(pltpu.make_async_copy(part, x_all.at[spot], sem.at[i]))
        base = 1 + count * per
        for i in range(per):
            spot = pl.ds(pl.multiple_of(at_ref[base + i] * chunk, chunk), chunk)
            target = cb.at[pl.ds(i * chunk, chunk)]
            copies.append(pltpu.make_async_copy(cots[0].at[spot, own], target, cot_sem.at[i]))
        for i, (source, spot) in enumerate(tiles_of(cots, at_ref, base + per, tile)):
            if i > 0:
                target = cb.at[pl.ds(i * tile, tile)]
                copies.append(
                    pltpu.make_async_copy(source.at[spot, own], target, cot_sem.at[per + i])
                )
        for copy in copies:
            copy.start()
        for copy in copies:
            copy.wait()

    hid[:tile, :], gbk[:tile, :], ubk[:tile, :] = own_hid[...], own_gate[...], own_up[...]
    wg, wu = wg_ref[...], wu_ref[...]
    for i in range(1, tiles):
        at = pl.ds(i * tile, tile)
        x = x_all[at, :]
        hid[at, :], gbk[at, :], ubk[at, :] = gate_math(
            dot(x, wg), dot(x, wu), hb_ref[at, :].astype(F32)
        )
    xb = x_all[:, own]
    gate_grad = dot_tn(xb, gbk[...])
    up_grad = dot_tn(xb, ubk[...])
    gg_ref[...] = gate_grad
    ug_ref[...] = up_grad
    dg_ref[...] = dot_tn(hid[...], cb[...])
    gain = jnp.sum(
        wg_ref[own, :].astype(F32) * gate_grad + wu_ref[own, :].astype(F32) * up_grad,
        axis=1, keepdims=True,
    )

    @pl.when(pl.program_id(0) == 0)
    def _():
        gain_sum[...] = gain

    @pl.when(pl.program_id(0) > 0)
    def _():
        gain_sum[...] += gain

    @pl.when(pl.program_id(0) == pl.num_programs(0) - 1)
    def _():
        gain_ref[...] = jnp.broadcast_to(gain_sum[...], (size, HD)).T[:1, :]


def mlp_grad(places, chunk, pieces, own, cots, hb, wg, wu, size):
    tile, width = pieces[0].shape
    rows, units = hb.shape
    block = min(256, units)
    wspec = pl.BlockSpec((width, block), lambda i, at: (0, i))
    ospec = pl.BlockSpec((tile, block), lambda i, at: (0, i))
    grid_spec = pltpu.PrefetchScalarGridSpec(
        num_scalar_prefetch=1,
        grid=(units // block,),
        in_specs=[HBM_WHOLE] * (len(pieces) + len(cots)) + [ospec] * 3
        + [pl.BlockSpec((rows, block), lambda i, at: (0, i)), wspec, wspec],
        out_specs=[pl.BlockSpec((size, block), lambda i, at: (0, i))] * 2
        + [pl.BlockSpec((block, size), lambda i, at: (i, 0)),
           pl.BlockSpec((1, size), lambda i, at: (0, 0))],
        scratch_shapes=[pltpu.VMEM((rows, width), BF), pltpu.VMEM((rows, size), BF)]
        + [pltpu.VMEM((rows, block), BF)] * 3
        + [pltpu.VMEM((size, 1), F32), pltpu.SemaphoreType.DMA((rows // chunk,)),
           pltpu.SemaphoreType.DMA((tile // chunk + rows // tile,))],
    )
    return pl.pallas_call(
        functools.partial(mlp_grad_kernel, len(pieces), chunk, len(cots)),
        grid_spec=grid_spec,
        out_shape=[jax.ShapeDtypeStruct((size, units), F32)] * 2
        + [jax.ShapeDtypeStruct((units, size), F32), jax.ShapeDtypeStruct((1, size), F32)],
        compiler_params=pltpu.CompilerParams(vmem_limit_bytes=56 * MIB),
        cost_estimate=pl.CostEstimate(
            flops=2 * rows * units * (2 * width + 3 * size),
            bytes_accessed=4 * width * units + 4 * rows * width,
            transcendentals=0,
        ),
    )(
        places, *pieces, *[in_hbm(cot) for cot in cots], *[in_hbm(rows) for rows in own],
        in_hbm(hb), in_hbm(wg), in_hbm(wu),
    )


def row_mean(values):
    return jnp.mean(values, axis=-1, keepdims=True)


def norm_parts(values):
    root = lax.rsqrt(row_mean(values * values) + EPS)
    return values * root, root


def norm_back(upstream, scaled, root, gain):
    inner = upstream * gain
    return root * (inner - scaled * row_mean(inner * scaled))


def per_device(
    activations, cotangent, doc_ids, attn_gain, query_weight, key_weight, value_weight,
    out_weight, mlp_gain, gate_weight, up_weight, down_weight,
):
    rows, width = activations.shape[1:]
    n_dp, n_ctx, n_t = lax.axis_size("dp"), lax.axis_size("ctx"), lax.axis_size("tensor")
    dp, ctx, place = lax.axis_index("dp"), lax.axis_index("ctx"), lax.axis_index("tensor")
    chunk = rows // n_t
    length = rows * n_ctx
    slots = slot_order(n_t)
    scale, shift = HD ** (-0.5), -math.log(length)
    gain_first, gain_second = attn_gain.astype(F32), mlp_gain.astype(F32)

    slot_places = jnp.stack([place ^ slot for slot in slots])
    normed_first, mine, cot, cot_mine, inputs_mine, scaled_mine, root_mine = arrange(
        slot_places, activations[0], cotangent[0], attn_gain[None]
    )

    bits = list(reversed(bits_of(n_t)))

    def spread(rings, beside=()):
        lists = [[ring] for ring in rings]
        for bit in bits:
            lists = [items + [swap(item, "tensor", bit) for item in items] for items in lists]
            if bit == bits[0]:
                lists = after(lists, beside)
        return lists

    rings = ring_of(mine)[1:]
    cot_own = lax.all_gather(cot_mine, ("ctx", "tensor"), axis=0, tiled=True)

    ring_at = ctx ^ jnp.arange(n_ctx, dtype=jnp.int32)
    seq_places = jnp.concatenate([
        ring_at[k : k + 1] * n_t + (place ^ slot) for k in range(n_ctx) for slot in slots
    ])
    docs = doc_ids
    out_cols = width // (n_dp * n_ctx)
    owners = jnp.stack([((dp + step) % n_dp) * n_ctx + ctx for step in range(n_dp)])
    starts = owners * out_cols
    owner = owners[0]
    half = place & 1
    places = [owner[None]]
    for flip in (0, 1):
        for step in range(n_dp):
            for index in range(n_t // 2):
                if step == 0:
                    group = jnp.arange(n_ctx, dtype=jnp.int32)
                else:
                    other_half = ring_at // (n_ctx // 2) != half
                    group = step * n_ctx + other_half * (n_ctx // 2) + ring_at % (n_ctx // 2)
                inside = place ^ slots[index] ^ flip
                if step == 0:
                    inside = jnp.where(group == 0, index + flip * (n_t // 2), inside)
                places.append(group * n_t + inside)
    places = jnp.concatenate(places + [ctx * n_t + slot_places, ring_at])
    frequency = np.float32(10000.0) ** (
        -np.arange(HD // 2, dtype=np.float32) * np.float32(2.0) / np.float32(HD)
    )
    angles = np.arange(length, dtype=np.float32)[:, None] * frequency[None, :]
    cos = jnp.asarray(np.concatenate([np.cos(angles), np.cos(angles)], axis=1))
    sin = jnp.asarray(np.concatenate([-np.sin(angles), np.sin(angles)], axis=1))
    rings = [after(ring, seq_places, starts, places) for ring in rings]
    hidden_back = lax.dot_general(
        after(cot, rings), down_weight, (((1,), (1,)), ((), ())), preferred_element_type=F32
    ).astype(BF)
    seq_pieces = spread(rings, hidden_back)
    own_pieces = [normed_first[i * chunk : (i + 1) * chunk] for i in range(n_t)]
    q, k, v, attended, mass, x_seq = attend(
        seq_places, own_pieces + sum(seq_pieces, []), docs, cos, sin,
        query_weight, key_weight, value_weight, n_t, scale, shift,
    )
    attn_mass = from_slots(mass[:, :, 0].T, slots, place)

    def over_dp(items):
        return [turn(item, "dp", step) for step in range(1, n_dp) for item in items]

    def over_tensor(items, bits):
        for bit in bits:
            items = items + [swap(item, "tensor", bit) for item in items]
        return items

    branch = scatter_tensor(
        jnp.dot(attended, out_weight, preferred_element_type=F32).astype(BF), attn_mass
    )
    middle = inputs_mine + branch
    scaled_second, root_second = norm_parts(middle)
    normed_chunk = (scaled_second * gain_second).astype(BF)
    cot_own = after(cot_own, normed_chunk)
    size = length // 2
    cot_half = lax.dynamic_slice_in_dim(cot_own, half * size, size, 0)
    cot_far = [turn(cot_half, "dp", step) for step in range(1, n_dp)]
    gate, up = fetch(after(gate_weight, normed_chunk), up_weight)
    normed_second = gather_tensor(normed_chunk, (gate, up))
    chunk_rings = ring_of(normed_chunk)
    hidden, gate_back, up_back, second_part = mlp(normed_second, hidden_back, gate, up)
    second_part, chunk_rings = lax.optimization_barrier((second_part, chunk_rings))
    x_near = [join(chunk_rings)]
    x_far = over_dp(x_near)
    x_near_more = over_tensor(x_near, bits[:-1])[1:]
    second_back = scatter_tensor(second_part)
    middle_back = cot_mine.astype(F32) + norm_back(
        second_back, scaled_second, root_second, gain_second
    )
    branch_back = middle_back.astype(BF)
    bb_rings = ring_of(branch_back)
    cots = [cot_own] + sum([[far, swap(far, "tensor", 1)] for far in cot_far], [])
    cots = after(cots, branch_back)
    hidden_back_all, mlp_part = hidden_back_of(ring_at, cots, down_weight, hidden, 0)
    bb_rings, x_far, x_near_more = after((bb_rings, x_far, x_near_more), hidden_back_all)
    hidden_back_all, mlp_part = hidden_back_of(
        ring_at, after(cots, bb_rings), down_weight, hidden, 1, (mlp_part, hidden_back_all)
    )
    bb_pieces = spread(bb_rings, mlp_part)
    x_far_more = over_tensor(x_far, bits[:-1])[len(x_far) :]

    mine_grads, theirs_grads, kept_half, given_half = attend_back(
        seq_places, starts, sum(bb_pieces, []), out_weight, q, k, v, cos, sin, docs, mlp_part,
        x_seq, query_weight, key_weight, value_weight, out_cols, n_t, scale, shift,
    )

    theirs = [turn(theirs_grads[step - 1], "dp", step) for step in range(1, n_dp)]

    x_pieces = over_tensor(x_near + x_near_more + x_far + x_far_more, bits[-1:])

    gate_grad, up_grad, down_grad, mlp_gain_sum = mlp_grad(
        after(places, kept_half), chunk, x_pieces, (hidden, gate_back, up_back), cots,
        hidden_back_all, gate_weight, up_weight, out_cols,
    )
    mlp_gain_sum = mlp_gain_sum[0]
    theirs = after(theirs, gate_grad)
    both = scatter_tensor((kept_half, given_half), gate_grad)
    first_back, mlp_out = both[:, :width], both[:, width:]
    input_grad = (
        middle_back + norm_back(first_back, scaled_mine, root_mine, gain_first)
    ).astype(BF)
    layer_out = (middle + mlp_out).astype(BF)
    results = gather_tensor(jnp.concatenate([layer_out, input_grad], axis=1))
    results = from_slots(results, slots, place)
    layer_out, input_grad = results[:, :width], results[:, width:]
    attn_grads = mine_grads + sum(part.astype(F32) for part in theirs)
    query_grad, key_grad, value_grad = attn_grads[0], attn_grads[1], attn_grads[2]
    out_grad = attn_grads[3].T

    def rows_of(weight):
        return lax.dynamic_slice_in_dim(weight, owner * out_cols, out_cols, 0).astype(F32)

    attn_gain_sum = jnp.sum(
        rows_of(query_weight) * query_grad + rows_of(key_weight) * key_grad
        + rows_of(value_weight) * value_grad, axis=1,
    )
    gains = jnp.stack([attn_gain_sum, mlp_gain_sum])
    for bit in bits:
        gains = gains + swap(gains, "tensor", bit)
    gain_grads = gains / lax.dynamic_slice_in_dim(
        jnp.stack([gain_first, gain_second]), owner * out_cols, out_cols, 1
    )

    return (
        layer_out[None], input_grad[None], gain_grads[0], query_grad, key_grad, value_grad,
        out_grad, gain_grads[1], gate_grad, up_grad, down_grad, attn_mass[None],
    )


def solution(mesh):
    return jax.shard_map(
        per_device,
        mesh=mesh,
        in_specs=(
            P("dp", "ctx", None),
            P("dp", "ctx", None),
            P("dp", None),
            P(),
            P(None, "tensor"),
            P(None, "tensor"),
            P(None, "tensor"),
            P("tensor", None),
            P(),
            P(None, "tensor"),
            P(None, "tensor"),
            P("tensor", None),
        ),
        out_specs=(
            P("dp", "ctx", None),
            P("dp", "ctx", None),
            P(("dp", "ctx")),
            P(("dp", "ctx"), "tensor"),
            P(("dp", "ctx"), "tensor"),
            P(("dp", "ctx"), "tensor"),
            P("tensor", ("dp", "ctx")),
            P(("dp", "ctx")),
            P(("dp", "ctx"), "tensor"),
            P(("dp", "ctx"), "tensor"),
            P("tensor", ("dp", "ctx")),
            P("dp", "ctx", "tensor"),
        ),
        check_vma=False,
    )
```

```python
import functools
import math

import jax
import jax.numpy as jnp
import numpy as np
from jax import lax
from jax.experimental import pallas as pl
from jax.experimental.pallas import tpu as pltpu
from jax.sharding import PartitionSpec as P

HD = 128
EPS = 1e-05
BF = jnp.bfloat16
F32 = jnp.float32
MIB = 1024 * 1024


def swap(values, axis, distance):
    count = lax.axis_size(axis)
    return lax.ppermute(values, axis, [(i, i ^ distance) for i in range(count)])


def turn(values, axis, shift):
    count = lax.axis_size(axis)
    return lax.ppermute(values, axis, [(i, (i + shift) % count) for i in range(count)])


def after(value, *others):
    return lax.optimization_barrier((value, others))[0]


def in_hbm(values):
    return pltpu.with_memory_space_constraint(values, pltpu.HBM)


def in_vmem(values):
    return pltpu.with_memory_space_constraint(values, pltpu.VMEM)


def bits_of(count):
    return [1 << i for i in range(count.bit_length() - 1)]


def slot_order(count):
    order = [0]
    for bit in reversed(bits_of(count)):
        order = order + [slot ^ bit for slot in order]
    return order


def gather_tensor(rows, beside=()):
    for bit in reversed(bits_of(lax.axis_size("tensor"))):
        got = after(swap(rows, "tensor", bit), beside)
        rows, beside = jnp.concatenate([rows, got], axis=0), ()
    return rows


def scatter_tensor(rows, beside=()):
    bits = bits_of(lax.axis_size("tensor"))
    for bit in bits:
        if not isinstance(rows, tuple):
            half = rows.shape[0] // 2
            rows = rows[:half], rows[half:]
        got = swap(rows[1].astype(BF), "tensor", bit)
        if bit == bits[-1]:
            got = after(got, beside)
        rows = rows[0].astype(F32) + got.astype(F32)
    return rows


def ring_of(rows):
    return [rows] + [swap(rows, "ctx", k) for k in range(1, lax.axis_size("ctx"))]


def from_slots(blocks, slots, place):
    size = blocks.shape[0] // len(slots)
    out = jnp.zeros_like(blocks)
    for index, slot in enumerate(slots):
        out = lax.dynamic_update_slice_in_dim(
            out, blocks[index * size : (index + 1) * size], (place ^ slot) * size, 0
        )
    return out


def rope_rows(u, cos, sin):
    return u * cos + pltpu.roll(u, HD // 2, 1) * sin


def rope_back_rows(u, cos, sin):
    return u * cos - pltpu.roll(u, HD // 2, 1) * sin


def dot(a, b):
    return lax.dot_general(a, b, (((1,), (0,)), ((), ())), preferred_element_type=F32)


def dot_nt(a, b):
    return lax.dot_general(a, b, (((1,), (1,)), ((), ())), preferred_element_type=F32)


def dot_tn(a, b):
    return lax.dot_general(a, b, (((0,), (0,)), ((), ())), preferred_element_type=F32)


def place_rows(step, pieces, places, rows, sem, start=True, wait=True):
    @pl.when(step == 0)
    def _():
        copies = []
        for i, (piece, place) in enumerate(zip(pieces, places, strict=True)):
            copies.append(pltpu.make_async_copy(piece, rows.at[place], sem.at[i]))
        if start:
            for copy in copies:
                copy.start()
        if wait:
            for copy in copies:
                copy.wait()


def chunk_places(at_ref, first, count, chunk):
    return [
        pl.ds(pl.multiple_of(at_ref[first + i] * chunk, chunk), chunk) for i in range(count)
    ]


NEVER = -1e30
VMEM_WHOLE = pl.BlockSpec(memory_space=pltpu.VMEM)
HBM_WHOLE = pl.BlockSpec(memory_space=pl.ANY)


def fetch_kernel(count, *refs):
    sources, targets, sem = refs[:count], refs[count : 2 * count], refs[-1]
    copies = [
        pltpu.make_async_copy(source, target, sem.at[i])
        for i, (source, target) in enumerate(zip(sources, targets, strict=True))
    ]
    for copy in copies:
        copy.start()
    for copy in copies:
        copy.wait()


def fetch(*weights):
    return pl.pallas_call(
        functools.partial(fetch_kernel, len(weights)),
        in_specs=[HBM_WHOLE] * len(weights),
        out_specs=[VMEM_WHOLE] * len(weights),
        out_shape=[pltpu.VMEM(weight.shape, weight.dtype) for weight in weights],
        scratch_shapes=[pltpu.SemaphoreType.DMA((len(weights),))],
        compiler_params=pltpu.CompilerParams(vmem_limit_bytes=2 * MIB),
        cost_estimate=pl.CostEstimate(
            flops=0, bytes_accessed=0, transcendentals=0
        ),
    )(*[in_hbm(weight) for weight in weights])


def arrange_kernel(
    at_ref, rows_hbm, cot_hbm, gain_ref, normed_ref, mine_ref, cots_ref, cot_mine_ref,
    inputs_ref, scaled_ref, root_ref, rows_in, rows_sem, cot_sem,
):
    chunk = mine_ref.shape[0]
    spots = chunk_places(at_ref, 0, normed_ref.shape[0] // chunk, chunk)
    parts = [slice(i * chunk, (i + 1) * chunk) for i in range(len(spots))]
    copies = []
    for i, (spot, part) in enumerate(zip(spots, parts, strict=True)):
        copies.append((
            pltpu.make_async_copy(rows_hbm.at[spot], rows_in.at[part], rows_sem.at[i]),
            pltpu.make_async_copy(cot_hbm.at[spot], cots_ref.at[part], cot_sem.at[i]),
        ))
    for pair in copies:
        for copy in pair:
            copy.start()
    gain = gain_ref[...].astype(F32).reshape(1, -1)
    for i, (part, pair) in enumerate(zip(parts, copies, strict=True)):
        pair[0].wait()
        rows = rows_in[part, :].astype(F32)
        root = lax.rsqrt(jnp.mean(rows * rows, axis=-1, keepdims=True) + EPS)
        normed = (rows * root * gain).astype(BF)
        normed_ref[part, :] = normed
        pair[1].wait()
        if i == 0:
            mine_ref[...] = normed
            cot_mine_ref[...] = cots_ref[part, :]
            inputs_ref[...] = rows
            scaled_ref[...] = rows * root
            root_ref[...] = jnp.broadcast_to(root, root_ref.shape)


def arrange(places, rows, cot, gain):
    count, width = rows.shape
    slots = places.shape[0]
    chunk = count // slots
    shapes = [(count, width), (chunk, width)] * 2
    more = [(chunk, width)] * 3
    return pl.pallas_call(
        arrange_kernel,
        in_specs=[pl.BlockSpec(memory_space=pltpu.SMEM), HBM_WHOLE, HBM_WHOLE, VMEM_WHOLE],
        out_specs=[VMEM_WHOLE] * 7,
        out_shape=[jax.ShapeDtypeStruct(shape, BF) for shape in shapes]
        + [jax.ShapeDtypeStruct(shape, F32) for shape in more],
        scratch_shapes=[pltpu.VMEM((count, width), BF),
                        pltpu.SemaphoreType.DMA((slots,)), pltpu.SemaphoreType.DMA((slots,))],
        compiler_params=pltpu.CompilerParams(vmem_limit_bytes=16 * MIB),
        cost_estimate=pl.CostEstimate(
            flops=8 * count * width, bytes_accessed=8 * count * width, transcendentals=0
        ),
    )(places, in_hbm(rows), in_hbm(cot), gain)


def column_of(row):
    return jnp.broadcast_to(row, (HD, row.shape[1])).T[:, :1]


def attend_kernel(chunk, slots, scale, shift, at_ref, *refs):
    count = len(refs) - 16
    pieces = refs[:count]
    (doc_ref, cos_ref, sin_ref, wq_ref, wk_ref, wv_ref, q_ref, k_ref, v_ref, att_ref, mass_ref,
     seq_hbm, x, doc_column, sem, out_sem) = refs[count:]
    step, last = pl.program_id(0), pl.num_programs(0) - 1
    place_rows(step, pieces, chunk_places(at_ref, 0, count, chunk), x, sem)
    keep = pltpu.make_async_copy(x, seq_hbm, out_sem)

    @pl.when(step == 0)
    def _():
        keep.start()

    cos, sin = cos_ref[...], sin_ref[...]
    own = chunk_places(at_ref, 0, slots, chunk)
    doc_column[...] = column_of(doc_ref[...])
    shape = (chunk, doc_ref.shape[1])
    bias = []
    for i, spot in enumerate(own):
        own_spots = lax.broadcasted_iota(jnp.int32, shape, 0) + at_ref[i] * chunk
        allowed = (lax.broadcasted_iota(jnp.int32, shape, 1) <= own_spots) & (
            doc_column[spot, :] == doc_ref[...]
        )
        bias.append(jnp.where(allowed, shift, NEVER))
    bias = jnp.concatenate(bias, axis=0)
    rows = x[...]
    q_all = dot(rows, wq_ref[...])
    k_all = dot(rows, wk_ref[...])
    v_all = dot(rows, wv_ref[...]).astype(BF)
    v_ref[...] = v_all
    for j in range(q_all.shape[1] // HD):
        cols = slice(j * HD, (j + 1) * HD)
        q_ref[:, cols] = rope_rows(q_all[:, cols], cos, sin).astype(BF)
        k = rope_rows(k_all[:, cols], cos, sin).astype(BF)
        k_ref[:, cols] = k
        q = jnp.concatenate([q_ref[spot, cols] for spot in own], axis=0)
        weights = jax.nn.sigmoid(dot_nt(q, k) * scale + bias)
        mass_ref[j] = jnp.sum(weights, axis=-1, keepdims=True)
        att_ref[:, cols] = dot(weights.astype(BF), v_all[:, cols]).astype(BF)

    @pl.when(step == last)
    def _():
        keep.wait()


def attend(places, pieces, docs, cos, sin, wq, wk, wv, slots, scale, shift):
    chunk, width = pieces[0].shape
    seq, rows = chunk * len(pieces), chunk * slots
    cols = wq.shape[1]
    heads = cols // HD
    step = min(2, heads)
    whole = lambda *shape: pl.BlockSpec(
        shape, lambda i: (0,) * len(shape), pipeline_mode=pl.Buffered(1)
    )
    hbm = pl.BlockSpec(memory_space=pl.ANY)
    wspec = pl.BlockSpec((width, step * HD), lambda i: (0, i))
    sspec = pl.BlockSpec((seq, step * HD), lambda i: (0, i))
    return pl.pallas_call(
        functools.partial(attend_kernel, chunk, slots, scale, shift),
        grid=(heads // step,),
        in_specs=[pl.BlockSpec(memory_space=pltpu.SMEM)] + [hbm] * len(pieces)
        + [whole(1, seq), whole(seq, HD), whole(seq, HD)]
        + [wspec] * 3,
        out_specs=[sspec, sspec, sspec,
                   pl.BlockSpec((rows, step * HD), lambda i: (0, i)),
                   pl.BlockSpec((step, rows, 1), lambda i: (i, 0, 0)),
                   pl.BlockSpec(memory_space=pltpu.HBM)],
        out_shape=[jax.ShapeDtypeStruct((seq, cols), BF)] * 3
        + [jax.ShapeDtypeStruct((rows, cols), BF), jax.ShapeDtypeStruct((heads, rows, 1), F32),
           jax.ShapeDtypeStruct((seq, width), BF)],
        scratch_shapes=[pltpu.VMEM((seq, width), BF), pltpu.VMEM((seq, 1), jnp.int32),
                        pltpu.SemaphoreType.DMA((len(pieces),)), pltpu.SemaphoreType.DMA],
        compiler_params=pltpu.CompilerParams(vmem_limit_bytes=56 * MIB),
        cost_estimate=pl.CostEstimate(
            flops=2 * seq * width * cols * 3, bytes_accessed=6 * width * cols, transcendentals=0
        ),
    )(places, *pieces, docs, cos, sin, wq, wk, wv)


def attend_back_kernel(chunk, slots, scale, shift, at_ref, starts_ref, *refs):
    count = len(refs) - 24
    pieces = refs[:count]
    (wo_ref, q_ref, k_ref, v_ref, cos_ref, sin_ref, doc_row_ref, more_ref,
     x_hbm, wq_hbm, wk_hbm, wv_hbm, mine_ref, theirs_ref, first_ref, give_ref,
     bb, x_cols, w_cols, acc, every, bb_sem, x_sem, w_sem) = refs[count:]
    step = pl.program_id(0)
    owners = x_cols.shape[0]
    spots = chunk_places(at_ref, 0, count, chunk)
    place_rows(step, pieces, spots, bb, bb_sem, wait=False)
    seq, size, width = bb.shape[0], x_cols.shape[2], w_cols.shape[2]
    starts = [pl.multiple_of(starts_ref[i], HD) for i in range(owners)]
    at = pl.ds(pl.multiple_of(step * width, HD), width)
    copies = [
        pltpu.make_async_copy(x_hbm.at[:, pl.ds(starts[i], size)], x_cols.at[i], x_sem.at[i])
        for i in range(owners)
    ] + [
        pltpu.make_async_copy(w_hbm.at[:, at], w_cols.at[i], w_sem.at[i])
        for i, w_hbm in enumerate((wq_hbm, wk_hbm, wv_hbm))
    ]
    for copy in copies:
        copy.start()

    block = min(256, seq)
    parts = [slice(i * block, (i + 1) * block) for i in range(seq // block)]
    heads = [slice(j * HD, (j + 1) * HD) for j in range(width // HD)]
    weights, attended = {}, []
    doc_column = column_of(doc_row_ref[...])
    for i, part in enumerate(parts):
        shape = (block, part.stop)
        allowed = (
            lax.broadcasted_iota(jnp.int32, shape, 1)
            <= lax.broadcasted_iota(jnp.int32, shape, 0) + part.start
        ) & (doc_column[part, :] == doc_row_ref[:, : part.stop])
        bias = jnp.where(allowed, shift, NEVER)
        row = []
        for j, cols in enumerate(heads):
            scores = dot_nt(q_ref[part, cols], k_ref[: part.stop, cols]) * scale + bias
            weights[i, j] = jax.nn.sigmoid(scores)
            row.append(dot(weights[i, j].astype(BF), v_ref[: part.stop, cols]).astype(BF))
        attended.append(jnp.concatenate(row, axis=1))
    attended = jnp.concatenate(attended, axis=0)

    place_rows(step, pieces, spots, bb, bb_sem, start=False)
    ab_all = dot_nt(bb[...], wo_ref[...]).astype(BF)
    for j, cols in enumerate(heads):
        key_sums, value_sums = [None] * len(parts), [None] * len(parts)
        for i, part in enumerate(parts):
            ab, weight = ab_all[part, cols], weights[i, j]
            slope = weight - weight * weight
            back = (dot_nt(ab, v_ref[: part.stop, cols]) * slope).astype(BF)
            weight = weight.astype(BF)
            query_back = dot(back, k_ref[: part.stop, cols]) * scale
            every[part, cols] = rope_back_rows(
                query_back, cos_ref[part, :], sin_ref[part, :]
            ).astype(BF)
            for n in range(i + 1):
                key_part = dot_tn(back[:, parts[n]], q_ref[part, cols])
                value_part = dot_tn(weight[:, parts[n]], ab)
                key_sums[n] = key_part if i == n else key_sums[n] + key_part
                value_sums[n] = value_part if i == n else value_sums[n] + value_part
        for n, part in enumerate(parts):
            at_key = slice(width + cols.start, width + cols.stop)
            at_value = slice(2 * width + cols.start, 2 * width + cols.stop)
            every[part, at_key] = rope_back_rows(
                key_sums[n] * scale, cos_ref[part, :], sin_ref[part, :]
            ).astype(BF)
            every[part, at_value] = value_sums[n].astype(BF)

    def give(i, n, part):
        if i == 0:
            mine_ref[n] = part
        else:
            theirs_ref[i - 1, n] = part.astype(BF)

    for i in range(owners):
        give(i, 3, dot_tn(bb[:, pl.ds(starts[i], size)], attended))

    for copy in copies:
        copy.wait()
    for i in range(owners):
        total = dot_tn(x_cols[i], every[...])
        for n in range(3):
            give(i, n, total[:, n * width : (n + 1) * width])
    own = jnp.concatenate([every[spot, :] for spot in spots[:slots]], axis=0)
    first = sum(dot_nt(own[:, n * width : (n + 1) * width], w_cols[n]) for n in range(3))

    @pl.when(step == 0)
    def _():
        acc[...] = first

    @pl.when(step > 0)
    def _():
        acc[...] += first

    @pl.when(step == pl.num_programs(0) - 1)
    def _():
        total, half = acc[...].astype(BF), acc.shape[0] // 2
        for n, at in enumerate((slice(0, half), slice(half, 2 * half))):
            keep_ref = first_ref if n == 0 else give_ref
            keep_ref[:, : acc.shape[1]] = total[at]
            keep_ref[:, acc.shape[1] :] = more_ref[at, :]


def attend_back(
    places, starts, pieces, wo, q, k, v, cos, sin, docs, more, x_seq, wq, wk, wv,
    size, slots, scale, shift,
):
    seq, width = x_seq.shape
    chunk = pieces[0].shape[0]
    cols = wo.shape[0]
    heads = cols // HD
    step = min(2, heads)
    own = slots * chunk
    owners = starts.shape[0]
    whole = lambda *shape: pl.BlockSpec(
        shape, lambda i: (0,) * len(shape), pipeline_mode=pl.Buffered(1)
    )
    sspec = pl.BlockSpec((seq, step * HD), lambda i: (0, i))
    hbm = pl.BlockSpec(memory_space=pl.ANY)
    return pl.pallas_call(
        functools.partial(attend_back_kernel, chunk, slots, scale, shift),
        grid=(heads // step,),
        in_specs=[pl.BlockSpec(memory_space=pltpu.SMEM)] * 2 + [hbm] * len(pieces)
        + [pl.BlockSpec((step * HD, width), lambda i: (i, 0)),
           sspec, sspec, sspec, whole(seq, HD), whole(seq, HD), whole(1, seq), whole(*more.shape)]
        + [hbm] * 4,
        out_specs=[pl.BlockSpec((4, size, step * HD), lambda i: (0, 0, i)),
                   pl.BlockSpec((owners - 1, 4, size, step * HD), lambda i: (0, 0, 0, i)),
                   whole(own // 2, 2 * width), whole(own // 2, 2 * width)],
        out_shape=[jax.ShapeDtypeStruct((4, size, cols), F32),
                   jax.ShapeDtypeStruct((owners - 1, 4, size, cols), BF),
                   jax.ShapeDtypeStruct((own // 2, 2 * width), BF),
                   jax.ShapeDtypeStruct((own // 2, 2 * width), BF)],
        scratch_shapes=[pltpu.VMEM((seq, width), BF), pltpu.VMEM((owners, seq, size), BF),
                        pltpu.VMEM((3, width, step * HD), BF),
                        pltpu.VMEM((own, width), F32),
                        pltpu.VMEM((seq, 3 * step * HD), BF),
                        pltpu.SemaphoreType.DMA((len(pieces),)),
                        pltpu.SemaphoreType.DMA((owners,)), pltpu.SemaphoreType.DMA((3,))],
        compiler_params=pltpu.CompilerParams(vmem_limit_bytes=56 * MIB),
        cost_estimate=pl.CostEstimate(
            flops=2 * seq * width * cols + 14 * seq * seq * cols,
            bytes_accessed=2 * (seq + cols) * width + 20 * seq * cols,
            transcendentals=seq * seq * heads,
        ),
    )(
        places, starts, *pieces, in_hbm(wo), q, k, v, cos, sin,
        docs, more, in_hbm(x_seq), in_hbm(wq), in_hbm(wk), in_hbm(wv),
    )


def gate_math(gate, up, hidden_back):
    sig = jax.nn.sigmoid(gate)
    act = gate * sig
    hidden = (act * up).astype(BF)
    gate_back = (hidden_back * up * sig * (1.0 + gate * (1.0 - sig))).astype(BF)
    up_back = (hidden_back * act).astype(BF)
    return hidden, gate_back, up_back


def mlp_kernel(
    block, x_ref, hb_ref, wg_ref, wu_ref, hidden_ref, gate_ref, up_ref, back_ref
):
    x, total = x_ref[...], None
    for i in range(wg_ref.shape[1] // block):
        at = slice(i * block, (i + 1) * block)
        wg, wu = wg_ref[:, at], wu_ref[:, at]
        hidden_ref[:, at], gate_back, up_back = gate_math(
            dot(x, wg), dot(x, wu), hb_ref[:, at].astype(F32)
        )
        gate_ref[:, at] = gate_back
        up_ref[:, at] = up_back
        back = dot_nt(gate_back, wg) + dot_nt(up_back, wu)
        total = back if total is None else total + back
    back_ref[...] = total.astype(BF)


def mlp(x, hidden_back, wg, wu):
    rows, width = x.shape
    units = wg.shape[1]
    return pl.pallas_call(
        functools.partial(mlp_kernel, min(512, units)),
        in_specs=[VMEM_WHOLE] * 4,
        out_specs=[VMEM_WHOLE] * 4,
        out_shape=[
            *[jax.ShapeDtypeStruct((rows, units), BF)] * 3, jax.ShapeDtypeStruct((rows, width), BF)
        ],
        compiler_params=pltpu.CompilerParams(vmem_limit_bytes=20 * MIB),
        cost_estimate=pl.CostEstimate(
            flops=0, bytes_accessed=0, transcendentals=0
        ),
    )(x, hidden_back, in_vmem(wg), in_vmem(wu))


def tiles_of(sources, at_ref, first, tile):
    listed = []
    for n, source in enumerate(sources):
        for i in range(source.shape[0] // tile):
            index = at_ref[first + i] if n == 0 else i
            at = pl.ds(pl.multiple_of(index * tile, tile), tile) if n == 0 else pl.ds(i * tile, tile)
            listed.append((source, at))
    return listed


def hidden_back_kernel(tile, more, count, at_ref, *refs):
    sources, (wd_ref, hidden_ref, before) = refs[:count], refs[count : count + 3]
    out_ref, sum_ref, cot, total, sem = refs[-5:]
    step, block = pl.program_id(0), wd_ref.shape[0]
    copies = []
    for i, (source, at) in enumerate(tiles_of(sources, at_ref, 0, tile)):
        if i > 0:
            target = cot.at[pl.ds(i * tile, tile)]
            copies.append(pltpu.make_async_copy(source.at[at], target, sem.at[i]))
    rows = len(copies) * tile
    parts = -(-rows // 512)
    size = rows // parts

    def every_tile(waits):
        wd = wd_ref[...]
        own = dot(hidden_ref[...], wd)
        done = 0
        for i in range(parts):
            while waits and done * tile < (i + 1) * size:
                copies[done].wait()
                done += 1
            at = pl.ds(tile + i * size, size)
            out_ref[at, :] = dot_nt(cot[at, :], wd).astype(BF)
        return own

    @pl.when(step == 0)
    def _():
        for copy in copies:
            copy.start()
        own = every_tile(True)
        total[...] = own + before[...] if more else own

    @pl.when(step > 0)
    def _():
        total[...] += every_tile(False)

    @pl.when(step == pl.num_programs(0) - 1)
    def _():
        sum_ref[...] = total[...].astype(sum_ref.dtype)


def hidden_back_of(turns, cots, wd, hidden, part, before=()):
    width = cots[0].shape[1]
    rows, units = sum(cot.shape[0] for cot in cots), wd.shape[0]
    tiles = rows // hidden.shape[0]
    block = min(512, units // 2)
    steps = units // 2 // block
    skip = part * steps
    tile = hidden.shape[0]
    whole = pl.BlockSpec((tile, width), lambda i: (0, 0), pipeline_mode=pl.Buffered(1))
    return pl.pallas_call(
        functools.partial(hidden_back_kernel, tile, len(before) > 0, len(cots)),
        grid=(steps,),
        in_specs=[pl.BlockSpec(memory_space=pltpu.SMEM)] + [HBM_WHOLE] * len(cots)
        + [pl.BlockSpec((block, width), lambda i: (i + skip, 0)),
           pl.BlockSpec((tile, block), lambda i: (0, i + skip))]
        + [whole, HBM_WHOLE][: len(before)],
        out_specs=[pl.BlockSpec((rows, block), lambda i: (0, i + skip)), whole],
        out_shape=[jax.ShapeDtypeStruct((rows, units), BF),
                   jax.ShapeDtypeStruct((tile, width), BF if part else F32)],
        scratch_shapes=[pltpu.VMEM((rows, width), BF), pltpu.VMEM((tile, width), F32),
                        pltpu.SemaphoreType.DMA((tiles,))],
        input_output_aliases={len(cots) + 4: 0} if before else {},
        compiler_params=pltpu.CompilerParams(vmem_limit_bytes=56 * MIB),
        cost_estimate=pl.CostEstimate(
            flops=rows * width * units, bytes_accessed=2 * width * (rows + units),
            transcendentals=0,
        ),
    )(turns, *[in_hbm(cot) for cot in cots], in_hbm(wd), hidden, *before)


def join_kernel(count, *refs):
    pieces, out_ref, sem = refs[:count], refs[count], refs[-1]
    size = pieces[0].shape[0]
    copies = [
        pltpu.make_async_copy(piece, out_ref.at[pl.ds(i * size, size)], sem.at[i])
        for i, piece in enumerate(pieces)
    ]
    for copy in copies:
        copy.start()
    for copy in copies:
        copy.wait()


def join(pieces):
    size, width = pieces[0].shape
    return pl.pallas_call(
        functools.partial(join_kernel, len(pieces)),
        in_specs=[HBM_WHOLE] * len(pieces),
        out_specs=pl.BlockSpec(memory_space=pl.ANY),
        out_shape=jax.ShapeDtypeStruct((size * len(pieces), width), BF),
        scratch_shapes=[pltpu.SemaphoreType.DMA((len(pieces),))],
        compiler_params=pltpu.CompilerParams(vmem_limit_bytes=2 * MIB),
        cost_estimate=pl.CostEstimate(flops=0, bytes_accessed=0, transcendentals=0),
    )(*pieces)


def mlp_grad_kernel(count, chunk, parts, at_ref, *refs):
    pieces, cots, refs = refs[:count], refs[count : count + parts], refs[count + parts :]
    (own_hid, own_gate, own_up, hb_ref, wg_ref, wu_ref, gg_ref, ug_ref, dg_ref, gain_ref,
     x_all, cb, hid, gbk, ubk, gain_sum, sem, cot_sem) = refs
    size = cb.shape[1]
    tile = pieces[0].shape[0]
    per = tile // chunk
    tiles = x_all.shape[0] // tile
    own = pl.ds(pl.multiple_of(at_ref[0] * size, size), size)

    @pl.when(pl.program_id(0) == 0)
    def _():
        copies = []
        for i in range(count * per):
            spot = pl.ds(pl.multiple_of(at_ref[1 + i] * chunk, chunk), chunk)
            part = pieces[i // per].at[pl.ds(i % per * chunk, chunk)]
            copies.append(pltpu.make_async_copy(part, x_all.at[spot], sem.at[i]))
        base = 1 + count * per
        for i in range(per):
            spot = pl.ds(pl.multiple_of(at_ref[base + i] * chunk, chunk), chunk)
            target = cb.at[pl.ds(i * chunk, chunk)]
            copies.append(pltpu.make_async_copy(cots[0].at[spot, own], target, cot_sem.at[i]))
        for i, (source, spot) in enumerate(tiles_of(cots, at_ref, base + per, tile)):
            if i > 0:
                target = cb.at[pl.ds(i * tile, tile)]
                copies.append(
                    pltpu.make_async_copy(source.at[spot, own], target, cot_sem.at[per + i])
                )
        for copy in copies:
            copy.start()
        for copy in copies:
            copy.wait()

    hid[:tile, :], gbk[:tile, :], ubk[:tile, :] = own_hid[...], own_gate[...], own_up[...]
    wg, wu = wg_ref[...], wu_ref[...]
    for i in range(1, tiles):
        at = pl.ds(i * tile, tile)
        x = x_all[at, :]
        hid[at, :], gbk[at, :], ubk[at, :] = gate_math(
            dot(x, wg), dot(x, wu), hb_ref[at, :].astype(F32)
        )
    xb = x_all[:, own]
    gate_grad = dot_tn(xb, gbk[...])
    up_grad = dot_tn(xb, ubk[...])
    gg_ref[...] = gate_grad
    ug_ref[...] = up_grad
    dg_ref[...] = dot_tn(hid[...], cb[...])
    gain = jnp.sum(
        wg_ref[own, :].astype(F32) * gate_grad + wu_ref[own, :].astype(F32) * up_grad,
        axis=1, keepdims=True,
    )

    @pl.when(pl.program_id(0) == 0)
    def _():
        gain_sum[...] = gain

    @pl.when(pl.program_id(0) > 0)
    def _():
        gain_sum[...] += gain

    @pl.when(pl.program_id(0) == pl.num_programs(0) - 1)
    def _():
        gain_ref[...] = jnp.broadcast_to(gain_sum[...], (size, HD)).T[:1, :]


def mlp_grad(places, chunk, pieces, own, cots, hb, wg, wu, size):
    tile, width = pieces[0].shape
    rows, units = hb.shape
    block = min(256, units)
    wspec = pl.BlockSpec((width, block), lambda i, at: (0, i))
    ospec = pl.BlockSpec((tile, block), lambda i, at: (0, i))
    grid_spec = pltpu.PrefetchScalarGridSpec(
        num_scalar_prefetch=1,
        grid=(units // block,),
        in_specs=[HBM_WHOLE] * (len(pieces) + len(cots)) + [ospec] * 3
        + [pl.BlockSpec((rows, block), lambda i, at: (0, i)), wspec, wspec],
        out_specs=[pl.BlockSpec((size, block), lambda i, at: (0, i))] * 2
        + [pl.BlockSpec((block, size), lambda i, at: (i, 0)),
           pl.BlockSpec((1, size), lambda i, at: (0, 0))],
        scratch_shapes=[pltpu.VMEM((rows, width), BF), pltpu.VMEM((rows, size), BF)]
        + [pltpu.VMEM((rows, block), BF)] * 3
        + [pltpu.VMEM((size, 1), F32), pltpu.SemaphoreType.DMA((rows // chunk,)),
           pltpu.SemaphoreType.DMA((tile // chunk + rows // tile,))],
    )
    return pl.pallas_call(
        functools.partial(mlp_grad_kernel, len(pieces), chunk, len(cots)),
        grid_spec=grid_spec,
        out_shape=[jax.ShapeDtypeStruct((size, units), F32)] * 2
        + [jax.ShapeDtypeStruct((units, size), F32), jax.ShapeDtypeStruct((1, size), F32)],
        compiler_params=pltpu.CompilerParams(vmem_limit_bytes=56 * MIB),
        cost_estimate=pl.CostEstimate(
            flops=2 * rows * units * (2 * width + 3 * size),
            bytes_accessed=4 * width * units + 4 * rows * width,
            transcendentals=0,
        ),
    )(
        places, *pieces, *[in_hbm(cot) for cot in cots], *[in_hbm(rows) for rows in own],
        in_hbm(hb), in_hbm(wg), in_hbm(wu),
    )


def row_mean(values):
    return jnp.mean(values, axis=-1, keepdims=True)


def norm_parts(values):
    root = lax.rsqrt(row_mean(values * values) + EPS)
    return values * root, root


def norm_back(upstream, scaled, root, gain):
    inner = upstream * gain
    return root * (inner - scaled * row_mean(inner * scaled))


def per_device(
    activations, cotangent, doc_ids, attn_gain, query_weight, key_weight, value_weight,
    out_weight, mlp_gain, gate_weight, up_weight, down_weight,
):
    rows, width = activations.shape[1:]
    n_dp, n_ctx, n_t = lax.axis_size("dp"), lax.axis_size("ctx"), lax.axis_size("tensor")
    dp, ctx, place = lax.axis_index("dp"), lax.axis_index("ctx"), lax.axis_index("tensor")
    chunk = rows // n_t
    length = rows * n_ctx
    slots = slot_order(n_t)
    scale, shift = HD ** (-0.5), -math.log(length)
    gain_first, gain_second = attn_gain.astype(F32), mlp_gain.astype(F32)

    slot_places = jnp.stack([place ^ slot for slot in slots])
    normed_first, mine, cot, cot_mine, inputs_mine, scaled_mine, root_mine = arrange(
        slot_places, activations[0], cotangent[0], attn_gain
    )

    bits = list(reversed(bits_of(n_t)))

    def spread(rings, beside=()):
        lists = [[ring] for ring in rings]
        for bit in bits:
            lists = [items + [swap(item, "tensor", bit) for item in items] for items in lists]
            if bit == bits[0]:
                lists = after(lists, beside)
        return lists

    rings = ring_of(mine)[1:]
    cot_own = lax.all_gather(cot_mine, ("ctx", "tensor"), axis=0, tiled=True)

    ring_at = ctx ^ jnp.arange(n_ctx, dtype=jnp.int32)
    seq_places = jnp.concatenate([
        ring_at[k : k + 1] * n_t + (place ^ slot) for k in range(n_ctx) for slot in slots
    ])
    docs = doc_ids
    out_cols = width // (n_dp * n_ctx)
    owners = jnp.stack([((dp + step) % n_dp) * n_ctx + ctx for step in range(n_dp)])
    starts = owners * out_cols
    owner = owners[0]
    half = place & 1
    places = [owner[None]]
    for flip in (0, 1):
        for step in range(n_dp):
            for index in range(n_t // 2):
                if step == 0:
                    group = jnp.arange(n_ctx, dtype=jnp.int32)
                else:
                    other_half = ring_at // (n_ctx // 2) != half
                    group = step * n_ctx + other_half * (n_ctx // 2) + ring_at % (n_ctx // 2)
                inside = place ^ slots[index] ^ flip
                if step == 0:
                    inside = jnp.where(group == 0, index + flip * (n_t // 2), inside)
                places.append(group * n_t + inside)
    places = jnp.concatenate(places + [ctx * n_t + slot_places, ring_at])
    frequency = np.float32(10000.0) ** (
        -np.arange(HD // 2, dtype=np.float32) * np.float32(2.0) / np.float32(HD)
    )
    angles = np.arange(length, dtype=np.float32)[:, None] * frequency[None, :]
    cos = jnp.asarray(np.concatenate([np.cos(angles), np.cos(angles)], axis=1))
    sin = jnp.asarray(np.concatenate([-np.sin(angles), np.sin(angles)], axis=1))
    rings = [after(ring, seq_places, starts, places) for ring in rings]
    hidden_back = lax.dot_general(
        after(cot, rings), down_weight, (((1,), (1,)), ((), ())), preferred_element_type=F32
    ).astype(BF)
    seq_pieces = spread(rings, hidden_back)
    own_pieces = [normed_first[i * chunk : (i + 1) * chunk] for i in range(n_t)]
    q, k, v, attended, mass, x_seq = attend(
        seq_places, own_pieces + sum(seq_pieces, []), docs, cos, sin,
        query_weight, key_weight, value_weight, n_t, scale, shift,
    )
    attn_mass = from_slots(mass[:, :, 0].T, slots, place)

    def over_dp(items):
        return [turn(item, "dp", step) for step in range(1, n_dp) for item in items]

    def over_tensor(items, bits):
        for bit in bits:
            items = items + [swap(item, "tensor", bit) for item in items]
        return items

    branch = scatter_tensor(
        jnp.dot(attended, out_weight, preferred_element_type=F32).astype(BF), attn_mass
    )
    middle = inputs_mine + branch
    scaled_second, root_second = norm_parts(middle)
    normed_chunk = (scaled_second * gain_second).astype(BF)
    cot_own = after(cot_own, normed_chunk)
    size = length // 2
    cot_half = lax.dynamic_slice_in_dim(cot_own, half * size, size, 0)
    cot_far = [turn(cot_half, "dp", step) for step in range(1, n_dp)]
    gate, up = fetch(after(gate_weight, normed_chunk), up_weight)
    normed_second = gather_tensor(normed_chunk, (gate, up))
    chunk_rings = ring_of(normed_chunk)
    hidden, gate_back, up_back, second_part = mlp(normed_second, hidden_back, gate, up)
    second_part, chunk_rings = lax.optimization_barrier((second_part, chunk_rings))
    x_near = [join(chunk_rings)]
    x_far = over_dp(x_near)
    x_near_more = over_tensor(x_near, bits[:-1])[1:]
    second_back = scatter_tensor(second_part)
    middle_back = cot_mine.astype(F32) + norm_back(
        second_back, scaled_second, root_second, gain_second
    )
    branch_back = middle_back.astype(BF)
    bb_rings = ring_of(branch_back)
    cots = [cot_own] + sum([[far, swap(far, "tensor", 1)] for far in cot_far], [])
    cots = after(cots, branch_back)
    hidden_back_all, mlp_part = hidden_back_of(ring_at, cots, down_weight, hidden, 0)
    bb_rings, x_far, x_near_more = after((bb_rings, x_far, x_near_more), hidden_back_all)
    hidden_back_all, mlp_part = hidden_back_of(
        ring_at, after(cots, bb_rings), down_weight, hidden, 1, (mlp_part, hidden_back_all)
    )
    bb_pieces = spread(bb_rings, mlp_part)
    x_far_more = over_tensor(x_far, bits[:-1])[len(x_far) :]

    mine_grads, theirs_grads, kept_half, given_half = attend_back(
        seq_places, starts, sum(bb_pieces, []), out_weight, q, k, v, cos, sin, docs, mlp_part,
        x_seq, query_weight, key_weight, value_weight, out_cols, n_t, scale, shift,
    )

    theirs = [turn(theirs_grads[step - 1], "dp", step) for step in range(1, n_dp)]

    x_pieces = over_tensor(x_near + x_near_more + x_far + x_far_more, bits[-1:])

    gate_grad, up_grad, down_grad, mlp_gain_sum = mlp_grad(
        after(places, kept_half), chunk, x_pieces, (hidden, gate_back, up_back), cots,
        hidden_back_all, gate_weight, up_weight, out_cols,
    )
    mlp_gain_sum = mlp_gain_sum[0]
    theirs = after(theirs, gate_grad)
    both = scatter_tensor((kept_half, given_half), gate_grad)
    first_back, mlp_out = both[:, :width], both[:, width:]
    input_grad = (
        middle_back + norm_back(first_back, scaled_mine, root_mine, gain_first)
    ).astype(BF)
    layer_out = (middle + mlp_out).astype(BF)
    results = gather_tensor(jnp.concatenate([layer_out, input_grad], axis=1))
    results = from_slots(results, slots, place)
    layer_out, input_grad = results[:, :width], results[:, width:]
    attn_grads = mine_grads + sum(part.astype(F32) for part in theirs)
    query_grad, key_grad, value_grad = attn_grads[0], attn_grads[1], attn_grads[2]
    out_grad = attn_grads[3].T

    def rows_of(weight):
        return lax.dynamic_slice_in_dim(weight, owner * out_cols, out_cols, 0).astype(F32)

    attn_gain_sum = jnp.sum(
        rows_of(query_weight) * query_grad + rows_of(key_weight) * key_grad
        + rows_of(value_weight) * value_grad, axis=1,
    )
    gains = jnp.stack([attn_gain_sum, mlp_gain_sum])
    for bit in bits:
        gains = gains + swap(gains, "tensor", bit)
    gain_grads = gains / lax.dynamic_slice_in_dim(
        jnp.stack([gain_first, gain_second]), owner * out_cols, out_cols, 1
    )

    return (
        layer_out[None], input_grad[None], gain_grads[0], query_grad, key_grad, value_grad,
        out_grad, gain_grads[1], gate_grad, up_grad, down_grad, attn_mass[None],
    )


def solution(mesh):
    return jax.shard_map(
        per_device,
        mesh=mesh,
        in_specs=(
            P("dp", "ctx", None),
            P("dp", "ctx", None),
            P("dp", None),
            P(),
            P(None, "tensor"),
            P(None, "tensor"),
            P(None, "tensor"),
            P("tensor", None),
            P(),
            P(None, "tensor"),
            P(None, "tensor"),
            P("tensor", None),
        ),
        out_specs=(
            P("dp", "ctx", None),
            P("dp", "ctx", None),
            P(("dp", "ctx")),
            P(("dp", "ctx"), "tensor"),
            P(("dp", "ctx"), "tensor"),
            P(("dp", "ctx"), "tensor"),
            P("tensor", ("dp", "ctx")),
            P(("dp", "ctx")),
            P(("dp", "ctx"), "tensor"),
            P(("dp", "ctx"), "tensor"),
            P("tensor", ("dp", "ctx")),
            P("dp", "ctx", "tensor"),
        ),
        check_vma=False,
    )
```

```python
import functools
import math

import jax
import jax.numpy as jnp
import numpy as np
from jax import lax
from jax.experimental import pallas as pl
from jax.experimental.pallas import tpu as pltpu
from jax.sharding import PartitionSpec as P

HD = 128
EPS = 1e-05
BF = jnp.bfloat16
F32 = jnp.float32
MIB = 1024 * 1024


def swap(values, axis, distance):
    count = lax.axis_size(axis)
    return lax.ppermute(values, axis, [(i, i ^ distance) for i in range(count)])


def turn(values, axis, shift):
    count = lax.axis_size(axis)
    return lax.ppermute(values, axis, [(i, (i + shift) % count) for i in range(count)])


def after(value, *others):
    return lax.optimization_barrier((value, others))[0]


def in_hbm(values):
    return pltpu.with_memory_space_constraint(values, pltpu.HBM)


def in_vmem(values):
    return pltpu.with_memory_space_constraint(values, pltpu.VMEM)


def bits_of(count):
    return [1 << i for i in range(count.bit_length() - 1)]


def slot_order(count):
    order = [0]
    for bit in reversed(bits_of(count)):
        order = order + [slot ^ bit for slot in order]
    return order


def gather_tensor(rows, beside=()):
    for bit in reversed(bits_of(lax.axis_size("tensor"))):
        got = after(swap(rows, "tensor", bit), beside)
        rows, beside = jnp.concatenate([rows, got], axis=0), ()
    return rows


def scatter_tensor(rows, beside=()):
    bits = bits_of(lax.axis_size("tensor"))
    for bit in bits:
        if not isinstance(rows, tuple):
            half = rows.shape[0] // 2
            rows = rows[:half], rows[half:]
        got = swap(rows[1].astype(BF), "tensor", bit)
        if bit == bits[-1]:
            got = after(got, beside)
        rows = rows[0].astype(F32) + got.astype(F32)
    return rows


def ring_of(rows):
    return [rows] + [swap(rows, "ctx", k) for k in range(1, lax.axis_size("ctx"))]


def from_slots(blocks, slots, place):
    size = blocks.shape[0] // len(slots)
    out = jnp.zeros_like(blocks)
    for index, slot in enumerate(slots):
        out = lax.dynamic_update_slice_in_dim(
            out, blocks[index * size : (index + 1) * size], (place ^ slot) * size, 0
        )
    return out


def rope_rows(u, cos, sin):
    return u * cos + pltpu.roll(u, HD // 2, 1) * sin


def rope_back_rows(u, cos, sin):
    return u * cos - pltpu.roll(u, HD // 2, 1) * sin


def dot(a, b):
    return lax.dot_general(a, b, (((1,), (0,)), ((), ())), preferred_element_type=F32)


def dot_nt(a, b):
    return lax.dot_general(a, b, (((1,), (1,)), ((), ())), preferred_element_type=F32)


def dot_tn(a, b):
    return lax.dot_general(a, b, (((0,), (0,)), ((), ())), preferred_element_type=F32)


def place_rows(step, pieces, places, rows, sem, start=True, wait=True):
    @pl.when(step == 0)
    def _():
        copies = []
        for i, (piece, place) in enumerate(zip(pieces, places, strict=True)):
            copies.append(pltpu.make_async_copy(piece, rows.at[place], sem.at[i]))
        if start:
            for copy in copies:
                copy.start()
        if wait:
            for copy in copies:
                copy.wait()


def chunk_places(at_ref, first, count, chunk):
    return [
        pl.ds(pl.multiple_of(at_ref[first + i] * chunk, chunk), chunk) for i in range(count)
    ]


NEVER = -1e30
VMEM_WHOLE = pl.BlockSpec(memory_space=pltpu.VMEM)
HBM_WHOLE = pl.BlockSpec(memory_space=pl.ANY)


def fetch_kernel(count, *refs):
    sources, targets, sem = refs[:count], refs[count : 2 * count], refs[-1]
    copies = [
        pltpu.make_async_copy(source, target, sem.at[i])
        for i, (source, target) in enumerate(zip(sources, targets, strict=True))
    ]
    for copy in copies:
        copy.start()
    for copy in copies:
        copy.wait()


def fetch(*weights):
    return pl.pallas_call(
        functools.partial(fetch_kernel, len(weights)),
        in_specs=[HBM_WHOLE] * len(weights),
        out_specs=[VMEM_WHOLE] * len(weights),
        out_shape=[pltpu.VMEM(weight.shape, weight.dtype) for weight in weights],
        scratch_shapes=[pltpu.SemaphoreType.DMA((len(weights),))],
        compiler_params=pltpu.CompilerParams(vmem_limit_bytes=2 * MIB),
        cost_estimate=pl.CostEstimate(
            flops=0, bytes_accessed=0, transcendentals=0
        ),
    )(*[in_hbm(weight) for weight in weights])


def arrange_kernel(
    at_ref, rows_hbm, cot_hbm, gain_ref, normed_ref, mine_ref, cots_ref, cot_mine_ref,
    inputs_ref, scaled_ref, root_ref, rows_in, gain_in, rows_sem, cot_sem, gain_sem,
):
    chunk = mine_ref.shape[0]
    gain_copy = pltpu.make_async_copy(gain_ref, gain_in, gain_sem)
    gain_copy.start()
    spots = chunk_places(at_ref, 0, normed_ref.shape[0] // chunk, chunk)
    parts = [slice(i * chunk, (i + 1) * chunk) for i in range(len(spots))]
    copies = []
    for i, (spot, part) in enumerate(zip(spots, parts, strict=True)):
        copies.append((
            pltpu.make_async_copy(rows_hbm.at[spot], rows_in.at[part], rows_sem.at[i]),
            pltpu.make_async_copy(cot_hbm.at[spot], cots_ref.at[part], cot_sem.at[i]),
        ))
    for pair in copies:
        for copy in pair:
            copy.start()
    gain_copy.wait()
    gain = gain_in[...].astype(F32).reshape(1, -1)
    for i, (part, pair) in enumerate(zip(parts, copies, strict=True)):
        pair[0].wait()
        rows = rows_in[part, :].astype(F32)
        root = lax.rsqrt(jnp.mean(rows * rows, axis=-1, keepdims=True) + EPS)
        normed = (rows * root * gain).astype(BF)
        normed_ref[part, :] = normed
        pair[1].wait()
        if i == 0:
            mine_ref[...] = normed
            cot_mine_ref[...] = cots_ref[part, :]
            inputs_ref[...] = rows
            scaled_ref[...] = rows * root
            root_ref[...] = jnp.broadcast_to(root, root_ref.shape)


def arrange(places, rows, cot, gain):
    count, width = rows.shape
    slots = places.shape[0]
    chunk = count // slots
    shapes = [(count, width), (chunk, width)] * 2
    more = [(chunk, width)] * 3
    return pl.pallas_call(
        arrange_kernel,
        in_specs=[pl.BlockSpec(memory_space=pltpu.SMEM), HBM_WHOLE, HBM_WHOLE, HBM_WHOLE],
        out_specs=[VMEM_WHOLE] * 7,
        out_shape=[jax.ShapeDtypeStruct(shape, BF) for shape in shapes]
        + [jax.ShapeDtypeStruct(shape, F32) for shape in more],
        scratch_shapes=[pltpu.VMEM((count, width), BF), pltpu.VMEM(gain.shape, BF),
                        pltpu.SemaphoreType.DMA((slots,)), pltpu.SemaphoreType.DMA((slots,)),
                        pltpu.SemaphoreType.DMA],
        compiler_params=pltpu.CompilerParams(vmem_limit_bytes=16 * MIB),
        cost_estimate=pl.CostEstimate(
            flops=8 * count * width, bytes_accessed=8 * count * width, transcendentals=0
        ),
    )(places, in_hbm(rows), in_hbm(cot), in_hbm(gain))


def column_of(row):
    return jnp.broadcast_to(row, (HD, row.shape[1])).T[:, :1]


def attend_kernel(chunk, slots, scale, shift, at_ref, *refs):
    count = len(refs) - 16
    pieces = refs[:count]
    (doc_ref, cos_ref, sin_ref, wq_ref, wk_ref, wv_ref, q_ref, k_ref, v_ref, att_ref, mass_ref,
     seq_hbm, x, doc_column, sem, out_sem) = refs[count:]
    step, last = pl.program_id(0), pl.num_programs(0) - 1
    place_rows(step, pieces, chunk_places(at_ref, 0, count, chunk), x, sem)
    keep = pltpu.make_async_copy(x, seq_hbm, out_sem)

    @pl.when(step == 0)
    def _():
        keep.start()

    cos, sin = cos_ref[...], sin_ref[...]
    own = chunk_places(at_ref, 0, slots, chunk)
    doc_column[...] = column_of(doc_ref[...])
    shape = (chunk, doc_ref.shape[1])
    bias = []
    for i, spot in enumerate(own):
        own_spots = lax.broadcasted_iota(jnp.int32, shape, 0) + at_ref[i] * chunk
        allowed = (lax.broadcasted_iota(jnp.int32, shape, 1) <= own_spots) & (
            doc_column[spot, :] == doc_ref[...]
        )
        bias.append(jnp.where(allowed, shift, NEVER))
    bias = jnp.concatenate(bias, axis=0)
    rows = x[...]
    q_all = dot(rows, wq_ref[...])
    k_all = dot(rows, wk_ref[...])
    v_all = dot(rows, wv_ref[...]).astype(BF)
    v_ref[...] = v_all
    for j in range(q_all.shape[1] // HD):
        cols = slice(j * HD, (j + 1) * HD)
        q_ref[:, cols] = rope_rows(q_all[:, cols], cos, sin).astype(BF)
        k = rope_rows(k_all[:, cols], cos, sin).astype(BF)
        k_ref[:, cols] = k
        q = jnp.concatenate([q_ref[spot, cols] for spot in own], axis=0)
        weights = jax.nn.sigmoid(dot_nt(q, k) * scale + bias)
        mass_ref[j] = jnp.sum(weights, axis=-1, keepdims=True)
        att_ref[:, cols] = dot(weights.astype(BF), v_all[:, cols]).astype(BF)

    @pl.when(step == last)
    def _():
        keep.wait()


def attend(places, pieces, docs, cos, sin, wq, wk, wv, slots, scale, shift):
    chunk, width = pieces[0].shape
    seq, rows = chunk * len(pieces), chunk * slots
    cols = wq.shape[1]
    heads = cols // HD
    step = min(2, heads)
    whole = lambda *shape: pl.BlockSpec(
        shape, lambda i: (0,) * len(shape), pipeline_mode=pl.Buffered(1)
    )
    hbm = pl.BlockSpec(memory_space=pl.ANY)
    wspec = pl.BlockSpec((width, step * HD), lambda i: (0, i))
    sspec = pl.BlockSpec((seq, step * HD), lambda i: (0, i))
    return pl.pallas_call(
        functools.partial(attend_kernel, chunk, slots, scale, shift),
        grid=(heads // step,),
        in_specs=[pl.BlockSpec(memory_space=pltpu.SMEM)] + [hbm] * len(pieces)
        + [whole(1, seq), whole(seq, HD), whole(seq, HD)]
        + [wspec] * 3,
        out_specs=[sspec, sspec, sspec,
                   pl.BlockSpec((rows, step * HD), lambda i: (0, i)),
                   pl.BlockSpec((step, rows, 1), lambda i: (i, 0, 0)),
                   pl.BlockSpec(memory_space=pltpu.HBM)],
        out_shape=[jax.ShapeDtypeStruct((seq, cols), BF)] * 3
        + [jax.ShapeDtypeStruct((rows, cols), BF), jax.ShapeDtypeStruct((heads, rows, 1), F32),
           jax.ShapeDtypeStruct((seq, width), BF)],
        scratch_shapes=[pltpu.VMEM((seq, width), BF), pltpu.VMEM((seq, 1), jnp.int32),
                        pltpu.SemaphoreType.DMA((len(pieces),)), pltpu.SemaphoreType.DMA],
        compiler_params=pltpu.CompilerParams(vmem_limit_bytes=56 * MIB),
        cost_estimate=pl.CostEstimate(
            flops=2 * seq * width * cols * 3, bytes_accessed=6 * width * cols, transcendentals=0
        ),
    )(places, *pieces, docs, cos, sin, wq, wk, wv)


def attend_back_kernel(chunk, slots, scale, shift, at_ref, starts_ref, *refs):
    count = len(refs) - 24
    pieces = refs[:count]
    (wo_ref, q_ref, k_ref, v_ref, cos_ref, sin_ref, doc_row_ref, more_ref,
     x_hbm, wq_hbm, wk_hbm, wv_hbm, mine_ref, theirs_ref, first_ref, give_ref,
     bb, x_cols, w_cols, acc, every, bb_sem, x_sem, w_sem) = refs[count:]
    step = pl.program_id(0)
    owners = x_cols.shape[0]
    spots = chunk_places(at_ref, 0, count, chunk)
    place_rows(step, pieces, spots, bb, bb_sem, wait=False)
    seq, size, width = bb.shape[0], x_cols.shape[2], w_cols.shape[2]
    starts = [pl.multiple_of(starts_ref[i], HD) for i in range(owners)]
    at = pl.ds(pl.multiple_of(step * width, HD), width)
    copies = [
        pltpu.make_async_copy(x_hbm.at[:, pl.ds(starts[i], size)], x_cols.at[i], x_sem.at[i])
        for i in range(owners)
    ] + [
        pltpu.make_async_copy(w_hbm.at[:, at], w_cols.at[i], w_sem.at[i])
        for i, w_hbm in enumerate((wq_hbm, wk_hbm, wv_hbm))
    ]
    for copy in copies:
        copy.start()

    block = min(256, seq)
    parts = [slice(i * block, (i + 1) * block) for i in range(seq // block)]
    heads = [slice(j * HD, (j + 1) * HD) for j in range(width // HD)]
    weights, attended = {}, []
    doc_column = column_of(doc_row_ref[...])
    for i, part in enumerate(parts):
        shape = (block, part.stop)
        allowed = (
            lax.broadcasted_iota(jnp.int32, shape, 1)
            <= lax.broadcasted_iota(jnp.int32, shape, 0) + part.start
        ) & (doc_column[part, :] == doc_row_ref[:, : part.stop])
        bias = jnp.where(allowed, shift, NEVER)
        row = []
        for j, cols in enumerate(heads):
            scores = dot_nt(q_ref[part, cols], k_ref[: part.stop, cols]) * scale + bias
            weights[i, j] = jax.nn.sigmoid(scores)
            row.append(dot(weights[i, j].astype(BF), v_ref[: part.stop, cols]).astype(BF))
        attended.append(jnp.concatenate(row, axis=1))
    attended = jnp.concatenate(attended, axis=0)

    place_rows(step, pieces, spots, bb, bb_sem, start=False)
    ab_all = dot_nt(bb[...], wo_ref[...]).astype(BF)
    for j, cols in enumerate(heads):
        key_sums, value_sums = [None] * len(parts), [None] * len(parts)
        for i, part in enumerate(parts):
            ab, weight = ab_all[part, cols], weights[i, j]
            slope = weight - weight * weight
            back = (dot_nt(ab, v_ref[: part.stop, cols]) * slope).astype(BF)
            weight = weight.astype(BF)
            query_back = dot(back, k_ref[: part.stop, cols]) * scale
            every[part, cols] = rope_back_rows(
                query_back, cos_ref[part, :], sin_ref[part, :]
            ).astype(BF)
            for n in range(i + 1):
                key_part = dot_tn(back[:, parts[n]], q_ref[part, cols])
                value_part = dot_tn(weight[:, parts[n]], ab)
                key_sums[n] = key_part if i == n else key_sums[n] + key_part
                value_sums[n] = value_part if i == n else value_sums[n] + value_part
        for n, part in enumerate(parts):
            at_key = slice(width + cols.start, width + cols.stop)
            at_value = slice(2 * width + cols.start, 2 * width + cols.stop)
            every[part, at_key] = rope_back_rows(
                key_sums[n] * scale, cos_ref[part, :], sin_ref[part, :]
            ).astype(BF)
            every[part, at_value] = value_sums[n].astype(BF)

    def give(i, n, part):
        if i == 0:
            mine_ref[n] = part
        else:
            theirs_ref[i - 1, n] = part.astype(BF)

    for i in range(owners):
        give(i, 3, dot_tn(bb[:, pl.ds(starts[i], size)], attended))

    for copy in copies:
        copy.wait()
    for i in range(owners):
        total = dot_tn(x_cols[i], every[...])
        for n in range(3):
            give(i, n, total[:, n * width : (n + 1) * width])
    own = jnp.concatenate([every[spot, :] for spot in spots[:slots]], axis=0)
    first = sum(dot_nt(own[:, n * width : (n + 1) * width], w_cols[n]) for n in range(3))

    @pl.when(step == 0)
    def _():
        acc[...] = first

    @pl.when(step > 0)
    def _():
        acc[...] += first

    @pl.when(step == pl.num_programs(0) - 1)
    def _():
        total, half = acc[...].astype(BF), acc.shape[0] // 2
        for n, at in enumerate((slice(0, half), slice(half, 2 * half))):
            keep_ref = first_ref if n == 0 else give_ref
            keep_ref[:, : acc.shape[1]] = total[at]
            keep_ref[:, acc.shape[1] :] = more_ref[at, :]


def attend_back(
    places, starts, pieces, wo, q, k, v, cos, sin, docs, more, x_seq, wq, wk, wv,
    size, slots, scale, shift,
):
    seq, width = x_seq.shape
    chunk = pieces[0].shape[0]
    cols = wo.shape[0]
    heads = cols // HD
    step = min(2, heads)
    own = slots * chunk
    owners = starts.shape[0]
    whole = lambda *shape: pl.BlockSpec(
        shape, lambda i: (0,) * len(shape), pipeline_mode=pl.Buffered(1)
    )
    sspec = pl.BlockSpec((seq, step * HD), lambda i: (0, i))
    hbm = pl.BlockSpec(memory_space=pl.ANY)
    return pl.pallas_call(
        functools.partial(attend_back_kernel, chunk, slots, scale, shift),
        grid=(heads // step,),
        in_specs=[pl.BlockSpec(memory_space=pltpu.SMEM)] * 2 + [hbm] * len(pieces)
        + [pl.BlockSpec((step * HD, width), lambda i: (i, 0)),
           sspec, sspec, sspec, whole(seq, HD), whole(seq, HD), whole(1, seq), whole(*more.shape)]
        + [hbm] * 4,
        out_specs=[pl.BlockSpec((4, size, step * HD), lambda i: (0, 0, i)),
                   pl.BlockSpec((owners - 1, 4, size, step * HD), lambda i: (0, 0, 0, i)),
                   whole(own // 2, 2 * width), whole(own // 2, 2 * width)],
        out_shape=[jax.ShapeDtypeStruct((4, size, cols), F32),
                   jax.ShapeDtypeStruct((owners - 1, 4, size, cols), BF),
                   jax.ShapeDtypeStruct((own // 2, 2 * width), BF),
                   jax.ShapeDtypeStruct((own // 2, 2 * width), BF)],
        scratch_shapes=[pltpu.VMEM((seq, width), BF), pltpu.VMEM((owners, seq, size), BF),
                        pltpu.VMEM((3, width, step * HD), BF),
                        pltpu.VMEM((own, width), F32),
                        pltpu.VMEM((seq, 3 * step * HD), BF),
                        pltpu.SemaphoreType.DMA((len(pieces),)),
                        pltpu.SemaphoreType.DMA((owners,)), pltpu.SemaphoreType.DMA((3,))],
        compiler_params=pltpu.CompilerParams(vmem_limit_bytes=56 * MIB),
        cost_estimate=pl.CostEstimate(
            flops=2 * seq * width * cols + 14 * seq * seq * cols,
            bytes_accessed=2 * (seq + cols) * width + 20 * seq * cols,
            transcendentals=seq * seq * heads,
        ),
    )(
        places, starts, *pieces, in_hbm(wo), q, k, v, cos, sin,
        docs, more, in_hbm(x_seq), in_hbm(wq), in_hbm(wk), in_hbm(wv),
    )


def gate_math(gate, up, hidden_back):
    sig = jax.nn.sigmoid(gate)
    act = gate * sig
    hidden = (act * up).astype(BF)
    gate_back = (hidden_back * up * sig * (1.0 + gate * (1.0 - sig))).astype(BF)
    up_back = (hidden_back * act).astype(BF)
    return hidden, gate_back, up_back


def mlp_kernel(
    block, x_ref, hb_ref, wg_ref, wu_ref, hidden_ref, gate_ref, up_ref, back_ref
):
    x, total = x_ref[...], None
    for i in range(wg_ref.shape[1] // block):
        at = slice(i * block, (i + 1) * block)
        wg, wu = wg_ref[:, at], wu_ref[:, at]
        hidden_ref[:, at], gate_back, up_back = gate_math(
            dot(x, wg), dot(x, wu), hb_ref[:, at].astype(F32)
        )
        gate_ref[:, at] = gate_back
        up_ref[:, at] = up_back
        back = dot_nt(gate_back, wg) + dot_nt(up_back, wu)
        total = back if total is None else total + back
    back_ref[...] = total.astype(BF)


def mlp(x, hidden_back, wg, wu):
    rows, width = x.shape
    units = wg.shape[1]
    return pl.pallas_call(
        functools.partial(mlp_kernel, min(512, units)),
        in_specs=[VMEM_WHOLE] * 4,
        out_specs=[VMEM_WHOLE] * 4,
        out_shape=[
            *[jax.ShapeDtypeStruct((rows, units), BF)] * 3, jax.ShapeDtypeStruct((rows, width), BF)
        ],
        compiler_params=pltpu.CompilerParams(vmem_limit_bytes=20 * MIB),
        cost_estimate=pl.CostEstimate(
            flops=0, bytes_accessed=0, transcendentals=0
        ),
    )(x, hidden_back, in_vmem(wg), in_vmem(wu))


def tiles_of(sources, at_ref, first, tile):
    listed = []
    for n, source in enumerate(sources):
        for i in range(source.shape[0] // tile):
            index = at_ref[first + i] if n == 0 else i
            at = pl.ds(pl.multiple_of(index * tile, tile), tile) if n == 0 else pl.ds(i * tile, tile)
            listed.append((source, at))
    return listed


def own_hidden_back_kernel(rows_ref, wd_ref, out_ref):
    out_ref[...] = dot_nt(rows_ref[...], wd_ref[...]).astype(BF)


def own_hidden_back(rows, wd):
    count, width = rows.shape
    units = wd.shape[0]
    block = min(512, units)
    return pl.pallas_call(
        own_hidden_back_kernel,
        grid=(units // block,),
        in_specs=[
            pl.BlockSpec((count, width), lambda i: (0, 0), pipeline_mode=pl.Buffered(1)),
            pl.BlockSpec((block, width), lambda i: (i, 0)),
        ],
        out_specs=pl.BlockSpec((count, block), lambda i: (0, i)),
        out_shape=jax.ShapeDtypeStruct((count, units), BF),
        compiler_params=pltpu.CompilerParams(vmem_limit_bytes=24 * MIB),
        cost_estimate=pl.CostEstimate(
            flops=2 * count * width * units, bytes_accessed=2 * width * units, transcendentals=0
        ),
    )(rows, in_hbm(wd))


def hidden_back_kernel(tile, more, count, at_ref, *refs):
    sources, (wd_ref, hidden_ref, before) = refs[:count], refs[count : count + 3]
    out_ref, sum_ref, cot, total, sem = refs[-5:]
    step, block = pl.program_id(0), wd_ref.shape[0]
    copies = []
    for i, (source, at) in enumerate(tiles_of(sources, at_ref, 0, tile)):
        if i > 0:
            target = cot.at[pl.ds(i * tile, tile)]
            copies.append(pltpu.make_async_copy(source.at[at], target, sem.at[i]))
    rows = len(copies) * tile
    parts = -(-rows // 512)
    size = rows // parts

    def every_tile(waits):
        wd = wd_ref[...]
        own = dot(hidden_ref[...], wd)
        done = 0
        for i in range(parts):
            while waits and done * tile < (i + 1) * size:
                copies[done].wait()
                done += 1
            at = pl.ds(tile + i * size, size)
            out_ref[at, :] = dot_nt(cot[at, :], wd).astype(BF)
        return own

    @pl.when(step == 0)
    def _():
        for copy in copies:
            copy.start()
        own = every_tile(True)
        total[...] = own + before[...] if more else own

    @pl.when(step > 0)
    def _():
        total[...] += every_tile(False)

    @pl.when(step == pl.num_programs(0) - 1)
    def _():
        sum_ref[...] = total[...].astype(sum_ref.dtype)


def hidden_back_of(turns, cots, wd, hidden, part, before=()):
    width = cots[0].shape[1]
    rows, units = sum(cot.shape[0] for cot in cots), wd.shape[0]
    tiles = rows // hidden.shape[0]
    block = min(512, units // 2)
    steps = units // 2 // block
    skip = part * steps
    tile = hidden.shape[0]
    whole = pl.BlockSpec((tile, width), lambda i: (0, 0), pipeline_mode=pl.Buffered(1))
    return pl.pallas_call(
        functools.partial(hidden_back_kernel, tile, len(before) > 0, len(cots)),
        grid=(steps,),
        in_specs=[pl.BlockSpec(memory_space=pltpu.SMEM)] + [HBM_WHOLE] * len(cots)
        + [pl.BlockSpec((block, width), lambda i: (i + skip, 0)),
           pl.BlockSpec((tile, block), lambda i: (0, i + skip))]
        + [whole, HBM_WHOLE][: len(before)],
        out_specs=[pl.BlockSpec((rows, block), lambda i: (0, i + skip)), whole],
        out_shape=[jax.ShapeDtypeStruct((rows, units), BF),
                   jax.ShapeDtypeStruct((tile, width), BF if part else F32)],
        scratch_shapes=[pltpu.VMEM((rows, width), BF), pltpu.VMEM((tile, width), F32),
                        pltpu.SemaphoreType.DMA((tiles,))],
        input_output_aliases={len(cots) + 4: 0} if before else {},
        compiler_params=pltpu.CompilerParams(vmem_limit_bytes=56 * MIB),
        cost_estimate=pl.CostEstimate(
            flops=rows * width * units, bytes_accessed=2 * width * (rows + units),
            transcendentals=0,
        ),
    )(turns, *[in_hbm(cot) for cot in cots], in_hbm(wd), hidden, *before)


def join_kernel(count, *refs):
    pieces, out_ref, sem = refs[:count], refs[count], refs[-1]
    size = pieces[0].shape[0]
    copies = [
        pltpu.make_async_copy(piece, out_ref.at[pl.ds(i * size, size)], sem.at[i])
        for i, piece in enumerate(pieces)
    ]
    for copy in copies:
        copy.start()
    for copy in copies:
        copy.wait()


def join(pieces):
    size, width = pieces[0].shape
    return pl.pallas_call(
        functools.partial(join_kernel, len(pieces)),
        in_specs=[HBM_WHOLE] * len(pieces),
        out_specs=pl.BlockSpec(memory_space=pl.ANY),
        out_shape=jax.ShapeDtypeStruct((size * len(pieces), width), BF),
        scratch_shapes=[pltpu.SemaphoreType.DMA((len(pieces),))],
        compiler_params=pltpu.CompilerParams(vmem_limit_bytes=2 * MIB),
        cost_estimate=pl.CostEstimate(flops=0, bytes_accessed=0, transcendentals=0),
    )(*pieces)


def mlp_grad_kernel(count, chunk, parts, at_ref, *refs):
    pieces, cots, refs = refs[:count], refs[count : count + parts], refs[count + parts :]
    (own_hid, own_gate, own_up, hb_ref, wg_ref, wu_ref, gg_ref, ug_ref, dg_ref, gain_ref,
     x_all, cb, hid, gbk, ubk, gain_sum, sem, cot_sem) = refs
    size = cb.shape[1]
    tile = pieces[0].shape[0]
    per = tile // chunk
    tiles = x_all.shape[0] // tile
    own = pl.ds(pl.multiple_of(at_ref[0] * size, size), size)

    @pl.when(pl.program_id(0) == 0)
    def _():
        copies = []
        for i in range(count * per):
            spot = pl.ds(pl.multiple_of(at_ref[1 + i] * chunk, chunk), chunk)
            part = pieces[i // per].at[pl.ds(i % per * chunk, chunk)]
            copies.append(pltpu.make_async_copy(part, x_all.at[spot], sem.at[i]))
        base = 1 + count * per
        for i in range(per):
            spot = pl.ds(pl.multiple_of(at_ref[base + i] * chunk, chunk), chunk)
            target = cb.at[pl.ds(i * chunk, chunk)]
            copies.append(pltpu.make_async_copy(cots[0].at[spot, own], target, cot_sem.at[i]))
        for i, (source, spot) in enumerate(tiles_of(cots, at_ref, base + per, tile)):
            if i > 0:
                target = cb.at[pl.ds(i * tile, tile)]
                copies.append(
                    pltpu.make_async_copy(source.at[spot, own], target, cot_sem.at[per + i])
                )
        for copy in copies:
            copy.start()
        for copy in copies:
            copy.wait()

    hid[:tile, :], gbk[:tile, :], ubk[:tile, :] = own_hid[...], own_gate[...], own_up[...]
    wg, wu = wg_ref[...], wu_ref[...]
    for i in range(1, tiles):
        at = pl.ds(i * tile, tile)
        x = x_all[at, :]
        hid[at, :], gbk[at, :], ubk[at, :] = gate_math(
            dot(x, wg), dot(x, wu), hb_ref[at, :].astype(F32)
        )
    xb = x_all[:, own]
    gate_grad = dot_tn(xb, gbk[...])
    up_grad = dot_tn(xb, ubk[...])
    gg_ref[...] = gate_grad
    ug_ref[...] = up_grad
    dg_ref[...] = dot_tn(hid[...], cb[...])
    gain = jnp.sum(
        wg_ref[own, :].astype(F32) * gate_grad + wu_ref[own, :].astype(F32) * up_grad,
        axis=1, keepdims=True,
    )

    @pl.when(pl.program_id(0) == 0)
    def _():
        gain_sum[...] = gain

    @pl.when(pl.program_id(0) > 0)
    def _():
        gain_sum[...] += gain

    @pl.when(pl.program_id(0) == pl.num_programs(0) - 1)
    def _():
        gain_ref[...] = jnp.broadcast_to(gain_sum[...], (size, HD)).T[:1, :]


def mlp_grad(places, chunk, pieces, own, cots, hb, wg, wu, size):
    tile, width = pieces[0].shape
    rows, units = hb.shape
    block = min(256, units)
    wspec = pl.BlockSpec((width, block), lambda i, at: (0, i))
    ospec = pl.BlockSpec((tile, block), lambda i, at: (0, i))
    grid_spec = pltpu.PrefetchScalarGridSpec(
        num_scalar_prefetch=1,
        grid=(units // block,),
        in_specs=[HBM_WHOLE] * (len(pieces) + len(cots)) + [ospec] * 3
        + [pl.BlockSpec((rows, block), lambda i, at: (0, i)), wspec, wspec],
        out_specs=[pl.BlockSpec((size, block), lambda i, at: (0, i))] * 2
        + [pl.BlockSpec((block, size), lambda i, at: (i, 0)),
           pl.BlockSpec((1, size), lambda i, at: (0, 0))],
        scratch_shapes=[pltpu.VMEM((rows, width), BF), pltpu.VMEM((rows, size), BF)]
        + [pltpu.VMEM((rows, block), BF)] * 3
        + [pltpu.VMEM((size, 1), F32), pltpu.SemaphoreType.DMA((rows // chunk,)),
           pltpu.SemaphoreType.DMA((tile // chunk + rows // tile,))],
    )
    return pl.pallas_call(
        functools.partial(mlp_grad_kernel, len(pieces), chunk, len(cots)),
        grid_spec=grid_spec,
        out_shape=[jax.ShapeDtypeStruct((size, units), F32)] * 2
        + [jax.ShapeDtypeStruct((units, size), F32), jax.ShapeDtypeStruct((1, size), F32)],
        compiler_params=pltpu.CompilerParams(vmem_limit_bytes=56 * MIB),
        cost_estimate=pl.CostEstimate(
            flops=2 * rows * units * (2 * width + 3 * size),
            bytes_accessed=4 * width * units + 4 * rows * width,
            transcendentals=0,
        ),
    )(
        places, *pieces, *[in_hbm(cot) for cot in cots], *[in_hbm(rows) for rows in own],
        in_hbm(hb), in_hbm(wg), in_hbm(wu),
    )


def row_mean(values):
    return jnp.mean(values, axis=-1, keepdims=True)


def norm_parts(values):
    root = lax.rsqrt(row_mean(values * values) + EPS)
    return values * root, root


def norm_back(upstream, scaled, root, gain):
    inner = upstream * gain
    return root * (inner - scaled * row_mean(inner * scaled))


def per_device(
    activations, cotangent, doc_ids, attn_gain, query_weight, key_weight, value_weight,
    out_weight, mlp_gain, gate_weight, up_weight, down_weight,
):
    rows, width = activations.shape[1:]
    n_dp, n_ctx, n_t = lax.axis_size("dp"), lax.axis_size("ctx"), lax.axis_size("tensor")
    dp, ctx, place = lax.axis_index("dp"), lax.axis_index("ctx"), lax.axis_index("tensor")
    chunk = rows // n_t
    length = rows * n_ctx
    slots = slot_order(n_t)
    scale, shift = HD ** (-0.5), -math.log(length)
    gain_first, gain_second = attn_gain.astype(F32), mlp_gain.astype(F32)

    slot_places = jnp.stack([place ^ slot for slot in slots])
    normed_first, mine, cot, cot_mine, inputs_mine, scaled_mine, root_mine = arrange(
        slot_places, activations[0], cotangent[0], attn_gain
    )

    bits = list(reversed(bits_of(n_t)))

    def spread(rings, beside=()):
        lists = [[ring] for ring in rings]
        for bit in bits:
            lists = [items + [swap(item, "tensor", bit) for item in items] for items in lists]
            if bit == bits[0]:
                lists = after(lists, beside)
        return lists

    rings = ring_of(mine)[1:]
    cot_own = lax.all_gather(cot_mine, ("ctx", "tensor"), axis=0, tiled=True)

    ring_at = ctx ^ jnp.arange(n_ctx, dtype=jnp.int32)
    seq_places = jnp.concatenate([
        ring_at[k : k + 1] * n_t + (place ^ slot) for k in range(n_ctx) for slot in slots
    ])
    docs = doc_ids
    out_cols = width // (n_dp * n_ctx)
    owners = jnp.stack([((dp + step) % n_dp) * n_ctx + ctx for step in range(n_dp)])
    starts = owners * out_cols
    owner = owners[0]
    half = place & 1
    places = [owner[None]]
    for flip in (0, 1):
        for step in range(n_dp):
            for index in range(n_t // 2):
                if step == 0:
                    group = jnp.arange(n_ctx, dtype=jnp.int32)
                else:
                    other_half = ring_at // (n_ctx // 2) != half
                    group = step * n_ctx + other_half * (n_ctx // 2) + ring_at % (n_ctx // 2)
                inside = place ^ slots[index] ^ flip
                if step == 0:
                    inside = jnp.where(group == 0, index + flip * (n_t // 2), inside)
                places.append(group * n_t + inside)
    places = jnp.concatenate(places + [ctx * n_t + slot_places, ring_at])
    frequency = np.float32(10000.0) ** (
        -np.arange(HD // 2, dtype=np.float32) * np.float32(2.0) / np.float32(HD)
    )
    angles = np.arange(length, dtype=np.float32)[:, None] * frequency[None, :]
    cos = jnp.asarray(np.concatenate([np.cos(angles), np.cos(angles)], axis=1))
    sin = jnp.asarray(np.concatenate([-np.sin(angles), np.sin(angles)], axis=1))
    rings = [after(ring, seq_places, starts, places) for ring in rings]
    hidden_back = own_hidden_back(after(cot, rings), down_weight)
    seq_pieces = spread(rings, hidden_back)
    own_pieces = [normed_first[i * chunk : (i + 1) * chunk] for i in range(n_t)]
    q, k, v, attended, mass, x_seq = attend(
        seq_places, own_pieces + sum(seq_pieces, []), docs, cos, sin,
        query_weight, key_weight, value_weight, n_t, scale, shift,
    )
    attn_mass = from_slots(mass[:, :, 0].T, slots, place)

    def over_dp(items):
        return [turn(item, "dp", step) for step in range(1, n_dp) for item in items]

    def over_tensor(items, bits):
        for bit in bits:
            items = items + [swap(item, "tensor", bit) for item in items]
        return items

    branch = scatter_tensor(
        jnp.dot(attended, out_weight, preferred_element_type=F32).astype(BF), attn_mass
    )
    middle = inputs_mine + branch
    scaled_second, root_second = norm_parts(middle)
    normed_chunk = (scaled_second * gain_second).astype(BF)
    cot_own = after(cot_own, normed_chunk)
    size = length // 2
    cot_half = lax.dynamic_slice_in_dim(cot_own, half * size, size, 0)
    cot_far = [turn(cot_half, "dp", step) for step in range(1, n_dp)]
    gate, up = fetch(after(gate_weight, normed_chunk), up_weight)
    normed_second = gather_tensor(normed_chunk, (gate, up))
    chunk_rings = ring_of(normed_chunk)
    hidden, gate_back, up_back, second_part = mlp(normed_second, hidden_back, gate, up)
    second_part, chunk_rings = lax.optimization_barrier((second_part, chunk_rings))
    x_near = [join(chunk_rings)]
    x_far = over_dp(x_near)
    x_near_more = over_tensor(x_near, bits[:-1])[1:]
    second_back = scatter_tensor(second_part)
    middle_back = cot_mine.astype(F32) + norm_back(
        second_back, scaled_second, root_second, gain_second
    )
    branch_back = middle_back.astype(BF)
    bb_rings = ring_of(branch_back)
    cots = [cot_own] + sum([[far, swap(far, "tensor", 1)] for far in cot_far], [])
    cots = after(cots, branch_back)
    hidden_back_all, mlp_part = hidden_back_of(ring_at, cots, down_weight, hidden, 0)
    bb_rings, x_far, x_near_more = after((bb_rings, x_far, x_near_more), hidden_back_all)
    hidden_back_all, mlp_part = hidden_back_of(
        ring_at, after(cots, bb_rings), down_weight, hidden, 1, (mlp_part, hidden_back_all)
    )
    bb_pieces = spread(bb_rings, mlp_part)
    x_far_more = over_tensor(x_far, bits[:-1])[len(x_far) :]

    mine_grads, theirs_grads, kept_half, given_half = attend_back(
        seq_places, starts, sum(bb_pieces, []), out_weight, q, k, v, cos, sin, docs, mlp_part,
        x_seq, query_weight, key_weight, value_weight, out_cols, n_t, scale, shift,
    )

    theirs = [turn(theirs_grads[step - 1], "dp", step) for step in range(1, n_dp)]

    x_pieces = over_tensor(x_near + x_near_more + x_far + x_far_more, bits[-1:])

    gate_grad, up_grad, down_grad, mlp_gain_sum = mlp_grad(
        after(places, kept_half), chunk, x_pieces, (hidden, gate_back, up_back), cots,
        hidden_back_all, gate_weight, up_weight, out_cols,
    )
    mlp_gain_sum = mlp_gain_sum[0]
    theirs = after(theirs, gate_grad)
    both = scatter_tensor((kept_half, given_half), gate_grad)
    first_back, mlp_out = both[:, :width], both[:, width:]
    input_grad = (
        middle_back + norm_back(first_back, scaled_mine, root_mine, gain_first)
    ).astype(BF)
    layer_out = (middle + mlp_out).astype(BF)
    results = gather_tensor(jnp.concatenate([layer_out, input_grad], axis=1))
    results = from_slots(results, slots, place)
    layer_out, input_grad = results[:, :width], results[:, width:]
    attn_grads = mine_grads + sum(part.astype(F32) for part in theirs)
    query_grad, key_grad, value_grad = attn_grads[0], attn_grads[1], attn_grads[2]
    out_grad = attn_grads[3].T

    def rows_of(weight):
        return lax.dynamic_slice_in_dim(weight, owner * out_cols, out_cols, 0).astype(F32)

    attn_gain_sum = jnp.sum(
        rows_of(query_weight) * query_grad + rows_of(key_weight) * key_grad
        + rows_of(value_weight) * value_grad, axis=1,
    )
    gains = jnp.stack([attn_gain_sum, mlp_gain_sum])
    for bit in bits:
        gains = gains + swap(gains, "tensor", bit)
    gain_grads = gains / lax.dynamic_slice_in_dim(
        jnp.stack([gain_first, gain_second]), owner * out_cols, out_cols, 1
    )

    return (
        layer_out[None], input_grad[None], gain_grads[0], query_grad, key_grad, value_grad,
        out_grad, gain_grads[1], gate_grad, up_grad, down_grad, attn_mass[None],
    )


def solution(mesh):
    return jax.shard_map(
        per_device,
        mesh=mesh,
        in_specs=(
            P("dp", "ctx", None),
            P("dp", "ctx", None),
            P("dp", None),
            P(),
            P(None, "tensor"),
            P(None, "tensor"),
            P(None, "tensor"),
            P("tensor", None),
            P(),
            P(None, "tensor"),
            P(None, "tensor"),
            P("tensor", None),
        ),
        out_specs=(
            P("dp", "ctx", None),
            P("dp", "ctx", None),
            P(("dp", "ctx")),
            P(("dp", "ctx"), "tensor"),
            P(("dp", "ctx"), "tensor"),
            P(("dp", "ctx"), "tensor"),
            P("tensor", ("dp", "ctx")),
            P(("dp", "ctx")),
            P(("dp", "ctx"), "tensor"),
            P(("dp", "ctx"), "tensor"),
            P("tensor", ("dp", "ctx")),
            P("dp", "ctx", "tensor"),
        ),
        check_vma=False,
    )
```

```python
import functools
import math

import jax
import jax.numpy as jnp
import numpy as np
from jax import lax
from jax.experimental import pallas as pl
from jax.experimental.pallas import tpu as pltpu
from jax.sharding import PartitionSpec as P

HD = 128
EPS = 1e-05
BF = jnp.bfloat16
F32 = jnp.float32
MIB = 1024 * 1024


def swap(values, axis, distance):
    count = lax.axis_size(axis)
    return lax.ppermute(values, axis, [(i, i ^ distance) for i in range(count)])


def turn(values, axis, shift):
    count = lax.axis_size(axis)
    return lax.ppermute(values, axis, [(i, (i + shift) % count) for i in range(count)])


def after(value, *others):
    return lax.optimization_barrier((value, others))[0]


def in_hbm(values):
    return pltpu.with_memory_space_constraint(values, pltpu.HBM)


def in_vmem(values):
    return pltpu.with_memory_space_constraint(values, pltpu.VMEM)


def bits_of(count):
    return [1 << i for i in range(count.bit_length() - 1)]


def slot_order(count):
    order = [0]
    for bit in reversed(bits_of(count)):
        order = order + [slot ^ bit for slot in order]
    return order


def gather_tensor(rows, beside=()):
    for bit in reversed(bits_of(lax.axis_size("tensor"))):
        got = after(swap(rows, "tensor", bit), beside)
        rows, beside = jnp.concatenate([rows, got], axis=0), ()
    return rows


def scatter_tensor(rows, beside=()):
    bits = bits_of(lax.axis_size("tensor"))
    for bit in bits:
        if not isinstance(rows, tuple):
            half = rows.shape[0] // 2
            rows = rows[:half], rows[half:]
        got = swap(rows[1].astype(BF), "tensor", bit)
        if bit == bits[-1]:
            got = after(got, beside)
        rows = rows[0].astype(F32) + got.astype(F32)
    return rows


def ring_of(rows):
    return [rows] + [swap(rows, "ctx", k) for k in range(1, lax.axis_size("ctx"))]


def from_slots(blocks, slots, place):
    size = blocks.shape[0] // len(slots)
    out = jnp.zeros_like(blocks)
    for index, slot in enumerate(slots):
        out = lax.dynamic_update_slice_in_dim(
            out, blocks[index * size : (index + 1) * size], (place ^ slot) * size, 0
        )
    return out


def rope_rows(u, cos, sin):
    return u * cos + pltpu.roll(u, HD // 2, 1) * sin


def rope_back_rows(u, cos, sin):
    return u * cos - pltpu.roll(u, HD // 2, 1) * sin


def dot(a, b):
    return lax.dot_general(a, b, (((1,), (0,)), ((), ())), preferred_element_type=F32)


def dot_nt(a, b):
    return lax.dot_general(a, b, (((1,), (1,)), ((), ())), preferred_element_type=F32)


def dot_tn(a, b):
    return lax.dot_general(a, b, (((0,), (0,)), ((), ())), preferred_element_type=F32)


def place_rows(step, pieces, places, rows, sem, start=True, wait=True):
    @pl.when(step == 0)
    def _():
        copies = []
        for i, (piece, place) in enumerate(zip(pieces, places, strict=True)):
            copies.append(pltpu.make_async_copy(piece, rows.at[place], sem.at[i]))
        if start:
            for copy in copies:
                copy.start()
        if wait:
            for copy in copies:
                copy.wait()


def chunk_places(at_ref, first, count, chunk):
    return [
        pl.ds(pl.multiple_of(at_ref[first + i] * chunk, chunk), chunk) for i in range(count)
    ]


NEVER = -1e30
VMEM_WHOLE = pl.BlockSpec(memory_space=pltpu.VMEM)
HBM_WHOLE = pl.BlockSpec(memory_space=pl.ANY)


def fetch_kernel(count, *refs):
    sources, targets, sem = refs[:count], refs[count : 2 * count], refs[-1]
    copies = [
        pltpu.make_async_copy(source, target, sem.at[i])
        for i, (source, target) in enumerate(zip(sources, targets, strict=True))
    ]
    for copy in copies:
        copy.start()
    for copy in copies:
        copy.wait()


def fetch(*weights):
    return pl.pallas_call(
        functools.partial(fetch_kernel, len(weights)),
        in_specs=[HBM_WHOLE] * len(weights),
        out_specs=[VMEM_WHOLE] * len(weights),
        out_shape=[pltpu.VMEM(weight.shape, weight.dtype) for weight in weights],
        scratch_shapes=[pltpu.SemaphoreType.DMA((len(weights),))],
        compiler_params=pltpu.CompilerParams(vmem_limit_bytes=2 * MIB),
        cost_estimate=pl.CostEstimate(
            flops=0, bytes_accessed=0, transcendentals=0
        ),
    )(*[in_hbm(weight) for weight in weights])


def arrange_kernel(
    at_ref, rows_hbm, cot_hbm, gain_ref, normed_ref, mine_ref, cots_ref, cot_mine_ref,
    inputs_ref, scaled_ref, root_ref, rows_in, gain_in, rows_sem, cot_sem, gain_sem,
):
    chunk = mine_ref.shape[0]
    gain_copy = pltpu.make_async_copy(gain_ref, gain_in, gain_sem)
    gain_copy.start()
    spots = chunk_places(at_ref, 0, normed_ref.shape[0] // chunk, chunk)
    parts = [slice(i * chunk, (i + 1) * chunk) for i in range(len(spots))]
    copies = []
    for i, (spot, part) in enumerate(zip(spots, parts, strict=True)):
        copies.append((
            pltpu.make_async_copy(rows_hbm.at[spot], rows_in.at[part], rows_sem.at[i]),
            pltpu.make_async_copy(cot_hbm.at[spot], cots_ref.at[part], cot_sem.at[i]),
        ))
    for pair in copies:
        for copy in pair:
            copy.start()
    gain_copy.wait()
    gain = gain_in[...].astype(F32).reshape(1, -1)
    for i, (part, pair) in enumerate(zip(parts, copies, strict=True)):
        pair[0].wait()
        rows = rows_in[part, :].astype(F32)
        root = lax.rsqrt(jnp.mean(rows * rows, axis=-1, keepdims=True) + EPS)
        normed = (rows * root * gain).astype(BF)
        normed_ref[part, :] = normed
        pair[1].wait()
        if i == 0:
            mine_ref[...] = normed
            cot_mine_ref[...] = cots_ref[part, :]
            inputs_ref[...] = rows
            scaled_ref[...] = rows * root
            root_ref[...] = jnp.broadcast_to(root, root_ref.shape)


def arrange(places, rows, cot, gain):
    count, width = rows.shape
    slots = places.shape[0]
    chunk = count // slots
    shapes = [(count, width), (chunk, width)] * 2
    more = [(chunk, width)] * 3
    return pl.pallas_call(
        arrange_kernel,
        in_specs=[pl.BlockSpec(memory_space=pltpu.SMEM), HBM_WHOLE, HBM_WHOLE, HBM_WHOLE],
        out_specs=[VMEM_WHOLE] * 7,
        out_shape=[jax.ShapeDtypeStruct(shape, BF) for shape in shapes]
        + [jax.ShapeDtypeStruct(shape, F32) for shape in more],
        scratch_shapes=[pltpu.VMEM((count, width), BF), pltpu.VMEM(gain.shape, BF),
                        pltpu.SemaphoreType.DMA((slots,)), pltpu.SemaphoreType.DMA((slots,)),
                        pltpu.SemaphoreType.DMA],
        compiler_params=pltpu.CompilerParams(vmem_limit_bytes=16 * MIB),
        cost_estimate=pl.CostEstimate(
            flops=8 * count * width, bytes_accessed=8 * count * width, transcendentals=0
        ),
    )(places, in_hbm(rows), in_hbm(cot), in_hbm(gain))


def column_of(row):
    return jnp.broadcast_to(row, (HD, row.shape[1])).T[:, :1]


def attend_kernel(chunk, slots, scale, shift, at_ref, *refs):
    count = len(refs) - 16
    pieces = refs[:count]
    (doc_ref, cos_ref, sin_ref, wq_ref, wk_ref, wv_ref, q_ref, k_ref, v_ref, att_ref, mass_ref,
     seq_hbm, x, doc_column, sem, out_sem) = refs[count:]
    step, last = pl.program_id(0), pl.num_programs(0) - 1
    place_rows(step, pieces, chunk_places(at_ref, 0, count, chunk), x, sem)
    keep = pltpu.make_async_copy(x, seq_hbm, out_sem)

    @pl.when(step == 0)
    def _():
        keep.start()

    cos, sin = cos_ref[...], sin_ref[...]
    own = chunk_places(at_ref, 0, slots, chunk)
    doc_column[...] = column_of(doc_ref[...])
    shape = (chunk, doc_ref.shape[1])
    bias = []
    for i, spot in enumerate(own):
        own_spots = lax.broadcasted_iota(jnp.int32, shape, 0) + at_ref[i] * chunk
        allowed = (lax.broadcasted_iota(jnp.int32, shape, 1) <= own_spots) & (
            doc_column[spot, :] == doc_ref[...]
        )
        bias.append(jnp.where(allowed, shift, NEVER))
    bias = jnp.concatenate(bias, axis=0)
    rows = x[...]
    q_all = dot(rows, wq_ref[...])
    k_all = dot(rows, wk_ref[...])
    v_all = dot(rows, wv_ref[...]).astype(BF)
    v_ref[...] = v_all
    for j in range(q_all.shape[1] // HD):
        cols = slice(j * HD, (j + 1) * HD)
        q_ref[:, cols] = rope_rows(q_all[:, cols], cos, sin).astype(BF)
        k = rope_rows(k_all[:, cols], cos, sin).astype(BF)
        k_ref[:, cols] = k
        q = jnp.concatenate([q_ref[spot, cols] for spot in own], axis=0)
        weights = jax.nn.sigmoid(dot_nt(q, k) * scale + bias)
        mass_ref[j] = jnp.sum(weights, axis=-1, keepdims=True)
        att_ref[:, cols] = dot(weights.astype(BF), v_all[:, cols]).astype(BF)

    @pl.when(step == last)
    def _():
        keep.wait()


def attend(places, pieces, docs, cos, sin, wq, wk, wv, slots, scale, shift):
    chunk, width = pieces[0].shape
    seq, rows = chunk * len(pieces), chunk * slots
    cols = wq.shape[1]
    heads = cols // HD
    step = min(2, heads)
    whole = lambda *shape: pl.BlockSpec(
        shape, lambda i: (0,) * len(shape), pipeline_mode=pl.Buffered(1)
    )
    hbm = pl.BlockSpec(memory_space=pl.ANY)
    wspec = pl.BlockSpec((width, step * HD), lambda i: (0, i))
    sspec = pl.BlockSpec((seq, step * HD), lambda i: (0, i))
    return pl.pallas_call(
        functools.partial(attend_kernel, chunk, slots, scale, shift),
        grid=(heads // step,),
        in_specs=[pl.BlockSpec(memory_space=pltpu.SMEM)] + [hbm] * len(pieces)
        + [whole(1, seq), whole(seq, HD), whole(seq, HD)]
        + [wspec] * 3,
        out_specs=[sspec, sspec, sspec,
                   pl.BlockSpec((rows, step * HD), lambda i: (0, i)),
                   pl.BlockSpec((step, rows, 1), lambda i: (i, 0, 0)),
                   pl.BlockSpec(memory_space=pltpu.HBM)],
        out_shape=[jax.ShapeDtypeStruct((seq, cols), BF)] * 3
        + [jax.ShapeDtypeStruct((rows, cols), BF), jax.ShapeDtypeStruct((heads, rows, 1), F32),
           jax.ShapeDtypeStruct((seq, width), BF)],
        scratch_shapes=[pltpu.VMEM((seq, width), BF), pltpu.VMEM((seq, 1), jnp.int32),
                        pltpu.SemaphoreType.DMA((len(pieces),)), pltpu.SemaphoreType.DMA],
        compiler_params=pltpu.CompilerParams(vmem_limit_bytes=56 * MIB),
        cost_estimate=pl.CostEstimate(
            flops=2 * seq * width * cols * 3, bytes_accessed=6 * width * cols, transcendentals=0
        ),
    )(places, *pieces, docs, cos, sin, wq, wk, wv)


def attend_back_kernel(chunk, slots, scale, shift, at_ref, starts_ref, *refs):
    count = len(refs) - 24
    pieces = refs[:count]
    (wo_ref, q_ref, k_ref, v_ref, cos_ref, sin_ref, doc_row_ref, more_ref,
     x_hbm, wq_hbm, wk_hbm, wv_hbm, mine_ref, theirs_ref, first_ref, give_ref,
     bb, x_cols, w_cols, acc, every, bb_sem, x_sem, w_sem) = refs[count:]
    step = pl.program_id(0)
    owners = x_cols.shape[0]
    spots = chunk_places(at_ref, 0, count, chunk)
    place_rows(step, pieces, spots, bb, bb_sem, wait=False)
    seq, size, width = bb.shape[0], x_cols.shape[2], w_cols.shape[2]
    starts = [pl.multiple_of(starts_ref[i], HD) for i in range(owners)]
    at = pl.ds(pl.multiple_of(step * width, HD), width)
    copies = [
        pltpu.make_async_copy(x_hbm.at[:, pl.ds(starts[i], size)], x_cols.at[i], x_sem.at[i])
        for i in range(owners)
    ] + [
        pltpu.make_async_copy(w_hbm.at[:, at], w_cols.at[i], w_sem.at[i])
        for i, w_hbm in enumerate((wq_hbm, wk_hbm, wv_hbm))
    ]
    for copy in copies:
        copy.start()

    block = min(256, seq)
    parts = [slice(i * block, (i + 1) * block) for i in range(seq // block)]
    heads = [slice(j * HD, (j + 1) * HD) for j in range(width // HD)]
    weights, attended = {}, []
    doc_column = column_of(doc_row_ref[...])
    for i, part in enumerate(parts):
        shape = (block, part.stop)
        allowed = (
            lax.broadcasted_iota(jnp.int32, shape, 1)
            <= lax.broadcasted_iota(jnp.int32, shape, 0) + part.start
        ) & (doc_column[part, :] == doc_row_ref[:, : part.stop])
        bias = jnp.where(allowed, shift, NEVER)
        row = []
        for j, cols in enumerate(heads):
            scores = dot_nt(q_ref[part, cols], k_ref[: part.stop, cols]) * scale + bias
            weights[i, j] = jax.nn.sigmoid(scores)
            row.append(dot(weights[i, j].astype(BF), v_ref[: part.stop, cols]).astype(BF))
        attended.append(jnp.concatenate(row, axis=1))
    attended = jnp.concatenate(attended, axis=0)

    place_rows(step, pieces, spots, bb, bb_sem, start=False)
    ab_all = dot_nt(bb[...], wo_ref[...]).astype(BF)
    for j, cols in enumerate(heads):
        key_sums, value_sums = [None] * len(parts), [None] * len(parts)
        for i, part in enumerate(parts):
            ab, weight = ab_all[part, cols], weights[i, j]
            slope = weight - weight * weight
            back = (dot_nt(ab, v_ref[: part.stop, cols]) * slope).astype(BF)
            weight = weight.astype(BF)
            query_back = dot(back, k_ref[: part.stop, cols]) * scale
            every[part, cols] = rope_back_rows(
                query_back, cos_ref[part, :], sin_ref[part, :]
            ).astype(BF)
            for n in range(i + 1):
                key_part = dot_tn(back[:, parts[n]], q_ref[part, cols])
                value_part = dot_tn(weight[:, parts[n]], ab)
                key_sums[n] = key_part if i == n else key_sums[n] + key_part
                value_sums[n] = value_part if i == n else value_sums[n] + value_part
        for n, part in enumerate(parts):
            at_key = slice(width + cols.start, width + cols.stop)
            at_value = slice(2 * width + cols.start, 2 * width + cols.stop)
            every[part, at_key] = rope_back_rows(
                key_sums[n] * scale, cos_ref[part, :], sin_ref[part, :]
            ).astype(BF)
            every[part, at_value] = value_sums[n].astype(BF)

    def give(i, n, part):
        if i == 0:
            mine_ref[n] = part
        else:
            theirs_ref[i - 1, n] = part.astype(BF)

    for i in range(owners):
        give(i, 3, dot_tn(bb[:, pl.ds(starts[i], size)], attended))

    for copy in copies:
        copy.wait()
    for i in range(owners):
        total = dot_tn(x_cols[i], every[...])
        for n in range(3):
            give(i, n, total[:, n * width : (n + 1) * width])
    own = jnp.concatenate([every[spot, :] for spot in spots[:slots]], axis=0)
    first = sum(dot_nt(own[:, n * width : (n + 1) * width], w_cols[n]) for n in range(3))

    @pl.when(step == 0)
    def _():
        acc[...] = first

    @pl.when(step > 0)
    def _():
        acc[...] += first

    @pl.when(step == pl.num_programs(0) - 1)
    def _():
        total, half = acc[...].astype(BF), acc.shape[0] // 2
        for n, at in enumerate((slice(0, half), slice(half, 2 * half))):
            keep_ref = first_ref if n == 0 else give_ref
            keep_ref[:, : acc.shape[1]] = total[at]
            keep_ref[:, acc.shape[1] :] = more_ref[at, :]


def attend_back(
    places, starts, pieces, wo, q, k, v, cos, sin, docs, more, x_seq, wq, wk, wv,
    size, slots, scale, shift,
):
    seq, width = x_seq.shape
    chunk = pieces[0].shape[0]
    cols = wo.shape[0]
    heads = cols // HD
    step = min(2, heads)
    own = slots * chunk
    owners = starts.shape[0]
    whole = lambda *shape: pl.BlockSpec(
        shape, lambda i: (0,) * len(shape), pipeline_mode=pl.Buffered(1)
    )
    sspec = pl.BlockSpec((seq, step * HD), lambda i: (0, i))
    hbm = pl.BlockSpec(memory_space=pl.ANY)
    return pl.pallas_call(
        functools.partial(attend_back_kernel, chunk, slots, scale, shift),
        grid=(heads // step,),
        in_specs=[pl.BlockSpec(memory_space=pltpu.SMEM)] * 2 + [hbm] * len(pieces)
        + [pl.BlockSpec((step * HD, width), lambda i: (i, 0)),
           sspec, sspec, sspec, whole(seq, HD), whole(seq, HD), whole(1, seq), whole(*more.shape)]
        + [hbm] * 4,
        out_specs=[pl.BlockSpec((4, size, step * HD), lambda i: (0, 0, i)),
                   pl.BlockSpec((owners - 1, 4, size, step * HD), lambda i: (0, 0, 0, i)),
                   whole(own // 2, 2 * width), whole(own // 2, 2 * width)],
        out_shape=[jax.ShapeDtypeStruct((4, size, cols), F32),
                   jax.ShapeDtypeStruct((owners - 1, 4, size, cols), BF),
                   jax.ShapeDtypeStruct((own // 2, 2 * width), BF),
                   jax.ShapeDtypeStruct((own // 2, 2 * width), BF)],
        scratch_shapes=[pltpu.VMEM((seq, width), BF), pltpu.VMEM((owners, seq, size), BF),
                        pltpu.VMEM((3, width, step * HD), BF),
                        pltpu.VMEM((own, width), F32),
                        pltpu.VMEM((seq, 3 * step * HD), BF),
                        pltpu.SemaphoreType.DMA((len(pieces),)),
                        pltpu.SemaphoreType.DMA((owners,)), pltpu.SemaphoreType.DMA((3,))],
        compiler_params=pltpu.CompilerParams(vmem_limit_bytes=56 * MIB),
        cost_estimate=pl.CostEstimate(
            flops=2 * seq * width * cols + 14 * seq * seq * cols,
            bytes_accessed=2 * (seq + cols) * width + 20 * seq * cols,
            transcendentals=seq * seq * heads,
        ),
    )(
        places, starts, *pieces, in_hbm(wo), q, k, v, cos, sin,
        docs, more, in_hbm(x_seq), in_hbm(wq), in_hbm(wk), in_hbm(wv),
    )


def gate_math(gate, up, hidden_back):
    sig = jax.nn.sigmoid(gate)
    act = gate * sig
    hidden = (act * up).astype(BF)
    gate_back = (hidden_back * up * sig * (1.0 + gate * (1.0 - sig))).astype(BF)
    up_back = (hidden_back * act).astype(BF)
    return hidden, gate_back, up_back


def mlp_kernel(
    block, x_ref, hb_ref, wg_ref, up_hbm, hidden_ref, gate_ref, up_ref, back_ref, wu_ref, sem
):
    tiles = [slice(i * block, (i + 1) * block) for i in range(wg_ref.shape[1] // block)]
    copies = [
        pltpu.make_async_copy(up_hbm.at[:, at], wu_ref.at[:, at], sem.at[i])
        for i, at in enumerate(tiles)
    ]
    for copy in copies:
        copy.start()
    x, total = x_ref[...], None
    for copy, at in zip(copies, tiles, strict=True):
        wg = wg_ref[:, at]
        gate = dot(x, wg)
        copy.wait()
        wu = wu_ref[:, at]
        hidden_ref[:, at], gate_back, up_back = gate_math(
            gate, dot(x, wu), hb_ref[:, at].astype(F32)
        )
        gate_ref[:, at] = gate_back
        up_ref[:, at] = up_back
        back = dot_nt(gate_back, wg) + dot_nt(up_back, wu)
        total = back if total is None else total + back
    back_ref[...] = total.astype(BF)


def mlp(x, hidden_back, wg, wu):
    rows, width = x.shape
    units = wg.shape[1]
    block = min(512, units)
    return pl.pallas_call(
        functools.partial(mlp_kernel, block),
        in_specs=[VMEM_WHOLE] * 3 + [HBM_WHOLE],
        out_specs=[VMEM_WHOLE] * 4,
        out_shape=[
            *[jax.ShapeDtypeStruct((rows, units), BF)] * 3, jax.ShapeDtypeStruct((rows, width), BF)
        ],
        scratch_shapes=[
            pltpu.VMEM(wu.shape, wu.dtype), pltpu.SemaphoreType.DMA((units // block,))
        ],
        compiler_params=pltpu.CompilerParams(vmem_limit_bytes=28 * MIB),
        cost_estimate=pl.CostEstimate(flops=0, bytes_accessed=0, transcendentals=0),
    )(x, hidden_back, in_vmem(wg), in_hbm(wu))


def tiles_of(sources, at_ref, first, tile):
    listed = []
    for n, source in enumerate(sources):
        for i in range(source.shape[0] // tile):
            index = at_ref[first + i] if n == 0 else i
            at = pl.ds(pl.multiple_of(index * tile, tile), tile) if n == 0 else pl.ds(i * tile, tile)
            listed.append((source, at))
    return listed


def own_hidden_back_kernel(rows_ref, wd_ref, out_ref):
    out_ref[...] = dot_nt(rows_ref[...], wd_ref[...]).astype(BF)


def own_hidden_back(rows, wd):
    count, width = rows.shape
    units = wd.shape[0]
    block = min(512, units)
    return pl.pallas_call(
        own_hidden_back_kernel,
        grid=(units // block,),
        in_specs=[
            pl.BlockSpec((count, width), lambda i: (0, 0), pipeline_mode=pl.Buffered(1)),
            pl.BlockSpec((block, width), lambda i: (i, 0)),
        ],
        out_specs=pl.BlockSpec((count, block), lambda i: (0, i)),
        out_shape=jax.ShapeDtypeStruct((count, units), BF),
        compiler_params=pltpu.CompilerParams(vmem_limit_bytes=24 * MIB),
        cost_estimate=pl.CostEstimate(
            flops=2 * count * width * units, bytes_accessed=2 * width * units, transcendentals=0
        ),
    )(rows, in_hbm(wd))


def hidden_back_kernel(tile, more, count, at_ref, *refs):
    sources, (wd_ref, hidden_ref, before) = refs[:count], refs[count : count + 3]
    out_ref, sum_ref, cot, total, sem = refs[-5:]
    step, block = pl.program_id(0), wd_ref.shape[0]
    copies = []
    for i, (source, at) in enumerate(tiles_of(sources, at_ref, 0, tile)):
        if i > 0:
            target = cot.at[pl.ds(i * tile, tile)]
            copies.append(pltpu.make_async_copy(source.at[at], target, sem.at[i]))
    rows = len(copies) * tile
    parts = -(-rows // 512)
    size = rows // parts

    def every_tile(waits):
        wd = wd_ref[...]
        own = dot(hidden_ref[...], wd)
        done = 0
        for i in range(parts):
            while waits and done * tile < (i + 1) * size:
                copies[done].wait()
                done += 1
            at = pl.ds(tile + i * size, size)
            out_ref[at, :] = dot_nt(cot[at, :], wd).astype(BF)
        return own

    @pl.when(step == 0)
    def _():
        for copy in copies:
            copy.start()
        own = every_tile(True)
        total[...] = own + before[...] if more else own

    @pl.when(step > 0)
    def _():
        total[...] += every_tile(False)

    @pl.when(step == pl.num_programs(0) - 1)
    def _():
        sum_ref[...] = total[...].astype(sum_ref.dtype)


def hidden_back_of(turns, cots, wd, hidden, part, before=()):
    width = cots[0].shape[1]
    rows, units = sum(cot.shape[0] for cot in cots), wd.shape[0]
    tiles = rows // hidden.shape[0]
    block = min(512, units // 2)
    steps = units // 2 // block
    skip = part * steps
    tile = hidden.shape[0]
    whole = pl.BlockSpec((tile, width), lambda i: (0, 0), pipeline_mode=pl.Buffered(1))
    return pl.pallas_call(
        functools.partial(hidden_back_kernel, tile, len(before) > 0, len(cots)),
        grid=(steps,),
        in_specs=[pl.BlockSpec(memory_space=pltpu.SMEM)] + [HBM_WHOLE] * len(cots)
        + [pl.BlockSpec((block, width), lambda i: (i + skip, 0)),
           pl.BlockSpec((tile, block), lambda i: (0, i + skip))]
        + [whole, HBM_WHOLE][: len(before)],
        out_specs=[pl.BlockSpec((rows, block), lambda i: (0, i + skip)), whole],
        out_shape=[jax.ShapeDtypeStruct((rows, units), BF),
                   jax.ShapeDtypeStruct((tile, width), BF if part else F32)],
        scratch_shapes=[pltpu.VMEM((rows, width), BF), pltpu.VMEM((tile, width), F32),
                        pltpu.SemaphoreType.DMA((tiles,))],
        input_output_aliases={len(cots) + 4: 0} if before else {},
        compiler_params=pltpu.CompilerParams(vmem_limit_bytes=56 * MIB),
        cost_estimate=pl.CostEstimate(
            flops=rows * width * units, bytes_accessed=2 * width * (rows + units),
            transcendentals=0,
        ),
    )(turns, *[in_hbm(cot) for cot in cots], in_hbm(wd), hidden, *before)


def join_kernel(count, *refs):
    pieces, out_ref, sem = refs[:count], refs[count], refs[-1]
    size = pieces[0].shape[0]
    copies = [
        pltpu.make_async_copy(piece, out_ref.at[pl.ds(i * size, size)], sem.at[i])
        for i, piece in enumerate(pieces)
    ]
    for copy in copies:
        copy.start()
    for copy in copies:
        copy.wait()


def join(pieces):
    size, width = pieces[0].shape
    return pl.pallas_call(
        functools.partial(join_kernel, len(pieces)),
        in_specs=[HBM_WHOLE] * len(pieces),
        out_specs=pl.BlockSpec(memory_space=pl.ANY),
        out_shape=jax.ShapeDtypeStruct((size * len(pieces), width), BF),
        scratch_shapes=[pltpu.SemaphoreType.DMA((len(pieces),))],
        compiler_params=pltpu.CompilerParams(vmem_limit_bytes=2 * MIB),
        cost_estimate=pl.CostEstimate(flops=0, bytes_accessed=0, transcendentals=0),
    )(*pieces)


def mlp_grad_kernel(count, chunk, parts, at_ref, *refs):
    pieces, cots, refs = refs[:count], refs[count : count + parts], refs[count + parts :]
    (own_hid, own_gate, own_up, hb_ref, wg_ref, wu_ref, gg_ref, ug_ref, dg_ref, gain_ref,
     x_all, cb, hid, gbk, ubk, gain_sum, sem, cot_sem) = refs
    size = cb.shape[1]
    tile = pieces[0].shape[0]
    per = tile // chunk
    tiles = x_all.shape[0] // tile
    own = pl.ds(pl.multiple_of(at_ref[0] * size, size), size)

    @pl.when(pl.program_id(0) == 0)
    def _():
        copies = []
        for i in range(count * per):
            spot = pl.ds(pl.multiple_of(at_ref[1 + i] * chunk, chunk), chunk)
            part = pieces[i // per].at[pl.ds(i % per * chunk, chunk)]
            copies.append(pltpu.make_async_copy(part, x_all.at[spot], sem.at[i]))
        base = 1 + count * per
        for i in range(per):
            spot = pl.ds(pl.multiple_of(at_ref[base + i] * chunk, chunk), chunk)
            target = cb.at[pl.ds(i * chunk, chunk)]
            copies.append(pltpu.make_async_copy(cots[0].at[spot, own], target, cot_sem.at[i]))
        for i, (source, spot) in enumerate(tiles_of(cots, at_ref, base + per, tile)):
            if i > 0:
                target = cb.at[pl.ds(i * tile, tile)]
                copies.append(
                    pltpu.make_async_copy(source.at[spot, own], target, cot_sem.at[per + i])
                )
        for copy in copies:
            copy.start()
        for copy in copies:
            copy.wait()

    hid[:tile, :], gbk[:tile, :], ubk[:tile, :] = own_hid[...], own_gate[...], own_up[...]
    wg, wu = wg_ref[...], wu_ref[...]
    for i in range(1, tiles):
        at = pl.ds(i * tile, tile)
        x = x_all[at, :]
        hid[at, :], gbk[at, :], ubk[at, :] = gate_math(
            dot(x, wg), dot(x, wu), hb_ref[at, :].astype(F32)
        )
    xb = x_all[:, own]
    gate_grad = dot_tn(xb, gbk[...])
    up_grad = dot_tn(xb, ubk[...])
    gg_ref[...] = gate_grad
    ug_ref[...] = up_grad
    dg_ref[...] = dot_tn(hid[...], cb[...])
    gain = jnp.sum(
        wg_ref[own, :].astype(F32) * gate_grad + wu_ref[own, :].astype(F32) * up_grad,
        axis=1, keepdims=True,
    )

    @pl.when(pl.program_id(0) == 0)
    def _():
        gain_sum[...] = gain

    @pl.when(pl.program_id(0) > 0)
    def _():
        gain_sum[...] += gain

    @pl.when(pl.program_id(0) == pl.num_programs(0) - 1)
    def _():
        gain_ref[...] = jnp.broadcast_to(gain_sum[...], (size, HD)).T[:1, :]


def mlp_grad(places, chunk, pieces, own, cots, hb, wg, wu, size):
    tile, width = pieces[0].shape
    rows, units = hb.shape
    block = min(256, units)
    wspec = pl.BlockSpec((width, block), lambda i, at: (0, i))
    ospec = pl.BlockSpec((tile, block), lambda i, at: (0, i))
    grid_spec = pltpu.PrefetchScalarGridSpec(
        num_scalar_prefetch=1,
        grid=(units // block,),
        in_specs=[HBM_WHOLE] * (len(pieces) + len(cots)) + [ospec] * 3
        + [pl.BlockSpec((rows, block), lambda i, at: (0, i)), wspec, wspec],
        out_specs=[pl.BlockSpec((size, block), lambda i, at: (0, i))] * 2
        + [pl.BlockSpec((block, size), lambda i, at: (i, 0)),
           pl.BlockSpec((1, size), lambda i, at: (0, 0))],
        scratch_shapes=[pltpu.VMEM((rows, width), BF), pltpu.VMEM((rows, size), BF)]
        + [pltpu.VMEM((rows, block), BF)] * 3
        + [pltpu.VMEM((size, 1), F32), pltpu.SemaphoreType.DMA((rows // chunk,)),
           pltpu.SemaphoreType.DMA((tile // chunk + rows // tile,))],
    )
    return pl.pallas_call(
        functools.partial(mlp_grad_kernel, len(pieces), chunk, len(cots)),
        grid_spec=grid_spec,
        out_shape=[jax.ShapeDtypeStruct((size, units), F32)] * 2
        + [jax.ShapeDtypeStruct((units, size), F32), jax.ShapeDtypeStruct((1, size), F32)],
        compiler_params=pltpu.CompilerParams(vmem_limit_bytes=56 * MIB),
        cost_estimate=pl.CostEstimate(
            flops=2 * rows * units * (2 * width + 3 * size),
            bytes_accessed=4 * width * units + 4 * rows * width,
            transcendentals=0,
        ),
    )(
        places, *pieces, *[in_hbm(cot) for cot in cots], *[in_hbm(rows) for rows in own],
        in_hbm(hb), in_hbm(wg), in_hbm(wu),
    )


def row_mean(values):
    return jnp.mean(values, axis=-1, keepdims=True)


def norm_parts(values):
    root = lax.rsqrt(row_mean(values * values) + EPS)
    return values * root, root


def norm_back(upstream, scaled, root, gain):
    inner = upstream * gain
    return root * (inner - scaled * row_mean(inner * scaled))


def per_device(
    activations, cotangent, doc_ids, attn_gain, query_weight, key_weight, value_weight,
    out_weight, mlp_gain, gate_weight, up_weight, down_weight,
):
    rows, width = activations.shape[1:]
    n_dp, n_ctx, n_t = lax.axis_size("dp"), lax.axis_size("ctx"), lax.axis_size("tensor")
    dp, ctx, place = lax.axis_index("dp"), lax.axis_index("ctx"), lax.axis_index("tensor")
    chunk = rows // n_t
    length = rows * n_ctx
    slots = slot_order(n_t)
    scale, shift = HD ** (-0.5), -math.log(length)
    gain_first, gain_second = attn_gain.astype(F32), mlp_gain.astype(F32)

    slot_places = jnp.stack([place ^ slot for slot in slots])
    normed_first, mine, cot, cot_mine, inputs_mine, scaled_mine, root_mine = arrange(
        slot_places, activations[0], cotangent[0], attn_gain
    )

    bits = list(reversed(bits_of(n_t)))

    def spread(rings, beside=()):
        lists = [[ring] for ring in rings]
        for bit in bits:
            lists = [items + [swap(item, "tensor", bit) for item in items] for items in lists]
            if bit == bits[0]:
                lists = after(lists, beside)
        return lists

    rings = ring_of(mine)[1:]
    cot_own = lax.all_gather(cot_mine, ("ctx", "tensor"), axis=0, tiled=True)

    ring_at = ctx ^ jnp.arange(n_ctx, dtype=jnp.int32)
    seq_places = jnp.concatenate([
        ring_at[k : k + 1] * n_t + (place ^ slot) for k in range(n_ctx) for slot in slots
    ])
    docs = doc_ids
    out_cols = width // (n_dp * n_ctx)
    owners = jnp.stack([((dp + step) % n_dp) * n_ctx + ctx for step in range(n_dp)])
    starts = owners * out_cols
    owner = owners[0]
    half = place & 1
    places = [owner[None]]
    for flip in (0, 1):
        for step in range(n_dp):
            for index in range(n_t // 2):
                if step == 0:
                    group = jnp.arange(n_ctx, dtype=jnp.int32)
                else:
                    other_half = ring_at // (n_ctx // 2) != half
                    group = step * n_ctx + other_half * (n_ctx // 2) + ring_at % (n_ctx // 2)
                inside = place ^ slots[index] ^ flip
                if step == 0:
                    inside = jnp.where(group == 0, index + flip * (n_t // 2), inside)
                places.append(group * n_t + inside)
    places = jnp.concatenate(places + [ctx * n_t + slot_places, ring_at])
    frequency = np.float32(10000.0) ** (
        -np.arange(HD // 2, dtype=np.float32) * np.float32(2.0) / np.float32(HD)
    )
    angles = np.arange(length, dtype=np.float32)[:, None] * frequency[None, :]
    cos = jnp.asarray(np.concatenate([np.cos(angles), np.cos(angles)], axis=1))
    sin = jnp.asarray(np.concatenate([-np.sin(angles), np.sin(angles)], axis=1))
    rings = [after(ring, seq_places, starts, places) for ring in rings]
    hidden_back = own_hidden_back(after(cot, rings), down_weight)
    seq_pieces = spread(rings, hidden_back)
    own_pieces = [normed_first[i * chunk : (i + 1) * chunk] for i in range(n_t)]
    q, k, v, attended, mass, x_seq = attend(
        seq_places, own_pieces + sum(seq_pieces, []), docs, cos, sin,
        query_weight, key_weight, value_weight, n_t, scale, shift,
    )
    attn_mass = from_slots(mass[:, :, 0].T, slots, place)

    def over_dp(items):
        return [turn(item, "dp", step) for step in range(1, n_dp) for item in items]

    def over_tensor(items, bits):
        for bit in bits:
            items = items + [swap(item, "tensor", bit) for item in items]
        return items

    branch = scatter_tensor(
        jnp.dot(attended, out_weight, preferred_element_type=F32).astype(BF), attn_mass
    )
    middle = inputs_mine + branch
    scaled_second, root_second = norm_parts(middle)
    normed_chunk = (scaled_second * gain_second).astype(BF)
    cot_own = after(cot_own, normed_chunk)
    size = length // 2
    cot_half = lax.dynamic_slice_in_dim(cot_own, half * size, size, 0)
    cot_far = [turn(cot_half, "dp", step) for step in range(1, n_dp)]
    (gate,) = fetch(after(gate_weight, normed_chunk))
    normed_second = gather_tensor(normed_chunk, gate)
    chunk_rings = ring_of(normed_chunk)
    hidden, gate_back, up_back, second_part = mlp(normed_second, hidden_back, gate, up_weight)
    second_part, chunk_rings = lax.optimization_barrier((second_part, chunk_rings))
    x_near = [join(chunk_rings)]
    x_far = over_dp(x_near)
    x_near_more = over_tensor(x_near, bits[:-1])[1:]
    second_back = scatter_tensor(second_part)
    middle_back = cot_mine.astype(F32) + norm_back(
        second_back, scaled_second, root_second, gain_second
    )
    branch_back = middle_back.astype(BF)
    bb_rings = ring_of(branch_back)
    cots = [cot_own] + sum([[far, swap(far, "tensor", 1)] for far in cot_far], [])
    cots = after(cots, branch_back)
    hidden_back_all, mlp_part = hidden_back_of(ring_at, cots, down_weight, hidden, 0)
    bb_rings, x_far, x_near_more = after((bb_rings, x_far, x_near_more), hidden_back_all)
    hidden_back_all, mlp_part = hidden_back_of(
        ring_at, after(cots, bb_rings), down_weight, hidden, 1, (mlp_part, hidden_back_all)
    )
    bb_pieces = spread(bb_rings, mlp_part)
    x_far_more = over_tensor(x_far, bits[:-1])[len(x_far) :]

    mine_grads, theirs_grads, kept_half, given_half = attend_back(
        seq_places, starts, sum(bb_pieces, []), out_weight, q, k, v, cos, sin, docs, mlp_part,
        x_seq, query_weight, key_weight, value_weight, out_cols, n_t, scale, shift,
    )

    theirs = [turn(theirs_grads[step - 1], "dp", step) for step in range(1, n_dp)]

    x_pieces = over_tensor(x_near + x_near_more + x_far + x_far_more, bits[-1:])

    gate_grad, up_grad, down_grad, mlp_gain_sum = mlp_grad(
        after(places, kept_half), chunk, x_pieces, (hidden, gate_back, up_back), cots,
        hidden_back_all, gate_weight, up_weight, out_cols,
    )
    mlp_gain_sum = mlp_gain_sum[0]
    theirs = after(theirs, gate_grad)
    both = scatter_tensor((kept_half, given_half), gate_grad)
    first_back, mlp_out = both[:, :width], both[:, width:]
    input_grad = (
        middle_back + norm_back(first_back, scaled_mine, root_mine, gain_first)
    ).astype(BF)
    layer_out = (middle + mlp_out).astype(BF)
    results = gather_tensor(jnp.concatenate([layer_out, input_grad], axis=1))
    results = from_slots(results, slots, place)
    layer_out, input_grad = results[:, :width], results[:, width:]
    attn_grads = mine_grads + sum(part.astype(F32) for part in theirs)
    query_grad, key_grad, value_grad = attn_grads[0], attn_grads[1], attn_grads[2]
    out_grad = attn_grads[3].T

    def rows_of(weight):
        return lax.dynamic_slice_in_dim(weight, owner * out_cols, out_cols, 0).astype(F32)

    attn_gain_sum = jnp.sum(
        rows_of(query_weight) * query_grad + rows_of(key_weight) * key_grad
        + rows_of(value_weight) * value_grad, axis=1,
    )
    gains = jnp.stack([attn_gain_sum, mlp_gain_sum])
    for bit in bits:
        gains = gains + swap(gains, "tensor", bit)
    gain_grads = gains / lax.dynamic_slice_in_dim(
        jnp.stack([gain_first, gain_second]), owner * out_cols, out_cols, 1
    )

    return (
        layer_out[None], input_grad[None], gain_grads[0], query_grad, key_grad, value_grad,
        out_grad, gain_grads[1], gate_grad, up_grad, down_grad, attn_mass[None],
    )


def solution(mesh):
    return jax.shard_map(
        per_device,
        mesh=mesh,
        in_specs=(
            P("dp", "ctx", None),
            P("dp", "ctx", None),
            P("dp", None),
            P(),
            P(None, "tensor"),
            P(None, "tensor"),
            P(None, "tensor"),
            P("tensor", None),
            P(),
            P(None, "tensor"),
            P(None, "tensor"),
            P("tensor", None),
        ),
        out_specs=(
            P("dp", "ctx", None),
            P("dp", "ctx", None),
            P(("dp", "ctx")),
            P(("dp", "ctx"), "tensor"),
            P(("dp", "ctx"), "tensor"),
            P(("dp", "ctx"), "tensor"),
            P("tensor", ("dp", "ctx")),
            P(("dp", "ctx")),
            P(("dp", "ctx"), "tensor"),
            P(("dp", "ctx"), "tensor"),
            P("tensor", ("dp", "ctx")),
            P("dp", "ctx", "tensor"),
        ),
        check_vma=False,
    )
```
